32 devices in a mesh: dp: 16 (over z, y, core), tensor: 2 (over x).
Axes of the slice: x: 2, y: 2, z: 4, core: 2. Of those that a mesh axis runs over, the one named last changes fastest.
Arguments:
- inputs: bfloat16 [2, 65536, 512], P(None, ('dp', 'tensor')), may hold values from -6 to 6
- lengths: int32 [2, 64], P(None, 'dp'), may hold values from 256 to 1024, as said below
- pre_gain: bfloat16 [512], replicated, may hold values from 0.099609375 to 1.8984375
- pre_shift: bfloat16 [512], replicated, may hold values from -1.75 to 1.75
- query_weight: bfloat16 [512, 512], P('dp', 'tensor'), may hold values from -0.25 to 0.25
- key_weight: bfloat16 [512, 512], P('dp', 'tensor'), may hold values from -0.25 to 0.25
- value_weight: bfloat16 [512, 512], P('dp', 'tensor'), may hold values from -0.25 to 0.25
- query_bias: bfloat16 [512], P('tensor'), may hold values from -3 to 3
- value_bias: bfloat16 [512], P('tensor'), may hold values from -3 to 3
- output_weight: bfloat16 [512, 512], P('tensor', 'dp'), may hold values from -0.75 to 0.75
- output_bias: bfloat16 [512], replicated, may hold values from -1.75 to 1.75
- mid_gain: bfloat16 [512], replicated, may hold values from 0.099609375 to 1.8984375
- mid_shift: bfloat16 [512], replicated, may hold values from -1.75 to 1.75
- up_weight: bfloat16 [512, 2048], P('dp', 'tensor'), may hold values from -0.25 to 0.25
- up_bias: bfloat16 [2048], P('tensor'), may hold values from -3 to 3
- down_weight: bfloat16 [2048, 512], P('tensor', 'dp'), may hold values from -0.125 to 0.125
- down_bias: bfloat16 [512], replicated, may hold values from -1.75 to 1.75
- cotangent: bfloat16 [2, 65536, 512], P(None, ('dp', 'tensor')), may hold values from -6 to 6
Outputs:
- outputs: bfloat16 [2, 65536, 512], P(None, ('dp', 'tensor'))
- input_grad: bfloat16 [2, 65536, 512], P(None, ('dp', 'tensor'))
- grad_pre_gain: float32 [512], replicated
- grad_pre_shift: float32 [512], replicated
- grad_query_weight: float32 [512, 512], P('dp', 'tensor')
- grad_key_weight: float32 [512, 512], P('dp', 'tensor')
- grad_value_weight: float32 [512, 512], P('dp', 'tensor')
- grad_query_bias: float32 [512], P('tensor')
- grad_value_bias: float32 [512], P('tensor')
- grad_output_weight: float32 [512, 512], P('tensor', 'dp')
- grad_output_bias: float32 [512], replicated
- grad_mid_gain: float32 [512], replicated
- grad_mid_shift: float32 [512], replicated
- grad_up_weight: float32 [512, 2048], P('dp', 'tensor')
- grad_up_bias: float32 [2048], P('tensor')
- grad_down_weight: float32 [2048, 512], P('tensor', 'dp')
- grad_down_bias: float32 [512], replicated
The draws below stay inside these ranges and needn't reach their ends.
Inputs may be any that keep to these rules, and one draw needn't show every extreme that they name: `lengths`: real tokens of each sequence; the first sequence of the first micro-batch is full.
All inputs are finite; a program needn't handle non-finite values.
Results may differ from the reference program's by a relative error of at most 0.02.
Values may be sent and summed in bfloat16 or wider, within the bound.
A program may use at most 960 MiB of HBM per device.

```python
import jax
import jax.numpy as jnp
import numpy as np
from jax import lax

D = 512
HEADS = 8
HD = 64
FF = 2048
NR = 16
LEVELS = 6
MICRO = 2
SEQ_MB = 4
SLOT = 1024
ROWS_ALL = 65536
N_DP = 16


def draw_lengths(key, part):
    values = jax.random.randint(key, (MICRO, N_DP * SEQ_MB), SLOT // 4, SLOT + 1, dtype=jnp.int32)
    return values.at[0, 0].set(SLOT).astype(jnp.int32)


def block_levels(own_key, shape, split, least, high):
    level = 1.0
    for position, parts in split:
        heights = jax.random.uniform(jax.random.fold_in(jax.random.fold_in(own_key, 6), position), (parts,), jnp.float32, least / len(split), high / len(split))
        level = level * jnp.repeat(jnp.exp(heights), shape[position] // parts).reshape((-1,) + (1,) * (len(shape) - 1 - position))
    return level


def noise(rng, extent, width, most, pieces=(), kind=jnp.bfloat16):
    drawn = width * jax.random.normal(rng, extent, jnp.float32)
    if pieces:
        drawn = drawn * block_levels(rng, extent, pieces, -0.22, 0.18)
    return jnp.clip(drawn, -most, most).astype(kind)


def setup_inputs(seed: int = 0) -> dict:
    key_list = jax.random.split(jax.random.key(seed), 19)
    return {
        "inputs": noise(key_list[0], (MICRO, ROWS_ALL, D), 1.0, 6.0, ((1, 32),)),
        "lengths": draw_lengths(jax.random.fold_in(key_list[18], 71), 0),
        "pre_gain": jnp.clip(1.0 + 0.18 * jax.random.normal(key_list[2], (D,), jnp.float32), 0.099609375, 1.8984375).astype(jnp.bfloat16),
        "pre_shift": noise(key_list[3], (D,), 0.3, 1.75),
        "query_weight": noise(key_list[4], (D, D), D ** -0.5, 0.25, ((0, 16), (1, 2))),
        "key_weight": noise(key_list[5], (D, D), D ** -0.5, 0.25, ((0, 16), (1, 2))),
        "value_weight": noise(key_list[6], (D, D), D ** -0.5, 0.25, ((0, 16), (1, 2))),
        "query_bias": noise(key_list[7], (D,), 0.5, 3.0, ((0, 2),)),
        "value_bias": noise(key_list[8], (D,), 0.5, 3.0, ((0, 2),)),
        "output_weight": noise(key_list[9], (D, D), HD ** -0.5, 0.75, ((0, 2), (1, 16))),
        "output_bias": noise(key_list[10], (D,), 0.3, 1.75),
        "mid_gain": jnp.clip(1.0 + 0.18 * jax.random.normal(key_list[11], (D,), jnp.float32), 0.099609375, 1.8984375).astype(jnp.bfloat16),
        "mid_shift": noise(key_list[12], (D,), 0.3, 1.75),
        "up_weight": noise(key_list[13], (D, FF), D ** -0.5, 0.25, ((0, 16), (1, 2))),
        "up_bias": noise(key_list[14], (FF,), 0.5, 3.0, ((0, 2),)),
        "down_weight": noise(key_list[15], (FF, D), FF ** -0.5, 0.125, ((0, 2), (1, 16))),
        "down_bias": noise(key_list[16], (D,), 0.3, 1.75),
        "cotangent": noise(key_list[17], (MICRO, ROWS_ALL, D), 1.0, 6.0, ((1, 32),)),
    }


@jax.custom_vjp
def low(v):
    return lax.optimization_barrier(v.astype(jnp.bfloat16)).astype(jnp.float32)

@jax.custom_vjp
def low_back(v):
    return v

def low_keep(v):
    return (low(v), None)

def low_pass(kept, grad):
    return (grad,)

def back_keep(v):
    return (v, None)

def back_low(kept, grad):
    return (low(grad),)
low.defvjp(low_keep, low_pass)
low_back.defvjp(back_keep, back_low)

def matmul(left, right):
    return jnp.dot(left, right, preferred_element_type=jnp.float32, precision=lax.Precision.HIGHEST)

def layer_norm(values, gain, shift):
    centre = values - lax.optimization_barrier(jnp.mean(values, axis=-1, keepdims=True))
    spread = lax.optimization_barrier(jnp.mean(centre * centre, axis=-1, keepdims=True))
    return centre * lax.rsqrt(spread + 1e-05) * gain + shift

def gelu_tanh(values):
    return jax.nn.gelu(values, approximate=True)

def allowed_table(block_count, level_index):
    block_ids = np.arange(block_count)[:, None, None]
    query_ids = np.arange(NR)[None, :, None]
    key_ids = np.arange(3 * NR)[None, None, :]
    key_cell = (block_ids - 1) * NR + key_ids
    query_cell = block_ids * NR + query_ids
    if level_index == 0:
        return np.ones((block_count, NR, 3 * NR), dtype=bool)
    return np.abs(2 * key_cell // NR - 2 * query_cell // NR) > 1

def neighbours(values, block_count):
    shaped = values.reshape((values.shape[0], block_count, NR) + values.shape[2:])
    padding = [(0, 0), (1, 1)] + [(0, 0)] * (shaped.ndim - 2)
    padded = jnp.pad(shaped, padding)
    return jnp.concatenate([padded[:, :-2], padded[:, 1:-1], padded[:, 2:]], axis=2)

def level_terms(queries, keys, values, live_rows, level_index):
    run_width = 2 ** level_index
    batch_size, seq_len, head_dim = queries.shape
    cell_count = seq_len // run_width
    block_count = cell_count // NR
    coarse_query = lax.optimization_barrier(jnp.mean(queries.reshape(batch_size, cell_count, run_width, head_dim), axis=2))
    counts = lax.optimization_barrier(jnp.sum(live_rows.reshape(batch_size, cell_count, run_width), axis=2))
    divisor = jnp.maximum(counts, 1.0)[..., None]
    coarse_key = lax.optimization_barrier(jnp.sum((keys * live_rows[..., None]).reshape(batch_size, cell_count, run_width, head_dim), axis=2)) / divisor
    coarse_value = lax.optimization_barrier(jnp.sum((values * live_rows[..., None]).reshape(batch_size, cell_count, run_width, head_dim), axis=2)) / divisor
    query_blocks = coarse_query.reshape(batch_size, block_count, NR, head_dim)
    key_near = neighbours(coarse_key, block_count)
    value_near = neighbours(coarse_value, block_count)
    count_near = neighbours(counts, block_count)
    scores = jnp.einsum('bnqe,bnke->bnqk', query_blocks, key_near, precision=lax.Precision.HIGHEST) * head_dim ** (-0.5)
    scores = scores + jnp.log(jnp.maximum(count_near, 1.0))[:, :, None, :]
    usable = jnp.logical_and(jnp.asarray(allowed_table(block_count, level_index))[None], (count_near > 0.5)[:, :, None, :])
    masked = jnp.where(usable, scores, -1e+30)
    top = lax.optimization_barrier(jnp.max(masked, axis=3))
    shares = jnp.where(usable, jnp.exp(masked - top[..., None]), 0.0)
    total = lax.optimization_barrier(jnp.sum(shares, axis=3))
    mixed = jnp.einsum('bnqk,bnke->bnqe', shares, value_near, precision=lax.Precision.HIGHEST)
    return (top.reshape(batch_size, cell_count), total.reshape(batch_size, cell_count), mixed.reshape(batch_size, cell_count, head_dim))

def hier_attention(queries, keys, values, seq_lengths):
    seq_len = queries.shape[1]
    positions = jnp.arange(seq_len, dtype=jnp.int32)
    live_rows = jnp.where(positions[None, :] < seq_lengths[:, None], 1.0, 0.0).astype(queries.dtype)
    results = []
    for level_index in range(LEVELS):
        top, total, mixed = level_terms(queries, keys, values, live_rows, level_index)
        reach = 2 ** level_index
        results.append((jnp.repeat(top, reach, axis=1), jnp.repeat(total, reach, axis=1), jnp.repeat(mixed, reach, axis=1)))
    highest = results[0][0]
    for entry in results[1:]:
        highest = jnp.maximum(highest, entry[0])
    denominator = jnp.zeros_like(highest)
    numerator = jnp.zeros_like(queries)
    for top, total, mixed in results:
        factor = jnp.exp(top - highest)
        denominator = denominator + factor * total
        numerator = numerator + factor[..., None] * mixed
    return numerator / denominator[..., None]

def split_heads(values, head_dim):
    row_count, feature_count = values.shape
    shaped = values.reshape(row_count // SLOT, SLOT, feature_count // head_dim, head_dim)
    return shaped.transpose(0, 2, 1, 3).reshape(-1, SLOT, head_dim)

def join_heads(values, head_count):
    shaped = values.reshape(-1, head_count, SLOT, values.shape[2])
    return shaped.transpose(0, 2, 1, 3).reshape(-1, head_count * values.shape[2])

def layer(params, block_inputs, seq_lengths):
    pre_gain, pre_shift, query_weight, key_weight, value_weight, query_bias, value_bias, output_weight, output_bias, mid_gain, mid_shift, up_weight, up_bias, down_weight, down_bias = params
    normed = low(layer_norm(block_inputs, pre_gain, pre_shift))
    queries = low_back(low(matmul(normed, query_weight) + query_bias))
    keys = low_back(low(matmul(normed, key_weight)))
    values = low_back(low(matmul(normed, value_weight) + value_bias))
    head_lengths = jnp.repeat(seq_lengths, HEADS)
    mixed = hier_attention(split_heads(queries, HD), split_heads(keys, HD), split_heads(values, HD), head_lengths)
    attended = low(join_heads(mixed, HEADS))
    branch = low_back(matmul(attended, output_weight) + output_bias)
    residual = block_inputs + branch
    normed_mid = low(layer_norm(residual, mid_gain, mid_shift))
    hidden_pre = low_back(matmul(normed_mid, up_weight) + up_bias)
    hidden = low(gelu_tanh(hidden_pre))
    return residual + matmul(hidden, down_weight) + down_bias

def reference(inputs, lengths, pre_gain, pre_shift, query_weight, key_weight, value_weight, query_bias, value_bias, output_weight, output_bias, mid_gain, mid_shift, up_weight, up_bias, down_weight, down_bias, cotangent):
    params = tuple((item.astype(jnp.float32) for item in (pre_gain, pre_shift, query_weight, key_weight, value_weight, query_bias, value_bias, output_weight, output_bias, mid_gain, mid_shift, up_weight, up_bias, down_weight, down_bias)))
    group_size = 4
    flat_inputs = inputs.astype(jnp.float32).reshape(-1, group_size * SLOT, D)
    flat_cotangent = cotangent.astype(jnp.float32).reshape(-1, group_size * SLOT, D)
    flat_lengths = lengths.reshape(-1, group_size).astype(jnp.int32)

    def one_block(carry, block):
        block_inputs, block_lengths, block_cotangent = block

        def forward(param_set, values):
            return layer(param_set, values, block_lengths)
        block_out, pull = jax.vjp(forward, params, block_inputs)
        param_grads, value_grad = pull(block_cotangent)
        carry = jax.tree.map(lambda left, right: left + right, carry, param_grads)
        return (carry, (block_out.astype(jnp.bfloat16), value_grad.astype(jnp.bfloat16)))
    zero_grads = tuple((jnp.zeros_like(item) for item in params))
    totals, (block_outs, block_grads) = lax.scan(one_block, zero_grads, (flat_inputs, flat_lengths, flat_cotangent))
    outputs = block_outs.reshape(inputs.shape)
    input_grad = block_grads.reshape(inputs.shape)
    return (outputs, input_grad, totals[0], totals[1], totals[2], totals[3], totals[4], totals[5], totals[6], totals[7], totals[8], totals[9], totals[10], totals[11], totals[12], totals[13], totals[14])
```

```python
import functools

import jax
import jax.numpy as jnp
import ml_dtypes
import numpy as np
from jax import lax
from jax.experimental import pallas as pl
from jax.experimental.pallas import tpu as pltpu
from jax.sharding import PartitionSpec as P

D = 512
HD = 64
FF = 2048
NR = 16
LEVELS = 6
SLOT = 1024
TILE = 128
TILES = SLOT // TILE
PAIRS = D // 128
HEADS = D // HD
EPS = 1e-05
NEG = -1e30

BASE = (0, 1056, 1600, 1888, 2048, 2144)
CELL_ROWS = 2176
WIN_ROWS = (160, 96, 64, 32, 32, 16)
WIN_AT = (0, 160, 256, 320, 352, 384)
WIN = 400
COARSE = WIN - 160
LANE_AT = (0, 0, 64, 96, 112, 120)
BF = jnp.bfloat16
F32 = jnp.float32


def window_parts(i):
    two, four = i // 2, i // 4
    return (
        (128 * i, 160),
        (BASE[1] + 64 * i, 96),
        (BASE[2] + 32 * i, 64),
        (BASE[3] + 16 * i, 16),
        (BASE[3] + 16 * i + 32, 16),
        (BASE[4] + 16 * two, 16),
        (BASE[4] + 16 * two + 32, 16),
        (BASE[5] + 16 * (1 - four), 16),
    )


def mask_table():
    table = np.full((TILES, WIN, TILE), NEG, np.float32)
    rows = np.arange(TILE)
    for i in range(TILES):
        at = 0
        for start, count in window_parts(i):
            level = max(l for l in range(LEVELS) if WIN_AT[l] <= at)
            pad = 0 if level == 5 else 16
            cell = (start - BASE[level] - pad + np.arange(count))[:, None]
            query = ((128 * i + rows) >> level)[None, :]
            good = np.abs(cell // 16 - query // 16) <= 1
            if level > 0:
                good &= np.abs((2 * cell) // 16 - (2 * query) // 16) > 1
            table[i, at : at + count] = np.where(good, 0.0, NEG)
            at += count
    return table


def constants():
    t = np.arange(TILE)
    pool_q = np.zeros((TILE, TILE), np.float32)
    pool_s = np.zeros((TILE, TILE), np.float32)
    spread = np.zeros((COARSE, TILE), np.int32)
    level_mask = np.zeros((COARSE, TILE), np.float32)
    pool_k = np.zeros((256, 256), np.float32)
    t2 = np.arange(256)
    at = 0
    for level in range(1, LEVELS):
        width = 2**level
        pool_q[LANE_AT[level] + t // width, t] = 1.0 / width
        pool_s[t, LANE_AT[level] + t // width] = 1.0
        rows = slice(WIN_AT[level] - 160, WIN_AT[level] - 160 + WIN_ROWS[level])
        spread[rows] = LANE_AT[level] + t // width
        level_mask[rows, LANE_AT[level] : LANE_AT[level] + TILE // width] = 1.0
        pool_k[at + t2 // width, t2] = 1.0
        at += 256 // width
    half = ml_dtypes.bfloat16
    return {
        "mask": mask_table(),
        "pool_q": pool_q.astype(half),
        "pool_s": pool_s.astype(half),
        "spread": spread,
        "level_mask": level_mask,
        "pool_k": pool_k.astype(half),
        "spread_k": pool_k.T.copy().astype(half),
    }


def mm(a, b):
    return lax.dot_general(a, b, (((1,), (0,)), ((), ())), preferred_element_type=F32)


def mm_nt(a, b):
    return lax.dot_general(a, b, (((1,), (1,)), ((), ())), preferred_element_type=F32)


def mm_tn(a, b):
    return lax.dot_general(a, b, (((0,), (0,)), ((), ())), preferred_element_type=F32)


def norm_parts(values):
    centre = values - jnp.mean(values, axis=-1, keepdims=True)
    spread = jnp.mean(centre * centre, axis=-1, keepdims=True)
    scale = lax.rsqrt(spread + EPS)
    return centre * scale, scale


def norm_back(grad, xhat, scale, gain):
    e = grad * gain
    return (e - jnp.mean(e, axis=-1, keepdims=True) - xhat * jnp.mean(e * xhat, axis=-1, keepdims=True)) * scale


def column_sum(values):
    return jnp.sum(values, axis=0, keepdims=True)


def count_tables(length, bias_ref, inv_ref):
    for level in range(LEVELS):
        width = 2**level
        pad = 0 if level == 5 else 16
        count = SLOT // width + 2 * pad
        cell = lax.broadcasted_iota(jnp.int32, (count, 128), 0) - pad
        live = jnp.clip(length - cell * width, 0, width)
        live = jnp.where(cell < 0, 0, live)
        live_f = live.astype(F32)
        some = jnp.maximum(live_f, 1.0)
        rows = pl.ds(BASE[level], count)
        bias_ref[rows, :] = jnp.where(live > 0, jnp.log(some), NEG)
        inv_ref[rows, :] = 1.0 / some


def window(ref, i, lanes):
    parts = []
    for start, count in window_parts(i):
        parts.append(ref[pl.ds(pl.multiple_of(start, 16), count), lanes])
    return jnp.concatenate(parts, axis=0)


def two_columns(block):
    zero = jnp.zeros((64, block.shape[1]), block.dtype)
    top = jnp.concatenate([block[:64], zero], axis=1)
    low = jnp.concatenate([zero, block[64:]], axis=1)
    return jnp.concatenate([top, low], axis=0)


def two_rows(block):
    first = lax.broadcasted_iota(jnp.int32, block.shape, 1) < 64
    zero = jnp.zeros_like(block)
    return jnp.concatenate([jnp.where(first, block, zero), jnp.where(first, zero, block)], axis=0)


def diagonal(block):
    n = block.shape[1] // 2
    return jnp.concatenate([block[:64, :n], block[64:, n:]], axis=0)


def pair_scores(keys, queries_t, cells_t, spread, bias):
    fine = mm(keys[:160], two_columns(queries_t))
    rough = mm(keys[160:], two_columns(cells_t))
    out = []
    for h in range(2):
        lanes = slice(128 * h, 128 * h + 128)
        wide = jnp.take_along_axis(rough[:, lanes], spread, axis=1)
        out.append(jnp.concatenate([fine[:, lanes], wide], axis=0) + bias)
    return out


def pack_cells(full, length, chunk, out_ref, rough_ref, inv_ref, pool):
    row = lax.broadcasted_iota(jnp.int32, full.shape, 0) + 256 * chunk
    live = jnp.where(row < length, full, 0.0).astype(BF)
    out_ref[0, pl.ds(pl.multiple_of(16 + 256 * chunk, 16), 256), :] = live
    sums = mm(pool, live)
    at = 0
    for level in range(1, LEVELS):
        count = 256 // 2**level
        pad = 0 if level == 5 else 16
        rows = pl.ds(pl.multiple_of(BASE[level] + pad + count * chunk, 8), count)
        inv = jnp.concatenate([inv_ref[rows, :]] * PAIRS, axis=1)
        cells = sums[at : at + count] * inv
        if level == 5:
            rough_ref[pl.ds(pl.multiple_of(8 * chunk, 8), 8), :] = cells
        else:
            out_ref[0, pl.ds(pl.multiple_of(BASE[level] + 16 + count * chunk, 16), count), :] = cells.astype(BF)
        at += count


def forward_kernel(
    lens, x_ref, gain_ref, shift_ref, wq_ref, wk_ref, wv_ref, bq_ref, bv_ref,
    mask_ref, pool_q_ref, spread_ref, pool_k_ref,
    n1_ref, q_ref, k_ref, v_ref, attn_ref, lse_ref,
    bias_ref, inv_ref, rough_ref, tile_bias_ref,
):
    length = lens[pl.program_id(0)]
    count_tables(length, bias_ref, inv_ref)
    zeros = jnp.zeros((16, D), BF)
    for level in range(LEVELS - 1):
        cells = SLOT // 2**level
        for ref in (k_ref, v_ref):
            ref[0, pl.ds(BASE[level], 16), :] = zeros
            ref[0, pl.ds(BASE[level] + 16 + cells, 16), :] = zeros
    rough_k, rough_v = rough_ref.at[0], rough_ref.at[1]

    def project(chunk, carry):
        rows = pl.ds(pl.multiple_of(256 * chunk, 256), 256)
        xhat, _ = norm_parts(x_ref[0, rows, :].astype(F32))
        n1 = (xhat * gain_ref[...] + shift_ref[...]).astype(BF)
        n1_ref[0, rows, :] = n1
        q = (mm(n1, wq_ref[...]) + bq_ref[...]).astype(BF)
        q_ref[0, rows, :] = q * BF(0.125)
        pool = pool_k_ref[...]
        pack_cells(mm(n1, wk_ref[...]), length, chunk, k_ref, rough_k, inv_ref, pool)
        pack_cells(mm(n1, wv_ref[...]) + bv_ref[...], length, chunk, v_ref, rough_v, inv_ref, pool)
        return carry

    lax.fori_loop(0, 4, project, 0)
    k_ref[0, pl.ds(BASE[5], 32), :] = rough_k[...].astype(BF)
    v_ref[0, pl.ds(BASE[5], 32), :] = rough_v[...].astype(BF)

    def attend(i, carry):
        rows = pl.ds(pl.multiple_of(128 * i, 128), 128)
        tile_bias_ref[...] = mask_ref[i] + window(bias_ref, i, slice(None))
        q = q_ref[0, rows, :]
        cells = mm(pool_q_ref[...], q).astype(BF)
        lse = []
        for pair in range(PAIRS):
            lanes = slice(128 * pair, 128 * pair + 128)
            keys = window(k_ref.at[0], i, lanes)
            values = window(v_ref.at[0], i, lanes)
            scores = pair_scores(keys, q[:, lanes].T, cells[:, lanes].T, spread_ref[...], tile_bias_ref[...])
            shares, inverse = [], []
            for s in scores:
                top = jnp.max(s, axis=0, keepdims=True)
                p = jnp.exp(s - top)
                total = jnp.sum(p, axis=0, keepdims=True)
                shares.append(p.astype(BF))
                inverse.append(1.0 / total)
                lse.append(top + jnp.log(total))
            mixed = mm_tn(values, jnp.concatenate(shares, axis=1))
            mixed = diagonal(mixed * jnp.concatenate(inverse, axis=1))
            attn_ref[0, rows, lanes] = mixed.T.astype(BF)
        lse_ref[0, :, rows] = jnp.concatenate(lse, axis=0)
        return carry

    lax.fori_loop(0, TILES, attend, 0)


def middle_kernel(
    x_ref, attn_ref, cot_ref, wo_ref, bo_ref, gain_ref, shift_ref, up_ref, bup_ref, down_ref, bdown_ref,
    out_ref, g1_ref, gwo_ref, gup_ref, gdown_ref, gvec_ref, gbup_ref,
):
    step = pl.program_id(0)

    @pl.when(step == 0)
    def _():
        gwo_ref[...] = jnp.zeros_like(gwo_ref)
        gup_ref[...] = jnp.zeros_like(gup_ref)
        gdown_ref[...] = jnp.zeros_like(gdown_ref)
        gvec_ref[...] = jnp.zeros_like(gvec_ref)
        gbup_ref[...] = jnp.zeros_like(gbup_ref)

    attn = attn_ref[...]
    cot = cot_ref[...]
    y1 = x_ref[...].astype(F32) + (mm(attn, wo_ref[...]) + bo_ref[...])
    xhat, scale = norm_parts(y1)
    n2 = (xhat * gain_ref[...] + shift_ref[...]).astype(BF)
    n2_t = n2.T
    cot_t = cot.T
    out = y1 + bdown_ref[...]
    dn2 = jnp.zeros_like(y1)
    c = np.float32(np.sqrt(2.0 / np.pi))
    for part in range(4):
        cols = slice(512 * part, 512 * part + 512)
        u = mm(n2, up_ref[:, cols]) + bup_ref[:, cols]
        dh = mm_nt(cot, down_ref[cols, :])
        u2 = u * u
        t = jnp.tanh(u * (c + (c * 0.044715) * u2))
        h = 0.5 + 0.5 * t
        hid = (u * h).astype(BF)
        slope = h + 2.0 * h * (1.0 - h) * u * (c + (3.0 * c * 0.044715) * u2)
        dhp = dh * slope
        dhp_b = dhp.astype(BF)
        gbup_ref[:, cols] += column_sum(dhp)
        out = out + mm(hid, down_ref[cols, :])
        dn2 = dn2 + mm_nt(dhp_b, up_ref[:, cols])
        gdown_ref[:, cols] += mm(cot_t, hid)
        gup_ref[:, cols] += mm(n2_t, dhp_b)
    out_ref[...] = out.astype(BF)
    cot_f = cot.astype(F32)
    dy1 = cot_f + norm_back(dn2, xhat, scale, gain_ref[...])
    g1 = dy1.astype(BF)
    g1_ref[...] = g1
    gwo_ref[...] += mm_tn(attn, g1)
    gvec_ref[...] += jnp.concatenate(
        [column_sum(g1.astype(F32)), column_sum(dn2 * xhat), column_sum(dn2), column_sum(cot_f), jnp.zeros((4, D), F32)],
        axis=0,
    )


def backward_kernel(
    lens, x_ref, n1_ref, q_ref, k_ref, v_ref, attn_ref, lse_ref, g1_ref,
    gain_ref, wq_ref, wk_ref, wv_ref, wo_ref,
    mask_ref, pool_q_ref, pool_s_ref, spread_ref, level_mask_ref, spread_k_ref,
    dx_ref, gqkv_ref, gvec_ref,
    bias_ref, inv_ref, tile_bias_ref, dk_ref, dv_ref, dqkv_ref,
):
    step = pl.program_id(0)

    @pl.when(step == 0)
    def _():
        gqkv_ref[...] = jnp.zeros_like(gqkv_ref)
        gvec_ref[...] = jnp.zeros_like(gvec_ref)

    length = lens[step]
    count_tables(length, bias_ref, inv_ref)
    dk_ref[...] = jnp.zeros_like(dk_ref)
    dv_ref[...] = jnp.zeros_like(dv_ref)
    head_of = lax.broadcasted_iota(jnp.int32, (HEADS, D), 1) // HD
    heads = (head_of == lax.broadcasted_iota(jnp.int32, (HEADS, D), 0)).astype(BF)

    def attend(i, carry):
        rows = pl.ds(pl.multiple_of(128 * i, 128), 128)
        tile_bias_ref[...] = mask_ref[i] + window(bias_ref, i, slice(None))
        q = q_ref[0, rows, :]
        cells = mm(pool_q_ref[...], q).astype(BF)
        da = mm_nt(g1_ref[0, rows, :], wo_ref[...])
        product = da * attn_ref[0, rows, :].astype(F32)
        high = product.astype(BF)
        delta = mm_nt(heads, high) + mm_nt(heads, (product - high.astype(F32)).astype(BF))
        da = da.astype(BF)
        lse = lse_ref[0, :, rows]
        for pair in range(PAIRS):
            lanes = slice(128 * pair, 128 * pair + 128)
            keys = window(k_ref.at[0], i, lanes)
            values = window(v_ref.at[0], i, lanes)
            scores = pair_scores(keys, q[:, lanes].T, cells[:, lanes].T, spread_ref[...], tile_bias_ref[...])
            dp = mm(values, two_columns(da[:, lanes].T))
            shares, fine, rough = [], [], []
            for h in range(2):
                head = 2 * pair + h
                p = jnp.exp(scores[h] - lse[head : head + 1])
                ds = (p * (dp[:, 128 * h : 128 * h + 128] - delta[head : head + 1])).astype(BF)
                shares.append(p.astype(BF))
                fine.append(ds[:160])
                pooled = mm(ds[160:], pool_s_ref[...]) * level_mask_ref[...]
                rough.append(pooled.astype(BF))
            shares = jnp.concatenate(shares, axis=1)
            fine = jnp.concatenate(fine, axis=1)
            rough = jnp.concatenate(rough, axis=1)
            dv = mm(shares, two_rows(da[:, lanes]))
            dk = jnp.concatenate([mm(fine, two_rows(q[:, lanes])), mm(rough, two_rows(cells[:, lanes]))], axis=0)
            at = 0
            for start, count in window_parts(i):
                part = pl.ds(pl.multiple_of(start, 16), count)
                dk_ref[part, lanes] += dk[at : at + count]
                dv_ref[part, lanes] += dv[at : at + count]
                at += count
            dq = diagonal(mm_tn(keys[:160], fine))
            dq_cells = diagonal(mm_tn(keys[160:], rough)).astype(BF)
            dq = (dq + mm(dq_cells, pool_q_ref[...])) * 0.125
            dqkv_ref[rows, lanes] = dq.T.astype(BF)
        return carry

    lax.fori_loop(0, TILES, attend, 0)

    def finish(chunk, carry):
        rows = pl.ds(pl.multiple_of(256 * chunk, 256), 256)
        own = pl.ds(pl.multiple_of(16 + 256 * chunk, 16), 256)
        live = lax.broadcasted_iota(jnp.int32, (256, D), 0) + 256 * chunk < length
        for ref, at in ((dk_ref, D), (dv_ref, 2 * D)):
            cells = []
            for level in range(1, LEVELS):
                count = 256 // 2**level
                pad = 0 if level == 5 else 16
                part = pl.ds(pl.multiple_of(BASE[level] + pad + count * chunk, 8), count)
                cells.append(ref[part, :] * jnp.concatenate([inv_ref[part, :]] * PAIRS, axis=1))
            cells.append(jnp.zeros((8, D), F32))
            wide = mm(spread_k_ref[...], jnp.concatenate(cells, axis=0).astype(BF))
            dqkv_ref[rows, at : at + D] = jnp.where(live, ref[own, :] + wide, 0.0).astype(BF)
        n1 = n1_ref[0, rows, :]
        dq, dk, dv = (dqkv_ref[rows, D * j : D * j + D] for j in range(3))
        dn1 = mm_nt(dq, wq_ref[...]) + mm_nt(dk, wk_ref[...]) + mm_nt(dv, wv_ref[...])
        xhat, scale = norm_parts(x_ref[0, rows, :].astype(F32))
        dx = g1_ref[0, rows, :].astype(F32) + norm_back(dn1, xhat, scale, gain_ref[...])
        dx_ref[0, rows, :] = dx.astype(BF)
        n1_t = n1.T
        for j, part in enumerate((dq, dk, dv)):
            gqkv_ref[:, D * j : D * j + D] += mm(n1_t, part)
        gvec_ref[...] += jnp.concatenate(
            [
                column_sum(dn1 * xhat), column_sum(dn1), column_sum(dq.astype(F32)), column_sum(dv.astype(F32)),
                jnp.zeros((4, D), F32),
            ],
            axis=0,
        )
        return carry

    lax.fori_loop(0, 4, finish, 0)


def whole(shape):
    return pl.BlockSpec(shape, lambda *_: (0,) * len(shape))


def per_sequence(*shape):
    return pl.BlockSpec((1,) + shape, lambda s, *_: (s,) + (0,) * len(shape))


LIMIT = 60 * 1024 * 1024


def attention_forward(x, lens, gain, shift, wq, wk, wv, bq, bv, const):
    count = x.shape[0]
    return pl.pallas_call(
        forward_kernel,
        grid_spec=pltpu.PrefetchScalarGridSpec(
            num_scalar_prefetch=1,
            grid=(count,),
            in_specs=[
                per_sequence(SLOT, D), whole((1, D)), whole((1, D)),
                whole((D, D)), whole((D, D)), whole((D, D)), whole((1, D)), whole((1, D)),
                whole((TILES, WIN, TILE)), whole((TILE, TILE)), whole((COARSE, TILE)), whole((256, 256)),
            ],
            out_specs=[
                per_sequence(SLOT, D), per_sequence(SLOT, D), per_sequence(CELL_ROWS, D), per_sequence(CELL_ROWS, D),
                per_sequence(SLOT, D), per_sequence(HEADS, SLOT),
            ],
            scratch_shapes=[
                pltpu.VMEM((CELL_ROWS, 128), F32), pltpu.VMEM((CELL_ROWS, 128), F32), pltpu.VMEM((2, 32, D), F32),
                pltpu.VMEM((WIN, TILE), F32),
            ],
        ),
        out_shape=[
            jax.ShapeDtypeStruct((count, SLOT, D), BF), jax.ShapeDtypeStruct((count, SLOT, D), BF),
            jax.ShapeDtypeStruct((count, CELL_ROWS, D), BF), jax.ShapeDtypeStruct((count, CELL_ROWS, D), BF),
            jax.ShapeDtypeStruct((count, SLOT, D), BF), jax.ShapeDtypeStruct((count, HEADS, SLOT), F32),
        ],
        compiler_params=pltpu.CompilerParams(vmem_limit_bytes=LIMIT),
        name="attention_forward",
    )(lens, x, gain, shift, wq, wk, wv, bq, bv, const["mask"], const["pool_q"], const["spread"], const["pool_k"])


ROWS = 512


def middle(x, attn, cot, wo, bo, gain, shift, up, bup, down, bdown):
    total = x.shape[0]
    rows = pl.BlockSpec((ROWS, D), lambda s: (s, 0))
    return pl.pallas_call(
        middle_kernel,
        grid=(total // ROWS,),
        in_specs=[
            rows, rows, rows, whole((D, D)), whole((1, D)), whole((1, D)), whole((1, D)),
            whole((D, FF)), whole((1, FF)), whole((FF, D)), whole((1, D)),
        ],
        out_specs=[rows, rows, whole((D, D)), whole((D, FF)), whole((D, FF)), whole((8, D)), whole((1, FF))],
        out_shape=[
            jax.ShapeDtypeStruct((total, D), BF), jax.ShapeDtypeStruct((total, D), BF),
            jax.ShapeDtypeStruct((D, D), F32), jax.ShapeDtypeStruct((D, FF), F32), jax.ShapeDtypeStruct((D, FF), F32),
            jax.ShapeDtypeStruct((8, D), F32), jax.ShapeDtypeStruct((1, FF), F32),
        ],
        compiler_params=pltpu.CompilerParams(vmem_limit_bytes=LIMIT),
        name="middle",
    )(x, attn, cot, wo, bo, gain, shift, up, bup, down, bdown)


def attention_backward(x, lens, n1, q, k, v, attn, lse, g1, gain, wq, wk, wv, wo, const):
    count = x.shape[0]
    return pl.pallas_call(
        backward_kernel,
        grid_spec=pltpu.PrefetchScalarGridSpec(
            num_scalar_prefetch=1,
            grid=(count,),
            in_specs=[
                per_sequence(SLOT, D), per_sequence(SLOT, D), per_sequence(SLOT, D),
                per_sequence(CELL_ROWS, D), per_sequence(CELL_ROWS, D), per_sequence(SLOT, D),
                per_sequence(HEADS, SLOT), per_sequence(SLOT, D),
                whole((1, D)), whole((D, D)), whole((D, D)), whole((D, D)), whole((D, D)),
                whole((TILES, WIN, TILE)), whole((TILE, TILE)), whole((TILE, TILE)), whole((COARSE, TILE)),
                whole((COARSE, TILE)), whole((256, 256)),
            ],
            out_specs=[per_sequence(SLOT, D), whole((D, 3 * D)), whole((8, D))],
            scratch_shapes=[
                pltpu.VMEM((CELL_ROWS, 128), F32), pltpu.VMEM((CELL_ROWS, 128), F32), pltpu.VMEM((WIN, TILE), F32),
                pltpu.VMEM((CELL_ROWS, D), F32), pltpu.VMEM((CELL_ROWS, D), F32), pltpu.VMEM((SLOT, 3 * D), BF),
            ],
        ),
        out_shape=[
            jax.ShapeDtypeStruct((count, SLOT, D), BF), jax.ShapeDtypeStruct((D, 3 * D), F32),
            jax.ShapeDtypeStruct((8, D), F32),
        ],
        compiler_params=pltpu.CompilerParams(vmem_limit_bytes=LIMIT),
        name="attention_backward",
    )(
        lens, x, n1, q, k, v, attn, lse, g1, gain, wq, wk, wv, wo,
        const["mask"], const["pool_q"], const["pool_s"], const["spread"], const["level_mask"], const["spread_k"],
    )


def own_sequences(values, lengths, tensor_count):
    micro, rows, width = values[0].shape
    t = lax.axis_index("tensor")
    if rows % SLOT == 0:
        per = rows // SLOT
        own = lax.dynamic_slice_in_dim(lengths, t * per, per, 1).reshape(-1)
        return [v.reshape(micro * per, SLOT, width) for v in values], own
    pieces = SLOT // rows
    assert micro == pieces
    groups = [[g * pieces + j for j in range(pieces)] for g in range(tensor_count // pieces)]
    out = [lax.all_to_all(v, "tensor", 0, 1, axis_index_groups=groups, tiled=True) for v in values]
    sequence = lax.dynamic_slice(lengths, (t % pieces, t // pieces), (1, 1))
    return out, sequence.reshape(-1)


def own_rows(values, shape, tensor_count):
    micro, rows, width = shape
    if rows % SLOT == 0:
        return [v.reshape(shape) for v in values]
    pieces = SLOT // rows
    groups = [[g * pieces + j for j in range(pieces)] for g in range(tensor_count // pieces)]
    return [
        lax.all_to_all(v, "tensor", 1, 0, axis_index_groups=groups, tiled=True).reshape(shape) for v in values
    ]


def core(x, lens, cot, pre_gain, pre_shift, wq, wk, wv, bq, bv, wo, bo, mid_gain, mid_shift, up, bup, down, bdown):
    const = {name: jnp.asarray(value) for name, value in constants().items()}
    count = x.shape[0]
    flat = (count * SLOT, D)
    n1, q, k, v, attn, lse = attention_forward(x, lens, pre_gain, pre_shift, wq, wk, wv, bq, bv, const)
    out, g1, gwo, gup, gdown_t, mid_vec, gbup = middle(
        x.reshape(flat), attn.reshape(flat), cot.reshape(flat), wo, bo, mid_gain, mid_shift, up, bup, down, bdown
    )
    dx, gqkv, pre_vec = attention_backward(
        x, lens, n1, q, k, v, attn, lse, g1.reshape(count, SLOT, D), pre_gain, wq, wk, wv, wo, const
    )
    return out, dx, gwo, gup, gdown_t, mid_vec, gbup, gqkv, pre_vec


def on_device(
    inputs, lengths, pre_gain, pre_shift, query_weight, key_weight, value_weight, query_bias, value_bias,
    output_weight, output_bias, mid_gain, mid_shift, up_weight, up_bias, down_weight, down_bias, cotangent,
):
    tensor_count = lax.axis_size("tensor")
    t = lax.axis_index("tensor")
    (x, cot), lens = own_sequences([inputs, cotangent], lengths, tensor_count)

    def gather(shard, dp_dim):
        part = lax.all_gather(shard, "dp", axis=dp_dim, tiled=True)
        return lax.all_gather(part, "tensor", axis=1 - dp_dim, tiled=True)

    def row(v):
        return v.astype(F32).reshape(1, -1)

    wq, wk, wv = (gather(w, 0) for w in (query_weight, key_weight, value_weight))
    wo, up, down = gather(output_weight, 1), gather(up_weight, 0), gather(down_weight, 1)
    biases = lax.all_gather(
        jnp.concatenate([query_bias, value_bias, up_bias]), "tensor", axis=0, tiled=False
    )
    width = query_bias.shape[0]
    bq, bv, bup = biases[:, :width], biases[:, width : 2 * width], biases[:, 2 * width :]
    out, dx, gwo, gup, gdown_t, mid_vec, gbup, gqkv, pre_vec = core(
        x, lens, cot, row(pre_gain), row(pre_shift), wq, wk, wv, row(bq), row(bv), wo, row(output_bias),
        row(mid_gain), row(mid_shift), up, row(bup), down, row(down_bias),
    )

    def scatter(grad, dp_dim):
        part = lax.psum_scatter(grad.astype(BF), "tensor", scatter_dimension=1 - dp_dim, tiled=True)
        return lax.psum_scatter(part, "dp", scatter_dimension=dp_dim, tiled=True).astype(F32)

    grad_q, grad_k, grad_v = (scatter(gqkv[:, D * j : D * j + D], 0) for j in range(3))
    grad_o, grad_up, grad_down = scatter(gwo, 1), scatter(gup, 0), scatter(gdown_t.T, 1)
    vec = lax.psum(jnp.concatenate([pre_vec[:4], mid_vec[:4], gbup.reshape(4, D)], axis=0), ("dp", "tensor"))

    def mine(v):
        n = v.shape[0] // tensor_count
        return lax.dynamic_slice_in_dim(v, t * n, n, 0)

    out, dx = own_rows([out.reshape(x.shape), dx], inputs.shape, tensor_count)
    return (
        out, dx, vec[0], vec[1], grad_q, grad_k, grad_v, mine(vec[2]), mine(vec[3]), grad_o, vec[4], vec[5], vec[6],
        grad_up, mine(vec[8:].reshape(-1)), grad_down, vec[7],
    )


def solution(mesh):
    rows = P(None, ("dp", "tensor"), None)
    by_row, by_column = P("dp", "tensor"), P("tensor", "dp")
    in_specs = (
        rows, P(None, "dp"), P(), P(), by_row, by_row, by_row, P("tensor"), P("tensor"), by_column, P(), P(), P(),
        by_row, P("tensor"), by_column, P(), rows,
    )
    out_specs = (
        rows, rows, P(), P(), by_row, by_row, by_row, P("tensor"), P("tensor"), by_column, P(), P(), P(),
        by_row, P("tensor"), by_column, P(),
    )
    return jax.shard_map(on_device, mesh=mesh, in_specs=in_specs, out_specs=out_specs, check_vma=False)
```

```python
import functools

import jax
import jax.numpy as jnp
import ml_dtypes
import numpy as np
from jax import lax
from jax.experimental import pallas as pl
from jax.experimental.pallas import tpu as pltpu
from jax.sharding import PartitionSpec as P

D = 512
HD = 64
FF = 2048
NR = 16
LEVELS = 6
SLOT = 1024
TILE = 128
TILES = SLOT // TILE
PAIRS = D // 128
HEADS = D // HD
HALF = D // 2
REST = HALF + FF
EPS = 1e-05
NEG = -1e30

BASE = (0, 1056, 1600, 1888, 2048, 2144)
CELL_ROWS = 2176
WIN_ROWS = (160, 96, 64, 32, 32, 16)
WIN_AT = (0, 160, 256, 320, 352, 384)
WIN = 400
COARSE = WIN - 160
LANE_AT = (0, 0, 64, 96, 112, 120)
BF = jnp.bfloat16
F32 = jnp.float32


def window_parts(i):
    two, four = i // 2, i // 4
    return (
        (128 * i, 160),
        (BASE[1] + 64 * i, 96),
        (BASE[2] + 32 * i, 64),
        (BASE[3] + 16 * i, 16),
        (BASE[3] + 16 * i + 32, 16),
        (BASE[4] + 16 * two, 16),
        (BASE[4] + 16 * two + 32, 16),
        (BASE[5] + 16 * (1 - four), 16),
    )


def mask_table():
    table = np.full((TILES, WIN, TILE), NEG, np.float32)
    rows = np.arange(TILE)
    for i in range(TILES):
        at = 0
        for start, count in window_parts(i):
            level = max(l for l in range(LEVELS) if WIN_AT[l] <= at)
            pad = 0 if level == 5 else 16
            cell = (start - BASE[level] - pad + np.arange(count))[:, None]
            query = ((128 * i + rows) >> level)[None, :]
            good = np.abs(cell // 16 - query // 16) <= 1
            if level > 0:
                good &= np.abs((2 * cell) // 16 - (2 * query) // 16) > 1
            table[i, at : at + count] = np.where(good, 0.0, NEG)
            at += count
    return table


def constants():
    t = np.arange(TILE)
    pool_q = np.zeros((TILE, TILE), np.float32)
    pool_s = np.zeros((TILE, TILE), np.float32)
    spread = np.zeros((COARSE, TILE), np.int32)
    level_mask = np.zeros((COARSE, TILE), np.float32)
    pool_k = np.zeros((256, 256), np.float32)
    t2 = np.arange(256)
    at = 0
    for level in range(1, LEVELS):
        width = 2**level
        pool_q[LANE_AT[level] + t // width, t] = 1.0 / width
        pool_s[t, LANE_AT[level] + t // width] = 1.0
        rows = slice(WIN_AT[level] - 160, WIN_AT[level] - 160 + WIN_ROWS[level])
        spread[rows] = LANE_AT[level] + t // width
        level_mask[rows, LANE_AT[level] : LANE_AT[level] + TILE // width] = 1.0
        pool_k[at + t2 // width, t2] = 1.0
        at += 256 // width
    half = ml_dtypes.bfloat16
    return {
        "mask": mask_table(),
        "pool_q": pool_q.astype(half),
        "pool_s": pool_s.astype(half),
        "spread": spread,
        "level_mask": level_mask,
        "pool_k": pool_k.astype(half),
        "spread_k": pool_k.T.copy().astype(half),
    }


def mm(a, b):
    return lax.dot_general(a, b, (((1,), (0,)), ((), ())), preferred_element_type=F32)


def mm_nt(a, b):
    return lax.dot_general(a, b, (((1,), (1,)), ((), ())), preferred_element_type=F32)


def mm_tn(a, b):
    return lax.dot_general(a, b, (((0,), (0,)), ((), ())), preferred_element_type=F32)


def norm_parts(values):
    centre = values - jnp.mean(values, axis=-1, keepdims=True)
    spread = jnp.mean(centre * centre, axis=-1, keepdims=True)
    scale = lax.rsqrt(spread + EPS)
    return centre * scale, scale


def norm_back(grad, xhat, scale, gain):
    e = grad * gain
    return (e - jnp.mean(e, axis=-1, keepdims=True) - xhat * jnp.mean(e * xhat, axis=-1, keepdims=True)) * scale


def column_sum(values):
    return jnp.sum(values, axis=0, keepdims=True)


def count_tables(length, bias_ref, inv_ref):
    for level in range(LEVELS):
        width = 2**level
        pad = 0 if level == 5 else 16
        count = SLOT // width + 2 * pad
        cell = lax.broadcasted_iota(jnp.int32, (count, 128), 0) - pad
        live = jnp.clip(length - cell * width, 0, width)
        live = jnp.where(cell < 0, 0, live)
        live_f = live.astype(F32)
        some = jnp.maximum(live_f, 1.0)
        rows = pl.ds(BASE[level], count)
        bias_ref[rows, :] = jnp.where(live > 0, jnp.log(some), NEG)
        inv_ref[rows, :] = 1.0 / some


def window(ref, i, lanes):
    parts = []
    for start, count in window_parts(i):
        parts.append(ref[pl.ds(pl.multiple_of(start, 16), count), lanes])
    return jnp.concatenate(parts, axis=0)


def two_columns(block):
    zero = jnp.zeros((64, block.shape[1]), block.dtype)
    top = jnp.concatenate([block[:64], zero], axis=1)
    low = jnp.concatenate([zero, block[64:]], axis=1)
    return jnp.concatenate([top, low], axis=0)


def two_rows(block):
    first = lax.broadcasted_iota(jnp.int32, block.shape, 1) < 64
    zero = jnp.zeros_like(block)
    return jnp.concatenate([jnp.where(first, block, zero), jnp.where(first, zero, block)], axis=0)


def diagonal(block):
    n = block.shape[1] // 2
    return jnp.concatenate([block[:64, :n], block[64:, n:]], axis=0)


def pair_scores(keys, queries_t, cells_t, spread, bias):
    fine = mm(keys[:160], two_columns(queries_t))
    rough = mm(keys[160:], two_columns(cells_t))
    out = []
    for h in range(2):
        lanes = slice(128 * h, 128 * h + 128)
        wide = jnp.take_along_axis(rough[:, lanes], spread, axis=1)
        out.append(jnp.concatenate([fine[:, lanes], wide], axis=0) + bias)
    return out


def pack_cells(full, length, chunk, out_ref, rough_ref, inv_ref, pool):
    row = lax.broadcasted_iota(jnp.int32, full.shape, 0) + 256 * chunk
    live = jnp.where(row < length, full, 0.0).astype(BF)
    out_ref[0, pl.ds(pl.multiple_of(16 + 256 * chunk, 16), 256), :] = live
    sums = mm(pool, live)
    at = 0
    for level in range(1, LEVELS):
        count = 256 // 2**level
        pad = 0 if level == 5 else 16
        rows = pl.ds(pl.multiple_of(BASE[level] + pad + count * chunk, 8), count)
        inv = jnp.concatenate([inv_ref[rows, :]] * PAIRS, axis=1)
        cells = sums[at : at + count] * inv
        if level == 5:
            rough_ref[pl.ds(pl.multiple_of(8 * chunk, 8), 8), :] = cells
        else:
            out_ref[0, pl.ds(pl.multiple_of(BASE[level] + 16 + count * chunk, 16), count), :] = cells.astype(BF)
        at += count


def forward_kernel(
    lens, x_ref, gain_ref, shift_ref, w_ref, bq_ref, bv_ref,
    mask_ref, pool_q_ref, spread_ref, pool_k_ref,
    n1_ref, q_ref, k_ref, v_ref, attn_ref, low_ref, lse_ref,
    bias_ref, inv_ref, rough_ref, tile_bias_ref,
):
    length = lens[pl.program_id(0)]
    count_tables(length, bias_ref, inv_ref)
    zeros = jnp.zeros((16, D), BF)
    for level in range(LEVELS - 1):
        cells = SLOT // 2**level
        for ref in (k_ref, v_ref):
            ref[0, pl.ds(BASE[level], 16), :] = zeros
            ref[0, pl.ds(BASE[level] + 16 + cells, 16), :] = zeros
    rough_k, rough_v = rough_ref.at[0], rough_ref.at[1]

    def project(chunk, carry):
        rows = pl.ds(pl.multiple_of(256 * chunk, 256), 256)
        xhat, _ = norm_parts(x_ref[0, rows, :].astype(F32))
        n1 = (xhat * gain_ref[...] + shift_ref[...]).astype(BF)
        n1_ref[0, rows, :] = n1
        joint = [mm(n1, w_ref[t]) for t in range(2)]
        q, k, v = (jnp.concatenate([j[:, at : at + HALF] for j in joint], axis=1) for at in (0, HALF, 2 * HALF))
        q_ref[0, rows, :] = (q + bq_ref[...]).astype(BF) * BF(0.125)
        pool = pool_k_ref[...]
        pack_cells(k, length, chunk, k_ref, rough_k, inv_ref, pool)
        pack_cells(v + bv_ref[...], length, chunk, v_ref, rough_v, inv_ref, pool)
        return carry

    lax.fori_loop(0, 4, project, 0)
    k_ref[0, pl.ds(BASE[5], 32), :] = rough_k[...].astype(BF)
    v_ref[0, pl.ds(BASE[5], 32), :] = rough_v[...].astype(BF)

    def attend(i, carry):
        rows = pl.ds(pl.multiple_of(128 * i, 128), 128)
        tile_bias_ref[...] = mask_ref[i] + window(bias_ref, i, slice(None))
        q = q_ref[0, rows, :]
        cells = mm(pool_q_ref[...], q).astype(BF)
        lse = []
        for pair in range(PAIRS):
            lanes = slice(128 * pair, 128 * pair + 128)
            keys = window(k_ref.at[0], i, lanes)
            values = window(v_ref.at[0], i, lanes)
            scores = pair_scores(keys, q[:, lanes].T, cells[:, lanes].T, spread_ref[...], tile_bias_ref[...])
            shares, inverse = [], []
            for s in scores:
                top = jnp.max(s, axis=0, keepdims=True)
                p = jnp.exp(s - top)
                total = jnp.sum(p, axis=0, keepdims=True)
                shares.append(p.astype(BF))
                inverse.append(1.0 / total)
                lse.append(top + jnp.log(total))
            mixed = mm_tn(values, jnp.concatenate(shares, axis=1))
            mixed = diagonal(mixed * jnp.concatenate(inverse, axis=1))
            mixed = mixed.T
            high = mixed.astype(BF)
            attn_ref[0, rows, lanes] = high
            low_ref[0, rows, lanes] = (mixed - high.astype(F32)).astype(BF)
        lse_ref[0, :, rows] = jnp.concatenate(lse, axis=0)
        return carry

    lax.fori_loop(0, TILES, attend, 0)


def middle_kernel(
    x_ref, attn_ref, cot_ref, w_ref, bo_ref, gain_ref, shift_ref, bup_ref, bdown_ref,
    out_ref, g1_ref, grad_ref, gvec_ref, gbup_ref,
    gwo_ref, gup_ref, gdown_ref,
):
    step = pl.program_id(0)

    @pl.when(step == 0)
    def _():
        gwo_ref[...] = jnp.zeros_like(gwo_ref)
        gup_ref[...] = jnp.zeros_like(gup_ref)
        gdown_ref[...] = jnp.zeros_like(gdown_ref)
        gvec_ref[...] = jnp.zeros_like(gvec_ref)
        gbup_ref[...] = jnp.zeros_like(gbup_ref)

    attn = attn_ref[...]
    cot = cot_ref[...]
    branch = sum(mm_nt(attn[:, HALF * t : HALF * t + HALF], w_ref[:, t, :, :HALF].reshape(D, HALF)) for t in range(2))
    y1 = x_ref[...].astype(F32) + (branch + bo_ref[...])
    xhat, scale = norm_parts(y1)
    n2 = (xhat * gain_ref[...] + shift_ref[...]).astype(BF)
    n2_t = n2.T
    cot_t = cot.T
    out = y1 + bdown_ref[...]
    dn2 = jnp.zeros_like(y1)
    c = np.float32(np.sqrt(2.0 / np.pi))
    for part in range(4):
        cols = slice(512 * part, 512 * part + 512)
        at = HALF + 512 * (part % 2)
        up = w_ref[:, part // 2, :, at : at + 512].reshape(D, 512)
        at += FF // 2
        down_t = w_ref[:, part // 2, :, at : at + 512].reshape(D, 512)
        u = mm(n2, up) + bup_ref[:, cols]
        dh = mm(cot, down_t)
        u2 = u * u
        t = jnp.tanh(u * (c + (c * 0.044715) * u2))
        h = 0.5 + 0.5 * t
        hid = (u * h).astype(BF)
        slope = h + 2.0 * h * (1.0 - h) * u * (c + (3.0 * c * 0.044715) * u2)
        dhp = dh * slope
        dhp_b = dhp.astype(BF)
        gbup_ref[:, cols] += column_sum(dhp)
        out = out + mm_nt(hid, down_t)
        dn2 = dn2 + mm_nt(dhp_b, up)
        gdown_ref[:, cols] += mm(cot_t, hid)
        gup_ref[:, cols] += mm(n2_t, dhp_b)
    out_ref[...] = out.astype(BF)
    cot_f = cot.astype(F32)
    dy1 = cot_f + norm_back(dn2, xhat, scale, gain_ref[...])
    g1 = dy1.astype(BF)
    g1_ref[...] = g1
    gwo_ref[...] += mm(g1.T, attn)
    gvec_ref[...] += jnp.concatenate(
        [column_sum(g1.astype(F32)), column_sum(dn2 * xhat), column_sum(dn2), column_sum(cot_f), jnp.zeros((4, D), F32)],
        axis=0,
    )


    @pl.when(step == pl.num_programs(0) - 1)
    def _():
        rows = D // grad_ref.shape[0]
        for t in range(2):
            at = 0
            for ref, width in ((gwo_ref, HALF), (gup_ref, FF // 2), (gdown_ref, FF // 2)):
                part = ref[:, width * t : width * t + width].astype(BF)
                grad_ref[:, t, :, at : at + width] = part.reshape(grad_ref.shape[0], rows, width)
                at += width


def backward_kernel(
    lens, x_ref, n1_ref, q_ref, k_ref, v_ref, attn_ref, low_ref, lse_ref, g1_ref,
    gain_ref, w_ref, wo_t_ref,
    mask_ref, pool_q_ref, pool_s_ref, spread_ref, level_mask_ref, spread_k_ref,
    dx_ref, gqkv_ref, gvec_ref,
    bias_ref, inv_ref, tile_bias_ref, dk_ref, dv_ref, dqkv_ref,
):
    step = pl.program_id(0)

    @pl.when(step == 0)
    def _():
        gqkv_ref[...] = jnp.zeros_like(gqkv_ref)
        gvec_ref[...] = jnp.zeros_like(gvec_ref)

    length = lens[step]
    count_tables(length, bias_ref, inv_ref)
    dk_ref[...] = jnp.zeros_like(dk_ref)
    dv_ref[...] = jnp.zeros_like(dv_ref)
    head_of = lax.broadcasted_iota(jnp.int32, (HEADS, D), 1) // HD
    heads = (head_of == lax.broadcasted_iota(jnp.int32, (HEADS, D), 0)).astype(BF)

    def attend(i, carry):
        rows = pl.ds(pl.multiple_of(128 * i, 128), 128)
        tile_bias_ref[...] = mask_ref[i] + window(bias_ref, i, slice(None))
        q = q_ref[0, rows, :]
        cells = mm(pool_q_ref[...], q).astype(BF)
        da = jnp.concatenate([mm(g1_ref[0, rows, :], wo_t_ref[:, t, :, :HALF].reshape(D, HALF)) for t in range(2)], axis=1)
        da = da.astype(BF)
        product = da.astype(F32) * (attn_ref[0, rows, :].astype(F32) + low_ref[0, rows, :].astype(F32))
        high = product.astype(BF)
        delta = mm_nt(heads, high) + mm_nt(heads, (product - high.astype(F32)).astype(BF))
        lse = lse_ref[0, :, rows]
        for pair in range(PAIRS):
            lanes = slice(128 * pair, 128 * pair + 128)
            keys = window(k_ref.at[0], i, lanes)
            values = window(v_ref.at[0], i, lanes)
            scores = pair_scores(keys, q[:, lanes].T, cells[:, lanes].T, spread_ref[...], tile_bias_ref[...])
            dp = mm(values, two_columns(da[:, lanes].T))
            shares, fine, rough = [], [], []
            for h in range(2):
                head = 2 * pair + h
                p = jnp.exp(scores[h] - lse[head : head + 1])
                ds = (p * (dp[:, 128 * h : 128 * h + 128] - delta[head : head + 1])).astype(BF)
                shares.append(p.astype(BF))
                fine.append(ds[:160])
                pooled = mm(ds[160:], pool_s_ref[...]) * level_mask_ref[...]
                rough.append(pooled.astype(BF))
            shares = jnp.concatenate(shares, axis=1)
            fine = jnp.concatenate(fine, axis=1)
            rough = jnp.concatenate(rough, axis=1)
            dv = mm(shares, two_rows(da[:, lanes]))
            dk = jnp.concatenate([mm(fine, two_rows(q[:, lanes])), mm(rough, two_rows(cells[:, lanes]))], axis=0)
            at = 0
            for start, count in window_parts(i):
                part = pl.ds(pl.multiple_of(start, 16), count)
                dk_ref[part, lanes] += dk[at : at + count]
                dv_ref[part, lanes] += dv[at : at + count]
                at += count
            dq = diagonal(mm_tn(keys[:160], fine))
            dq_cells = diagonal(mm_tn(keys[160:], rough)).astype(BF)
            dq = (dq + mm(dq_cells, pool_q_ref[...])) * 0.125
            at = 3 * HALF * (pair // 2) + 128 * (pair % 2)
            dqkv_ref[rows, at : at + 128] = dq.T.astype(BF)
        return carry

    lax.fori_loop(0, TILES, attend, 0)

    def finish(chunk, carry):
        rows = pl.ds(pl.multiple_of(256 * chunk, 256), 256)
        own = pl.ds(pl.multiple_of(16 + 256 * chunk, 16), 256)
        live = lax.broadcasted_iota(jnp.int32, (256, D), 0) + 256 * chunk < length
        for ref, at in ((dk_ref, HALF), (dv_ref, 2 * HALF)):
            cells = []
            for level in range(1, LEVELS):
                count = 256 // 2**level
                pad = 0 if level == 5 else 16
                part = pl.ds(pl.multiple_of(BASE[level] + pad + count * chunk, 8), count)
                cells.append(ref[part, :] * jnp.concatenate([inv_ref[part, :]] * PAIRS, axis=1))
            cells.append(jnp.zeros((8, D), F32))
            wide = mm(spread_k_ref[...], jnp.concatenate(cells, axis=0).astype(BF))
            grad = jnp.where(live, ref[own, :] + wide, 0.0).astype(BF)
            dqkv_ref[rows, at : at + HALF] = grad[:, :HALF]
            dqkv_ref[rows, at + 3 * HALF : at + 4 * HALF] = grad[:, HALF:]
        n1 = n1_ref[0, rows, :]
        parts = [dqkv_ref[rows, 3 * HALF * t : 3 * HALF * t + 3 * HALF] for t in range(2)]
        dn1 = mm_nt(parts[0], w_ref[0]) + mm_nt(parts[1], w_ref[1])
        xhat, scale = norm_parts(x_ref[0, rows, :].astype(F32))
        dx = g1_ref[0, rows, :].astype(F32) + norm_back(dn1, xhat, scale, gain_ref[...])
        dx_ref[0, rows, :] = dx.astype(BF)
        n1_t = n1.T
        for t in range(2):
            gqkv_ref[t] += mm(n1_t, parts[t])
        sums = [column_sum(part.astype(F32)) for part in parts]
        gvec_ref[...] += jnp.concatenate(
            [
                column_sum(dn1 * xhat), column_sum(dn1),
                jnp.concatenate([sums[0][:, :HALF], sums[1][:, :HALF]], axis=1),
                jnp.concatenate([sums[0][:, 2 * HALF :], sums[1][:, 2 * HALF :]], axis=1),
                jnp.zeros((4, D), F32),
            ],
            axis=0,
        )
        return carry

    lax.fori_loop(0, 4, finish, 0)


def whole(shape):
    return pl.BlockSpec(shape, lambda *_: (0,) * len(shape))


def per_sequence(*shape):
    return pl.BlockSpec((1,) + shape, lambda s, *_: (s,) + (0,) * len(shape))


LIMIT = 60 * 1024 * 1024


def attention_forward(x, lens, gain, shift, w, bq, bv, const):
    count = x.shape[0]
    return pl.pallas_call(
        forward_kernel,
        grid_spec=pltpu.PrefetchScalarGridSpec(
            num_scalar_prefetch=1,
            grid=(count,),
            in_specs=[
                per_sequence(SLOT, D), whole((1, D)), whole((1, D)),
                whole((2, D, 3 * HALF)), whole((1, D)), whole((1, D)),
                whole((TILES, WIN, TILE)), whole((TILE, TILE)), whole((COARSE, TILE)), whole((256, 256)),
            ],
            out_specs=[
                per_sequence(SLOT, D), per_sequence(SLOT, D), per_sequence(CELL_ROWS, D), per_sequence(CELL_ROWS, D),
                per_sequence(SLOT, D), per_sequence(SLOT, D), per_sequence(HEADS, SLOT),
            ],
            scratch_shapes=[
                pltpu.VMEM((CELL_ROWS, 128), F32), pltpu.VMEM((CELL_ROWS, 128), F32), pltpu.VMEM((2, 32, D), F32),
                pltpu.VMEM((WIN, TILE), F32),
            ],
        ),
        out_shape=[
            jax.ShapeDtypeStruct((count, SLOT, D), BF), jax.ShapeDtypeStruct((count, SLOT, D), BF),
            jax.ShapeDtypeStruct((count, CELL_ROWS, D), BF), jax.ShapeDtypeStruct((count, CELL_ROWS, D), BF),
            jax.ShapeDtypeStruct((count, SLOT, D), BF), jax.ShapeDtypeStruct((count, SLOT, D), BF),
            jax.ShapeDtypeStruct((count, HEADS, SLOT), F32),
        ],
        compiler_params=pltpu.CompilerParams(vmem_limit_bytes=LIMIT),
        cost_estimate=pl.CostEstimate(flops=count * 30 * 10**9, bytes_accessed=count * 10**7, transcendentals=0),
        name="attention_forward",
    )(lens, x, gain, shift, w, bq, bv, const["mask"], const["pool_q"], const["spread"], const["pool_k"])


ROWS = 512


def middle(x, attn, cot, w, bo, gain, shift, bup, bdown):
    total = x.shape[0]
    rows = pl.BlockSpec((ROWS, D), lambda s: (s, 0))
    return pl.pallas_call(
        middle_kernel,
        grid=(total // ROWS,),
        in_specs=[
            rows, rows, rows, whole(w.shape), whole((1, D)), whole((1, D)), whole((1, D)), whole((1, FF)), whole((1, D)),
        ],
        out_specs=[rows, rows, whole(w.shape), whole((8, D)), whole((1, FF))],
        scratch_shapes=[pltpu.VMEM((D, D), F32), pltpu.VMEM((D, FF), F32), pltpu.VMEM((D, FF), F32)],
        out_shape=[
            jax.ShapeDtypeStruct((total, D), BF), jax.ShapeDtypeStruct((total, D), BF), jax.ShapeDtypeStruct(w.shape, BF),
            jax.ShapeDtypeStruct((8, D), F32), jax.ShapeDtypeStruct((1, FF), F32),
        ],
        compiler_params=pltpu.CompilerParams(vmem_limit_bytes=LIMIT),
        name="middle",
    )(x, attn, cot, w, bo, gain, shift, bup, bdown)


def attention_backward(x, lens, n1, q, k, v, attn, low, lse, g1, gain, w, rest, const):
    count = x.shape[0]
    wo_t = pl.BlockSpec(rest.shape[:3] + (HALF,), lambda *_: (0, 0, 0, 0))
    return pl.pallas_call(
        backward_kernel,
        grid_spec=pltpu.PrefetchScalarGridSpec(
            num_scalar_prefetch=1,
            grid=(count,),
            in_specs=[
                per_sequence(SLOT, D), per_sequence(SLOT, D), per_sequence(SLOT, D),
                per_sequence(CELL_ROWS, D), per_sequence(CELL_ROWS, D), per_sequence(SLOT, D), per_sequence(SLOT, D),
                per_sequence(HEADS, SLOT), per_sequence(SLOT, D),
                whole((1, D)), whole((2, D, 3 * HALF)), wo_t,
                whole((TILES, WIN, TILE)), whole((TILE, TILE)), whole((TILE, TILE)), whole((COARSE, TILE)),
                whole((COARSE, TILE)), whole((256, 256)),
            ],
            out_specs=[per_sequence(SLOT, D), whole((2, D, 3 * HALF)), whole((8, D))],
            scratch_shapes=[
                pltpu.VMEM((CELL_ROWS, 128), F32), pltpu.VMEM((CELL_ROWS, 128), F32), pltpu.VMEM((WIN, TILE), F32),
                pltpu.VMEM((CELL_ROWS, D), F32), pltpu.VMEM((CELL_ROWS, D), F32), pltpu.VMEM((SLOT, 3 * D), BF),
            ],
        ),
        out_shape=[
            jax.ShapeDtypeStruct((count, SLOT, D), BF), jax.ShapeDtypeStruct((2, D, 3 * HALF), F32),
            jax.ShapeDtypeStruct((8, D), F32),
        ],
        compiler_params=pltpu.CompilerParams(vmem_limit_bytes=LIMIT),
        cost_estimate=pl.CostEstimate(flops=count * 40 * 10**9, bytes_accessed=count * 10**7, transcendentals=0),
        name="attention_backward",
    )(
        lens, x, n1, q, k, v, attn, low, lse, g1, gain, w, rest,
        const["mask"], const["pool_q"], const["pool_s"], const["spread"], const["level_mask"], const["spread_k"],
    )


def bits_of(count):
    return count.bit_length() - 1


def all_bits(n_dp, n_t):
    return [("tensor", b) for b in reversed(range(bits_of(n_t)))] + [("dp", b) for b in reversed(range(bits_of(n_dp)))]


def gather_orders(n_dp, n_t):
    far = [("dp", b) for b in reversed(range(2, bits_of(n_dp)))]
    near = [("dp", 1)]
    side = [("tensor", b) for b in reversed(range(bits_of(n_t)))]
    core_bit = [("dp", 0)]
    return far + near + side + core_bit, far + side + near + core_bit


def own_bit(bit):
    axis, b = bit
    return (lax.axis_index(axis) // 2**b) % 2


def partner(bit):
    axis, b = bit
    return {axis: lax.axis_index(axis) + (1 - 2 * own_bit(bit)) * 2**b}


def meet(bits):
    barrier = pltpu.get_barrier_semaphore()
    for bit in bits:
        pl.semaphore_signal(barrier, inc=1, device_id=partner(bit), device_id_type=pl.DeviceIdType.MESH)
    pl.semaphore_wait(barrier, len(bits))


def halves(width):
    if width % 256:
        return [(0, width)]
    return [(0, width // 2), (width // 2, width // 2)]


def gather_kernel(bits, orders, parts, shard_ref, out_ref, own_sem, send_sems, recv_sems):
    own = pltpu.make_async_copy(shard_ref, out_ref.at[tuple(own_bit(bit) for bit in bits)], own_sem)
    own.start()
    meet(bits)
    pending = []
    for step in range(len(bits)):
        for part, (at, width) in enumerate(parts):
            order = orders[part]
            done = order[:step]
            index = tuple(slice(None) if bit in done else own_bit(bit) for bit in bits)
            place = out_ref.at[index + (slice(None), pl.ds(at, width))]
            source = shard_ref.at[:, pl.ds(at, width)] if step == 0 else place
            if step > 0:
                pending[(step - 1) * len(parts) + part].wait_recv()
            copy = pltpu.make_async_remote_copy(
                src_ref=source, dst_ref=place,
                send_sem=send_sems.at[step, part], recv_sem=recv_sems.at[step, part],
                device_id=partner(order[step]), device_id_type=pl.DeviceIdType.MESH,
            )
            if step == 1 and part == 0:
                own.wait()
            copy.start()
            pending.append(copy)
    for copy in pending[-len(parts) :]:
        copy.wait_recv()
    for copy in pending:
        copy.wait_send()


def gather(shard, n_dp, n_t):
    rows, width = shard.shape
    bits, orders, parts = all_bits(n_dp, n_t), gather_orders(n_dp, n_t), halves(width)
    out = pl.pallas_call(
        functools.partial(gather_kernel, bits, orders, parts),
        in_specs=[pl.BlockSpec(memory_space=pl.ANY)],
        out_specs=pl.BlockSpec(memory_space=pl.ANY),
        out_shape=jax.ShapeDtypeStruct((2,) * len(bits) + (rows, width), shard.dtype),
        scratch_shapes=[
            pltpu.SemaphoreType.DMA, pltpu.SemaphoreType.DMA((len(bits), len(parts))),
            pltpu.SemaphoreType.DMA((len(bits), len(parts))),
        ],
        compiler_params=pltpu.CompilerParams(collective_id=0, has_side_effects=True),
        name="gather",
    )(shard)
    return out.reshape(n_t, n_dp, rows, width)


def reduce_kernel(bits, orders, parts, rows, grad_ref, vec_ref, out_ref, vec_out_ref, *scratch):
    steps, count = len(bits), len(parts)
    sends, recvs, sums = (scratch[j * steps * count : (j + 1) * steps * count] for j in range(3))
    vec_recv, send_sems, recv_sems, vec_send_sems, vec_recv_sems = scratch[3 * steps * count :]
    meet(bits)
    vec_out_ref[...] = vec_ref[...]

    def vec_copy(step):
        return pltpu.make_async_remote_copy(
            src_ref=vec_recv.at[2 * step], dst_ref=vec_recv.at[2 * step + 1],
            send_sem=vec_send_sems.at[step], recv_sem=vec_recv_sems.at[step],
            device_id=partner(orders[0][steps - 1 - step]), device_id_type=pl.DeviceIdType.MESH,
        )

    def copy_of(step, part):
        j = step * count + part
        return pltpu.make_async_remote_copy(
            src_ref=sends[j], dst_ref=recvs[j], send_sem=send_sems.at[step, part], recv_sem=recv_sems.at[step, part],
            device_id=partner(orders[part][steps - 1 - step]), device_id_type=pl.DeviceIdType.MESH,
        )

    def pieces(step, part):
        order = orders[part][::-1]
        left = [bit for bit in bits if bit not in order[:step]]
        j = left.index(order[step])
        low = 2 ** (len(left) - 1 - j)
        mine = own_bit(order[step])
        out = []
        for a in range(2**j):
            for c in range(low):
                out.append(((a * 2 + 1 - mine) * low + c, (a * 2 + mine) * low + c, a * low + c))
        at, width = parts[part]
        source = sums[(step - 1) * count + part] if step else grad_ref.at[:, :, pl.ds(at, width)]
        return out, source

    for step in range(steps):
        vec_recv[2 * step] = vec_out_ref[...]
        vec_copy(step).start()
        for part in range(count):
            blocks, source = pieces(step, part)
            for away, _, to in blocks:
                sends[step * count + part][to] = source[away].astype(BF)
            copy_of(step, part).start()
        for part in range(count):
            copy_of(step, part).wait_recv()
            blocks, source = pieces(step, part)
            for _, keep, to in blocks:
                total = source[keep] + recvs[step * count + part][to].astype(F32)
                if step == steps - 1:
                    at, width = parts[part]
                    out_ref[:, at : at + width] = total
                else:
                    sums[step * count + part][to] = total
        vec_copy(step).wait_recv()
        vec_out_ref[...] += vec_recv[2 * step + 1]
    for step in range(steps):
        vec_copy(step).wait_send()
        for part in range(count):
            copy_of(step, part).wait_send()


def reduce(grad, vec, n_dp, n_t):
    rows, width = grad.shape[2:]
    bits, orders, parts = all_bits(n_dp, n_t), gather_orders(n_dp, n_t), halves(width)
    steps = len(bits)
    blocks = [(2 ** (steps - 1 - step), rows, w) for step in range(steps) for _, w in parts]
    sems = pltpu.SemaphoreType.DMA
    vmem = pl.BlockSpec(memory_space=pltpu.VMEM)
    return pl.pallas_call(
        functools.partial(reduce_kernel, bits, orders, parts, rows),
        in_specs=[vmem, vmem],
        out_specs=[vmem, vmem],
        out_shape=[jax.ShapeDtypeStruct((rows, width), F32), jax.ShapeDtypeStruct(vec.shape, F32)],
        scratch_shapes=[pltpu.VMEM(b, BF) for b in blocks] * 2
        + [pltpu.VMEM(b, F32) for b in blocks]
        + [
            pltpu.VMEM((2 * steps,) + vec.shape, F32), sems((steps, len(parts))), sems((steps, len(parts))),
            sems((steps,)), sems((steps,)),
        ],
        compiler_params=pltpu.CompilerParams(collective_id=1, has_side_effects=True, vmem_limit_bytes=LIMIT),
        name="reduce",
    )(grad.reshape(n_t * n_dp, rows, width), vec)


def to_pairs(grid, widths):
    n_t, n_dp, rows, _ = grid.shape
    grid = grid.reshape(n_t, n_dp * rows, -1)
    if n_t == 2:
        return grid
    out, at = [], 0
    for width in widths:
        part = grid[:, :, at : at + width].reshape(2, n_t // 2, D, width)
        out.append(part.transpose(0, 2, 1, 3).reshape(2, D, n_t // 2 * width))
        at += width
    return jnp.concatenate(out, axis=2)


def from_pairs(grid, widths, n_dp, n_t):
    if n_t != 2:
        out, at = [], 0
        for width in widths:
            full = width * n_t // 2
            part = grid[:, :, at : at + full].reshape(2, D, n_t // 2, width)
            out.append(part.transpose(0, 2, 1, 3).reshape(n_t, D, width))
            at += full
        grid = jnp.concatenate(out, axis=2)
    return grid.reshape(n_t, n_dp, D // n_dp, -1)


def own_sequences(values, lengths, tensor_count):
    micro, rows, width = values[0].shape
    t = lax.axis_index("tensor")
    if rows % SLOT == 0:
        per = rows // SLOT
        own = lax.dynamic_slice_in_dim(lengths, t * per, per, 1).reshape(-1)
        return [v.reshape(micro * per, SLOT, width) for v in values], own
    pieces = SLOT // rows
    assert micro == pieces
    groups = [[g * pieces + j for j in range(pieces)] for g in range(tensor_count // pieces)]
    out = [lax.all_to_all(v, "tensor", 0, 1, axis_index_groups=groups, tiled=True) for v in values]
    sequence = lax.dynamic_slice(lengths, (t % pieces, t // pieces), (1, 1))
    return out, sequence.reshape(-1)


def own_rows(values, shape, tensor_count):
    micro, rows, width = shape
    if rows % SLOT == 0:
        return [v.reshape(shape) for v in values]
    pieces = SLOT // rows
    groups = [[g * pieces + j for j in range(pieces)] for g in range(tensor_count // pieces)]
    return [
        lax.all_to_all(v, "tensor", 1, 0, axis_index_groups=groups, tiled=True).reshape(shape) for v in values
    ]


def core(x, lens, cot, pre_gain, pre_shift, w, bq, bv, rest, bo, mid_gain, mid_shift, bup, bdown):
    const = {name: jnp.asarray(value) for name, value in constants().items()}
    count = x.shape[0]
    flat = (count * SLOT, D)
    n1, q, k, v, attn, low, lse = attention_forward(x, lens, pre_gain, pre_shift, w, bq, bv, const)
    out, g1, grad_rest, mid_vec, gbup = middle(
        x.reshape(flat), attn.reshape(flat), cot.reshape(flat), rest, bo, mid_gain, mid_shift, bup, bdown
    )
    dx, gqkv, pre_vec = attention_backward(
        x, lens, n1, q, k, v, attn, low, lse, g1.reshape(count, SLOT, D), pre_gain, w, rest, const
    )
    return out, dx, grad_rest, mid_vec, gbup, gqkv, pre_vec


def on_device(
    inputs, lengths, pre_gain, pre_shift, query_weight, key_weight, value_weight, query_bias, value_bias,
    output_weight, output_bias, mid_gain, mid_shift, up_weight, up_bias, down_weight, down_bias, cotangent,
):
    n_dp, n_t = lax.axis_size("dp"), lax.axis_size("tensor")
    t = lax.axis_index("tensor")
    (x, cot), lens = own_sequences([inputs, cotangent], lengths, n_t)

    def row(v):
        return v.astype(F32).reshape(1, -1)

    n_q, n_f = query_weight.shape[1], up_weight.shape[1]
    first = jnp.concatenate([query_weight, key_weight, value_weight], axis=1)
    second = jnp.concatenate([output_weight.T, up_weight, down_weight.T], axis=1)
    w = to_pairs(gather(first, n_dp, n_t), (n_q,) * 3)
    rest = lax.all_gather(second, ("dp", "tensor"), axis=0, tiled=False)
    rest = rest.reshape(n_dp, n_t, D // n_dp, -1)
    if n_t != 2:
        rest = to_pairs(rest.transpose(1, 0, 2, 3), (n_q, n_f, n_f)).reshape(2, 16, 32, REST).transpose(1, 0, 2, 3)
    biases = lax.all_gather(jnp.concatenate([query_bias, value_bias, up_bias]), "tensor", axis=0, tiled=False)
    bq, bv, bup = biases[:, :n_q], biases[:, n_q : 2 * n_q], biases[:, 2 * n_q :]
    out, dx, grad_rest, mid_vec, gbup, gqkv, pre_vec = core(
        x, lens, cot, row(pre_gain), row(pre_shift), w, row(bq), row(bv), rest, row(output_bias),
        row(mid_gain), row(mid_shift), row(bup), row(down_bias),
    )
    if n_t != 2:
        grad_rest = grad_rest.transpose(1, 0, 2, 3).reshape(2, D, REST)
        grad_rest = from_pairs(grad_rest, (n_q, n_f, n_f), n_dp, n_t).transpose(1, 0, 2, 3)
    grad_rest = grad_rest.reshape(n_dp * n_t, D // n_dp, -1)
    grad_rest = lax.psum_scatter(grad_rest, ("dp", "tensor"), scatter_dimension=0, tiled=False).astype(F32)
    vec = jnp.concatenate([pre_vec[:4], mid_vec[:4], gbup.reshape(4, D), jnp.zeros((4, D), F32)], axis=0)
    grad_first, vec = reduce(from_pairs(gqkv, (n_q,) * 3, n_dp, n_t), vec, n_dp, n_t)
    grad_q, grad_k, grad_v = (grad_first[:, n_q * j : n_q * j + n_q] for j in range(3))
    grad_o, grad_up, grad_down = grad_rest[:, :n_q].T, grad_rest[:, n_q : n_q + n_f], grad_rest[:, n_q + n_f :].T

    def mine(v):
        n = v.shape[0] // n_t
        return lax.dynamic_slice_in_dim(v, t * n, n, 0)

    out, dx = own_rows([out.reshape(x.shape), dx], inputs.shape, n_t)
    return (
        out, dx, vec[0], vec[1], grad_q, grad_k, grad_v, mine(vec[2]), mine(vec[3]), grad_o, vec[4], vec[5], vec[6],
        grad_up, mine(vec[8:12].reshape(-1)), grad_down, vec[7],
    )


def solution(mesh):
    rows = P(None, ("dp", "tensor"), None)
    by_row, by_column = P("dp", "tensor"), P("tensor", "dp")
    in_specs = (
        rows, P(None, "dp"), P(), P(), by_row, by_row, by_row, P("tensor"), P("tensor"), by_column, P(), P(), P(),
        by_row, P("tensor"), by_column, P(), rows,
    )
    out_specs = (
        rows, rows, P(), P(), by_row, by_row, by_row, P("tensor"), P("tensor"), by_column, P(), P(), P(),
        by_row, P("tensor"), by_column, P(),
    )
    return jax.shard_map(on_device, mesh=mesh, in_specs=in_specs, out_specs=out_specs, check_vma=False)
```

```python
import functools

import jax
import jax.numpy as jnp
import ml_dtypes
import numpy as np
from jax import lax
from jax.experimental import pallas as pl
from jax.experimental.pallas import tpu as pltpu
from jax.sharding import PartitionSpec as P

D = 512
HD = 64
FF = 2048
NR = 16
LEVELS = 6
SLOT = 1024
TILE = 128
TILES = SLOT // TILE
PAIRS = D // 128
HEADS = D // HD
HALF = D // 2
REST = HALF + FF
EPS = 1e-05
NEG = -1e30

BASE = (0, 1056, 1600, 1888, 2048, 2144)
CELL_ROWS = 2176
WIN_ROWS = (160, 96, 64, 32, 32, 16)
WIN_AT = (0, 160, 256, 320, 352, 384)
WIN = 400
COARSE = WIN - 160
LANE_AT = (0, 0, 64, 96, 112, 120)
BF = jnp.bfloat16
F32 = jnp.float32


def window_parts(i):
    two, four = i // 2, i // 4
    return (
        (128 * i, 160),
        (BASE[1] + 64 * i, 96),
        (BASE[2] + 32 * i, 64),
        (BASE[3] + 16 * i, 16),
        (BASE[3] + 16 * i + 32, 16),
        (BASE[4] + 16 * two, 16),
        (BASE[4] + 16 * two + 32, 16),
        (BASE[5] + 16 * (1 - four), 16),
    )


def mask_table():
    table = np.full((TILES, WIN, TILE), NEG, np.float32)
    rows = np.arange(TILE)
    for i in range(TILES):
        at = 0
        for start, count in window_parts(i):
            level = max(l for l in range(LEVELS) if WIN_AT[l] <= at)
            pad = 0 if level == 5 else 16
            cell = (start - BASE[level] - pad + np.arange(count))[:, None]
            query = ((128 * i + rows) >> level)[None, :]
            good = np.abs(cell // 16 - query // 16) <= 1
            if level > 0:
                good &= np.abs((2 * cell) // 16 - (2 * query) // 16) > 1
            table[i, at : at + count] = np.where(good, 0.0, NEG)
            at += count
    return table


def constants():
    t = np.arange(TILE)
    pool_q = np.zeros((TILE, TILE), np.float32)
    pool_s = np.zeros((TILE, TILE), np.float32)
    spread = np.zeros((COARSE, TILE), np.int32)
    level_mask = np.zeros((COARSE, TILE), np.float32)
    pool_k = np.zeros((256, 256), np.float32)
    t2 = np.arange(256)
    at = 0
    for level in range(1, LEVELS):
        width = 2**level
        pool_q[LANE_AT[level] + t // width, t] = 1.0 / width
        pool_s[t, LANE_AT[level] + t // width] = 1.0
        rows = slice(WIN_AT[level] - 160, WIN_AT[level] - 160 + WIN_ROWS[level])
        spread[rows] = LANE_AT[level] + t // width
        level_mask[rows, LANE_AT[level] : LANE_AT[level] + TILE // width] = 1.0
        pool_k[at + t2 // width, t2] = 1.0
        at += 256 // width
    half = ml_dtypes.bfloat16
    return {
        "mask": mask_table(),
        "pool_q": pool_q.astype(half),
        "pool_s": pool_s.astype(half),
        "spread": spread,
        "level_mask": level_mask,
        "pool_k": pool_k.astype(half),
        "spread_k": pool_k.T.copy().astype(half),
    }


def mm(a, b):
    return lax.dot_general(a, b, (((1,), (0,)), ((), ())), preferred_element_type=F32)


def mm_nt(a, b):
    return lax.dot_general(a, b, (((1,), (1,)), ((), ())), preferred_element_type=F32)


def mm_tn(a, b):
    return lax.dot_general(a, b, (((0,), (0,)), ((), ())), preferred_element_type=F32)


def norm_parts(values):
    centre = values - jnp.mean(values, axis=-1, keepdims=True)
    spread = jnp.mean(centre * centre, axis=-1, keepdims=True)
    scale = lax.rsqrt(spread + EPS)
    return centre * scale, scale


def norm_back(grad, xhat, scale, gain):
    e = grad * gain
    return (e - jnp.mean(e, axis=-1, keepdims=True) - xhat * jnp.mean(e * xhat, axis=-1, keepdims=True)) * scale


def joined(ref, first, count):
    parts = [ref[t, r : r + 1, :].astype(F32) for t in range(2) for r in range(first, first + count)]
    return jnp.concatenate(parts, axis=1)


def column_sum(values):
    return jnp.sum(values, axis=0, keepdims=True)


def count_tables(length, bias_ref, inv_ref):
    length = length.astype(F32)
    for level in range(LEVELS):
        width = 2**level
        pad = 0 if level == 5 else 16
        count = SLOT // width + 2 * pad
        cell = lax.broadcasted_iota(jnp.int32, (count, 128), 0) - pad
        live = jnp.where(cell < 0, 0.0, length - (cell * width).astype(F32))
        rows = pl.ds(BASE[level], count)
        if level == 0:
            bias_ref[rows, :] = jnp.where(live > 0.0, 0.0, NEG)
        else:
            some = jnp.clip(live, 1.0, np.float32(width))
            bias_ref[rows, :] = jnp.where(live > 0.0, jnp.log(some), NEG)
            inv_ref[rows, :] = 1.0 / some


SKEW_F = 0
SKEW_B = 0
SKEW_P = 1
SKEW_E = 1
SKEW_M = 1


def interleave(chains, skew):
    live = dict(enumerate(chains))
    turn = 0
    while live:
        for j in sorted(live):
            if turn >= skew * j and next(live[j], live) is live:
                del live[j]
        turn += 1


def window(ref, i, lanes):
    parts = []
    for start, count in window_parts(i):
        parts.append(ref[pl.ds(pl.multiple_of(start, 16), count), lanes])
    return jnp.concatenate(parts, axis=0)


def two_columns(block):
    zero = jnp.zeros((64, block.shape[1]), block.dtype)
    top = jnp.concatenate([block[:64], zero], axis=1)
    low = jnp.concatenate([zero, block[64:]], axis=1)
    return jnp.concatenate([top, low], axis=0)


def two_rows(block):
    first = lax.broadcasted_iota(jnp.int32, block.shape, 1) < 64
    zero = jnp.zeros_like(block)
    return jnp.concatenate([jnp.where(first, block, zero), jnp.where(first, zero, block)], axis=0)


def diagonal(block):
    n = block.shape[1] // 2
    return jnp.concatenate([block[:64, :n], block[64:, n:]], axis=0)


def pair_scores(keys, queries_t, cells_t, spread, bias):
    return finish_scores(mm(keys[:160], two_columns(queries_t)), mm(keys[160:], two_columns(cells_t)), spread, bias)


def finish_scores(fine, rough, spread, bias):
    out = []
    for h in range(2):
        lanes = slice(128 * h, 128 * h + 128)
        wide = jnp.take_along_axis(rough[:, lanes], spread, axis=1)
        out.append(jnp.concatenate([fine[:, lanes], wide], axis=0) + bias)
    return out


def keep_live(full, length, chunk, out_ref):
    row = lax.broadcasted_iota(jnp.int32, full.shape, 0) + 256 * chunk
    live = jnp.where(row < length, full, 0.0).astype(BF)
    out_ref[0, pl.ds(16 + 256 * chunk, 256), :] = live
    return live


def pack_cells(sums, chunk, out_ref, rough_ref, inv_ref):
    at = 0
    for level in range(1, LEVELS):
        count = 256 // 2**level
        pad = 0 if level == 5 else 16
        rows = pl.ds(BASE[level] + pad + count * chunk, count)
        cells = sums[at : at + count] * jnp.concatenate([inv_ref[rows, :]] * PAIRS, axis=1)
        if level == 5:
            rough_ref[pl.ds(8 * chunk, 8), :] = cells
        else:
            out_ref[0, rows, :] = cells.astype(BF)
        at += count


def forward_kernel(
    lens, x_ref, row_ref, w_ref, ends_ref,
    mask_ref, pool_q_ref, spread_ref, pool_k_ref,
    n1_ref, q_ref, k_ref, v_ref, attn_ref, low_ref, lse_ref,
    bias_ref, inv_ref, rough_ref, tile_bias_ref,
):
    length = lens[pl.program_id(0)]
    count_tables(length, bias_ref, inv_ref)
    zeros = jnp.zeros((16, D), BF)
    for level in range(LEVELS - 1):
        cells = SLOT // 2**level
        for ref in (k_ref, v_ref):
            ref[0, pl.ds(BASE[level], 16), :] = zeros
            ref[0, pl.ds(BASE[level] + 16 + cells, 16), :] = zeros
    rough_k, rough_v = rough_ref.at[0], rough_ref.at[1]
    query_shift, value_shift = joined(ends_ref, 0, 2), joined(ends_ref, 2, 2)

    def project(chunk):
        rows = pl.ds(256 * chunk, 256)
        xhat, _ = norm_parts(x_ref[0, rows, :].astype(F32))
        n1 = (xhat * row_ref[0:1] + row_ref[1:2]).astype(BF)
        n1_ref[0, rows, :] = n1
        yield
        joint = [mm(n1, w_ref[t]) for t in range(2)]
        yield
        q, k, v = (jnp.concatenate([j[:, at : at + HALF] for j in joint], axis=1) for at in (0, HALF, 2 * HALF))
        q_ref[0, rows, :] = (q + query_shift).astype(BF) * BF(0.125)
        k = keep_live(k, length, chunk, k_ref)
        v = keep_live(v + value_shift, length, chunk, v_ref)
        yield
        k, v = mm(pool_k_ref[...], k), mm(pool_k_ref[...], v)
        yield
        pack_cells(k, chunk, k_ref, rough_k, inv_ref)
        pack_cells(v, chunk, v_ref, rough_v, inv_ref)
        yield

    interleave([project(chunk) for chunk in range(4)], SKEW_P)
    k_ref[0, pl.ds(BASE[5], 32), :] = rough_k[...].astype(BF)
    v_ref[0, pl.ds(BASE[5], 32), :] = rough_v[...].astype(BF)

    def attend(i, carry):
        rows = pl.ds(pl.multiple_of(128 * i, 128), 128)
        tile_bias_ref[...] = mask_ref[i] + window(bias_ref, i, slice(None))
        q = q_ref[0, rows, :]
        cells = mm(pool_q_ref[...], q).astype(BF)
        lse = {}

        def one_pair(pair):
            lanes = slice(128 * pair, 128 * pair + 128)
            keys = window(k_ref.at[0], i, lanes)
            q_t, cells_t = q[:, lanes].T, cells[:, lanes].T
            yield
            fine = mm(keys[:160], two_columns(q_t))
            rough = mm(keys[160:], two_columns(cells_t))
            yield
            scores = finish_scores(fine, rough, spread_ref[...], tile_bias_ref[...])
            tops = [jnp.max(s, axis=0, keepdims=True) for s in scores]
            yield
            shares, inverse = [], []
            for h, (s, top) in enumerate(zip(scores, tops)):
                p = jnp.exp(s - top)
                total = jnp.sum(p, axis=0, keepdims=True)
                shares.append(p.astype(BF))
                inverse.append(1.0 / total)
                lse[2 * pair + h] = top + jnp.log(total)
            values_t = window(v_ref.at[0], i, lanes).T
            yield
            mixed = mm(values_t, jnp.concatenate(shares, axis=1))
            yield
            mixed = diagonal(mixed * jnp.concatenate(inverse, axis=1))
            mixed = mixed.T
            high = mixed.astype(BF)
            attn_ref[0, rows, lanes] = high
            low_ref[0, rows, lanes] = (mixed - high.astype(F32)).astype(BF)
            yield

        interleave([one_pair(pair) for pair in range(PAIRS)], SKEW_F)
        lse_ref[0, :, rows] = jnp.concatenate([lse[h] for h in range(HEADS)], axis=0)
        return carry

    lax.fori_loop(0, TILES, attend, 0)


def middle_kernel(
    x_ref, attn_ref, cot_ref, w_ref, row_ref, ends_ref,
    out_ref, g1_ref, grad_ref, gvec_ref, gbup_ref,
    gwo_ref, gup_ref, gdown_ref,
):
    step = pl.program_id(0)

    @pl.when(step == 0)
    def _():
        gwo_ref[...] = jnp.zeros_like(gwo_ref)
        gup_ref[...] = jnp.zeros_like(gup_ref)
        gdown_ref[...] = jnp.zeros_like(gdown_ref)
        gvec_ref[...] = jnp.zeros_like(gvec_ref)
        gbup_ref[...] = jnp.zeros_like(gbup_ref)

    attn = attn_ref[...]
    cot = cot_ref[...]
    branch = sum(mm_nt(attn[:, HALF * t : HALF * t + HALF], w_ref[:, t, :, :HALF].reshape(D, HALF)) for t in range(2))
    y1 = x_ref[...].astype(F32) + (branch + row_ref[2:3])
    xhat, scale = norm_parts(y1)
    n2 = (xhat * row_ref[3:4] + row_ref[4:5]).astype(BF)
    up_shift = joined(ends_ref, 4, 8)
    n2_t = n2.T
    cot_t = cot.T
    total = [y1 + row_ref[5:6], jnp.zeros_like(y1)]
    c = np.float32(np.sqrt(2.0 / np.pi))

    def hidden(part):
        cols = slice(512 * part, 512 * part + 512)
        at = HALF + 512 * (part % 2)
        up = w_ref[:, part // 2, :, at : at + 512].reshape(D, 512)
        at += FF // 2
        down_t = w_ref[:, part // 2, :, at : at + 512].reshape(D, 512)
        u = mm(n2, up) + up_shift[:, cols]
        dh = mm(cot, down_t)
        yield
        u2 = u * u
        t = jnp.tanh(u * (c + (c * 0.044715) * u2))
        h = 0.5 + 0.5 * t
        hid = (u * h).astype(BF)
        slope = h + 2.0 * h * (1.0 - h) * u * (c + (3.0 * c * 0.044715) * u2)
        dhp = dh * slope
        dhp_b = dhp.astype(BF)
        gbup_ref[:, cols] += column_sum(dhp)
        yield
        total[0] = total[0] + mm_nt(hid, down_t)
        total[1] = total[1] + mm_nt(dhp_b, up)
        gdown_ref[:, cols] += mm(cot_t, hid)
        gup_ref[:, cols] += mm(n2_t, dhp_b)
        yield

    interleave([hidden(part) for part in range(4)], SKEW_M)
    out, dn2 = total
    out_ref[...] = out.astype(BF)
    cot_f = cot.astype(F32)
    dy1 = cot_f + norm_back(dn2, xhat, scale, row_ref[3:4])
    g1 = dy1.astype(BF)
    g1_ref[...] = g1
    gwo_ref[...] += mm(g1.T, attn)
    gvec_ref[...] += jnp.concatenate(
        [column_sum(g1.astype(F32)), column_sum(dn2 * xhat), column_sum(dn2), column_sum(cot_f), jnp.zeros((4, D), F32)],
        axis=0,
    )


    @pl.when(step == pl.num_programs(0) - 1)
    def _():
        rows = D // grad_ref.shape[0]
        for t in range(2):
            at = 0
            for ref, width in ((gwo_ref, HALF), (gup_ref, FF // 2), (gdown_ref, FF // 2)):
                part = ref[:, width * t : width * t + width].astype(BF)
                grad_ref[:, t, :, at : at + width] = part.reshape(grad_ref.shape[0], rows, width)
                at += width


def backward_kernel(
    lens, x_ref, n1_ref, q_ref, k_ref, v_ref, attn_ref, low_ref, lse_ref, g1_ref,
    row_ref, w_ref, wo_t_ref,
    mask_ref, pool_q_ref, pool_s_ref, spread_ref, level_mask_ref, spread_k_ref,
    dx_ref, gqkv_ref, gvec_ref,
    bias_ref, inv_ref, tile_bias_ref, dk_ref, dv_ref, dqkv_ref,
):
    step = pl.program_id(0)

    @pl.when(step == 0)
    def _():
        gqkv_ref[...] = jnp.zeros_like(gqkv_ref)
        gvec_ref[...] = jnp.zeros_like(gvec_ref)

    length = lens[step]
    count_tables(length, bias_ref, inv_ref)
    dk_ref[...] = jnp.zeros_like(dk_ref)
    dv_ref[...] = jnp.zeros_like(dv_ref)
    head_of = lax.broadcasted_iota(jnp.int32, (HEADS, D), 1) // HD
    heads = (head_of == lax.broadcasted_iota(jnp.int32, (HEADS, D), 0)).astype(BF)

    def attend(i, carry):
        rows = pl.ds(pl.multiple_of(128 * i, 128), 128)
        tile_bias_ref[...] = mask_ref[i] + window(bias_ref, i, slice(None))
        q = q_ref[0, rows, :]
        cells = mm(pool_q_ref[...], q).astype(BF)
        da = jnp.concatenate([mm(g1_ref[0, rows, :], wo_t_ref[:, t, :, :HALF].reshape(D, HALF)) for t in range(2)], axis=1)
        da = da.astype(BF)
        product = da.astype(F32) * (attn_ref[0, rows, :].astype(F32) + low_ref[0, rows, :].astype(F32))
        high = product.astype(BF)
        delta = mm_nt(heads, high) + mm_nt(heads, (product - high.astype(F32)).astype(BF))
        lse = lse_ref[0, :, rows]

        def one_pair(pair):
            lanes = slice(128 * pair, 128 * pair + 128)
            keys = window(k_ref.at[0], i, lanes)
            values = window(v_ref.at[0], i, lanes)
            q_t, cells_t, da_t = q[:, lanes].T, cells[:, lanes].T, da[:, lanes].T
            yield
            fine = mm(keys[:160], two_columns(q_t))
            rough = mm(keys[160:], two_columns(cells_t))
            dp = mm(values, two_columns(da_t))
            yield
            scores = finish_scores(fine, rough, spread_ref[...], tile_bias_ref[...])
            shares, slopes = [], []
            for h in range(2):
                head = 2 * pair + h
                p = jnp.exp(scores[h] - lse[head : head + 1])
                slopes.append((p * (dp[:, 128 * h : 128 * h + 128] - delta[head : head + 1])).astype(BF))
                shares.append(p.astype(BF))
            keys_t = keys.T
            yield
            fine = jnp.concatenate([ds[:160] for ds in slopes], axis=1)
            rough = [mm(ds[160:], pool_s_ref[...]) for ds in slopes]
            yield
            rough = jnp.concatenate([(r * level_mask_ref[...]).astype(BF) for r in rough], axis=1)
            dv = mm(jnp.concatenate(shares, axis=1), two_rows(da[:, lanes]))
            yield
            dq_cells = diagonal(mm(keys_t[:, 160:], rough)).astype(BF)
            dq = diagonal(mm(keys_t[:, :160], fine))
            dk = jnp.concatenate([mm(fine, two_rows(q[:, lanes])), mm(rough, two_rows(cells[:, lanes]))], axis=0)
            yield
            dq = (dq + mm(dq_cells, pool_q_ref[...])) * 0.125
            at = 0
            for start, count in window_parts(i):
                part = pl.ds(pl.multiple_of(start, 16), count)
                dk_ref[part, lanes] += dk[at : at + count]
                dv_ref[part, lanes] += dv[at : at + count]
                at += count
            yield
            at = 3 * HALF * (pair // 2) + 128 * (pair % 2)
            dqkv_ref[rows, at : at + 128] = dq.T.astype(BF)
            yield

        interleave([one_pair(pair) for pair in range(PAIRS)], SKEW_B)
        return carry

    lax.fori_loop(0, TILES, attend, 0)

    sums = []

    def finish(chunk):
        rows = pl.ds(256 * chunk, 256)
        own = pl.ds(16 + 256 * chunk, 256)
        live = lax.broadcasted_iota(jnp.int32, (256, D), 0) + 256 * chunk < length
        wide = []
        for ref in (dk_ref, dv_ref):
            cells = []
            for level in range(1, LEVELS):
                count = 256 // 2**level
                pad = 0 if level == 5 else 16
                part = pl.ds(BASE[level] + pad + count * chunk, count)
                cells.append(ref[part, :] * jnp.concatenate([inv_ref[part, :]] * PAIRS, axis=1))
            cells.append(jnp.zeros((8, D), F32))
            wide.append(jnp.concatenate(cells, axis=0).astype(BF))
        yield
        wide = [mm(spread_k_ref[...], w) for w in wide]
        yield
        for ref, at, w in zip((dk_ref, dv_ref), (HALF, 2 * HALF), wide):
            grad = jnp.where(live, ref[own, :] + w, 0.0).astype(BF)
            dqkv_ref[rows, at : at + HALF] = grad[:, :HALF]
            dqkv_ref[rows, at + 3 * HALF : at + 4 * HALF] = grad[:, HALF:]
        yield
        parts = [dqkv_ref[rows, 3 * HALF * t : 3 * HALF * t + 3 * HALF] for t in range(2)]
        dn1 = mm_nt(parts[0], w_ref[0]) + mm_nt(parts[1], w_ref[1])
        xhat, scale = norm_parts(x_ref[0, rows, :].astype(F32))
        yield
        dx = g1_ref[0, rows, :].astype(F32) + norm_back(dn1, xhat, scale, row_ref[0:1])
        dx_ref[0, rows, :] = dx.astype(BF)
        col = [column_sum(part.astype(F32)) for part in parts]
        sums.append(
            jnp.concatenate(
                [
                    column_sum(dn1 * xhat), column_sum(dn1),
                    jnp.concatenate([c[:, :HALF] for c in col], axis=1),
                    jnp.concatenate([c[:, 2 * HALF :] for c in col], axis=1),
                    jnp.zeros((4, D), F32),
                ],
                axis=0,
            )
        )
        yield

    interleave([finish(chunk) for chunk in range(4)], SKEW_E)
    gvec_ref[...] += sums[0] + sums[1] + sums[2] + sums[3]
    n1_t = n1_ref[0].T
    for t in range(2):
        gqkv_ref[t] += mm(n1_t, dqkv_ref[:, 3 * HALF * t : 3 * HALF * t + 3 * HALF])


def whole(shape):
    return pl.BlockSpec(shape, lambda *_: (0,) * len(shape))


def per_sequence(*shape):
    return pl.BlockSpec((1,) + shape, lambda s, *_: (s,) + (0,) * len(shape))


LIMIT = 60 * 1024 * 1024


def attention_forward(x, lens, row, w, ends, const):
    count = x.shape[0]
    return pl.pallas_call(
        forward_kernel,
        grid_spec=pltpu.PrefetchScalarGridSpec(
            num_scalar_prefetch=1,
            grid=(count,),
            in_specs=[
                per_sequence(SLOT, D), whole((8, D)), whole((2, D, 3 * HALF)), whole((2, 16, 128)),
                whole((TILES, WIN, TILE)), whole((TILE, TILE)), whole((COARSE, TILE)), whole((256, 256)),
            ],
            out_specs=[
                per_sequence(SLOT, D), per_sequence(SLOT, D), per_sequence(CELL_ROWS, D), per_sequence(CELL_ROWS, D),
                per_sequence(SLOT, D), per_sequence(SLOT, D), per_sequence(HEADS, SLOT),
            ],
            scratch_shapes=[
                pltpu.VMEM((CELL_ROWS, 128), F32), pltpu.VMEM((CELL_ROWS, 128), F32), pltpu.VMEM((2, 32, D), F32),
                pltpu.VMEM((WIN, TILE), F32),
            ],
        ),
        out_shape=[
            jax.ShapeDtypeStruct((count, SLOT, D), BF), jax.ShapeDtypeStruct((count, SLOT, D), BF),
            jax.ShapeDtypeStruct((count, CELL_ROWS, D), BF), jax.ShapeDtypeStruct((count, CELL_ROWS, D), BF),
            jax.ShapeDtypeStruct((count, SLOT, D), BF), jax.ShapeDtypeStruct((count, SLOT, D), BF),
            jax.ShapeDtypeStruct((count, HEADS, SLOT), F32),
        ],
        compiler_params=pltpu.CompilerParams(vmem_limit_bytes=LIMIT),
        cost_estimate=pl.CostEstimate(flops=count * 30 * 10**9, bytes_accessed=count * 10**7, transcendentals=0),
        name="attention_forward",
    )(lens, x, row, w, ends, const["mask"], const["pool_q"], const["spread"], const["pool_k"])


ROWS = 512


def middle(x, attn, cot, w, row, ends):
    total = x.shape[0]
    rows = pl.BlockSpec((ROWS, D), lambda s: (s, 0))
    return pl.pallas_call(
        middle_kernel,
        grid=(total // ROWS,),
        in_specs=[
            rows, rows, rows, whole(w.shape), whole((8, D)), whole((2, 16, 128)),
        ],
        out_specs=[rows, rows, whole(w.shape), whole((8, D)), whole((1, FF))],
        scratch_shapes=[pltpu.VMEM((D, D), F32), pltpu.VMEM((D, FF), F32), pltpu.VMEM((D, FF), F32)],
        out_shape=[
            jax.ShapeDtypeStruct((total, D), BF), jax.ShapeDtypeStruct((total, D), BF), jax.ShapeDtypeStruct(w.shape, BF),
            jax.ShapeDtypeStruct((8, D), F32), jax.ShapeDtypeStruct((1, FF), F32),
        ],
        compiler_params=pltpu.CompilerParams(vmem_limit_bytes=LIMIT),
        name="middle",
    )(x, attn, cot, w, row, ends)


def attention_backward(x, lens, n1, q, k, v, attn, low, lse, g1, row, w, rest, const):
    count = x.shape[0]
    wo_t = pl.BlockSpec(rest.shape[:3] + (HALF,), lambda *_: (0, 0, 0, 0))
    return pl.pallas_call(
        backward_kernel,
        grid_spec=pltpu.PrefetchScalarGridSpec(
            num_scalar_prefetch=1,
            grid=(count,),
            in_specs=[
                per_sequence(SLOT, D), per_sequence(SLOT, D), per_sequence(SLOT, D),
                per_sequence(CELL_ROWS, D), per_sequence(CELL_ROWS, D), per_sequence(SLOT, D), per_sequence(SLOT, D),
                per_sequence(HEADS, SLOT), per_sequence(SLOT, D),
                whole((8, D)), whole((2, D, 3 * HALF)), wo_t,
                whole((TILES, WIN, TILE)), whole((TILE, TILE)), whole((TILE, TILE)), whole((COARSE, TILE)),
                whole((COARSE, TILE)), whole((256, 256)),
            ],
            out_specs=[per_sequence(SLOT, D), whole((2, D, 3 * HALF)), whole((8, D))],
            scratch_shapes=[
                pltpu.VMEM((CELL_ROWS, 128), F32), pltpu.VMEM((CELL_ROWS, 128), F32), pltpu.VMEM((WIN, TILE), F32),
                pltpu.VMEM((CELL_ROWS, D), F32), pltpu.VMEM((CELL_ROWS, D), F32), pltpu.VMEM((SLOT, 3 * D), BF),
            ],
        ),
        out_shape=[
            jax.ShapeDtypeStruct((count, SLOT, D), BF), jax.ShapeDtypeStruct((2, D, 3 * HALF), F32),
            jax.ShapeDtypeStruct((8, D), F32),
        ],
        compiler_params=pltpu.CompilerParams(vmem_limit_bytes=LIMIT),
        cost_estimate=pl.CostEstimate(flops=count * 40 * 10**9, bytes_accessed=count * 10**7, transcendentals=0),
        name="attention_backward",
    )(
        lens, x, n1, q, k, v, attn, low, lse, g1, row, w, rest,
        const["mask"], const["pool_q"], const["pool_s"], const["spread"], const["level_mask"], const["spread_k"],
    )


def bits_of(count):
    return count.bit_length() - 1


def all_bits(n_dp, n_t):
    return [("tensor", b) for b in reversed(range(bits_of(n_t)))] + [("dp", b) for b in reversed(range(bits_of(n_dp)))]


def gather_orders(n_dp, n_t):
    far = [("dp", b) for b in reversed(range(2, bits_of(n_dp)))]
    near = [("dp", 1)]
    side = [("tensor", b) for b in reversed(range(bits_of(n_t)))]
    core_bit = [("dp", 0)]
    return far + near + side + core_bit, far + side + near + core_bit


def own_bit(bit):
    axis, b = bit
    return (lax.axis_index(axis) // 2**b) % 2


def partner(bit):
    axis, b = bit
    return {axis: lax.axis_index(axis) + (1 - 2 * own_bit(bit)) * 2**b}


def meet(bits):
    barrier = pltpu.get_barrier_semaphore()
    for bit in bits:
        pl.semaphore_signal(barrier, inc=1, device_id=partner(bit), device_id_type=pl.DeviceIdType.MESH)
    pl.semaphore_wait(barrier, len(bits))


def halves(width):
    if width % 256:
        return [(0, width)]
    return [(0, width // 2), (width // 2, width // 2)]


def gather_kernel(
    bits, orders, parts, shard_ref, ends_ref, out_ref, all_ends_ref, own_sem, send_sems, recv_sems, ends_own_sem, ends_sems
):
    own = pltpu.make_async_copy(shard_ref, out_ref.at[tuple(own_bit(bit) for bit in bits)], own_sem)
    own.start()
    side = [bit for bit in bits if bit[0] == "tensor"]
    own_ends = pltpu.make_async_copy(ends_ref, all_ends_ref.at[tuple(own_bit(bit) for bit in side)], ends_own_sem)
    own_ends.start()
    meet(bits)
    pending = []
    own_ends.wait()

    def ends_copy(step):
        place = all_ends_ref.at[tuple(slice(None) if j < step else own_bit(bit) for j, bit in enumerate(side))]
        return pltpu.make_async_remote_copy(
            src_ref=place, dst_ref=place, send_sem=ends_sems.at[0, step], recv_sem=ends_sems.at[1, step],
            device_id=partner(side[step]), device_id_type=pl.DeviceIdType.MESH,
        )

    if side:
        ends_copy(0).start()
    for step in range(len(bits)):
        for part, (at, width) in enumerate(parts):
            order = orders[part]
            done = order[:step]
            index = tuple(slice(None) if bit in done else own_bit(bit) for bit in bits)
            place = out_ref.at[index + (slice(None), pl.ds(at, width))]
            source = shard_ref.at[:, pl.ds(at, width)] if step == 0 else place
            if step > 0:
                pending[(step - 1) * len(parts) + part].wait_recv()
            copy = pltpu.make_async_remote_copy(
                src_ref=source, dst_ref=place,
                send_sem=send_sems.at[step, part], recv_sem=recv_sems.at[step, part],
                device_id=partner(order[step]), device_id_type=pl.DeviceIdType.MESH,
            )
            if step == 1 and part == 0:
                own.wait()
            copy.start()
            pending.append(copy)
    for copy in pending[-len(parts) :]:
        copy.wait_recv()
    for step in range(len(side)):
        ends_copy(step).wait_recv()
        if step + 1 < len(side):
            ends_copy(step + 1).start()
    for step in range(len(side)):
        ends_copy(step).wait_send()
    for copy in pending:
        copy.wait_send()


def gather(shard, ends, n_dp, n_t):
    rows, width = shard.shape
    bits, orders, parts = all_bits(n_dp, n_t), gather_orders(n_dp, n_t), halves(width)
    side = bits_of(n_t)
    anywhere = pl.BlockSpec(memory_space=pl.ANY)
    out, all_ends = pl.pallas_call(
        functools.partial(gather_kernel, bits, orders, parts),
        in_specs=[anywhere, anywhere],
        out_specs=[anywhere, anywhere],
        out_shape=[
            jax.ShapeDtypeStruct((2,) * len(bits) + (rows, width), shard.dtype),
            jax.ShapeDtypeStruct((2,) * side + ends.shape, ends.dtype),
        ],
        scratch_shapes=[
            pltpu.SemaphoreType.DMA, pltpu.SemaphoreType.DMA((len(bits), len(parts))),
            pltpu.SemaphoreType.DMA((len(bits), len(parts))), pltpu.SemaphoreType.DMA,
            pltpu.SemaphoreType.DMA((2, max(side, 1))),
        ],
        compiler_params=pltpu.CompilerParams(collective_id=0, has_side_effects=True),
        name="gather",
    )(shard, ends)
    return out.reshape(n_t, n_dp, rows, width), all_ends.reshape((n_t,) + ends.shape)


def reduce_kernel(bits, orders, parts, rows, grad_ref, vec_ref, out_ref, vec_out_ref, *scratch):
    steps, count = len(bits), len(parts)
    sends, recvs, sums = (scratch[j * steps * count : (j + 1) * steps * count] for j in range(3))
    vec_recv, send_sems, recv_sems, vec_send_sems, vec_recv_sems = scratch[3 * steps * count :]
    meet(bits)
    vec_out_ref[...] = vec_ref[...]

    def vec_copy(step):
        return pltpu.make_async_remote_copy(
            src_ref=vec_recv.at[2 * step], dst_ref=vec_recv.at[2 * step + 1],
            send_sem=vec_send_sems.at[step], recv_sem=vec_recv_sems.at[step],
            device_id=partner(orders[0][steps - 1 - step]), device_id_type=pl.DeviceIdType.MESH,
        )

    def copy_of(step, part):
        j = step * count + part
        return pltpu.make_async_remote_copy(
            src_ref=sends[j], dst_ref=recvs[j], send_sem=send_sems.at[step, part], recv_sem=recv_sems.at[step, part],
            device_id=partner(orders[part][steps - 1 - step]), device_id_type=pl.DeviceIdType.MESH,
        )

    def pieces(step, part):
        order = orders[part][::-1]
        left = [bit for bit in bits if bit not in order[:step]]
        j = left.index(order[step])
        low = 2 ** (len(left) - 1 - j)
        mine = own_bit(order[step])
        out = []
        for a in range(2**j):
            for c in range(low):
                out.append(((a * 2 + 1 - mine) * low + c, (a * 2 + mine) * low + c, a * low + c))
        at, width = parts[part]
        source = sums[(step - 1) * count + part] if step else grad_ref.at[:, :, pl.ds(at, width)]
        return out, source

    for step in range(steps):
        vec_recv[2 * step] = vec_out_ref[...]
        vec_copy(step).start()
        for part in range(count):
            blocks, source = pieces(step, part)
            for away, _, to in blocks:
                sends[step * count + part][to] = source[away].astype(BF)
            copy_of(step, part).start()
        for part in range(count):
            copy_of(step, part).wait_recv()
            blocks, source = pieces(step, part)
            for _, keep, to in blocks:
                total = source[keep] + recvs[step * count + part][to].astype(F32)
                if step == steps - 1:
                    at, width = parts[part]
                    out_ref[:, at : at + width] = total
                else:
                    sums[step * count + part][to] = total
        vec_copy(step).wait_recv()
        vec_out_ref[...] += vec_recv[2 * step + 1]
    for step in range(steps):
        vec_copy(step).wait_send()
        for part in range(count):
            copy_of(step, part).wait_send()


def reduce(grad, vec, n_dp, n_t):
    rows, width = grad.shape[2:]
    bits, orders, parts = all_bits(n_dp, n_t), gather_orders(n_dp, n_t), halves(width)
    steps = len(bits)
    blocks = [(2 ** (steps - 1 - step), rows, w) for step in range(steps) for _, w in parts]
    sems = pltpu.SemaphoreType.DMA
    vmem = pl.BlockSpec(memory_space=pltpu.VMEM)
    return pl.pallas_call(
        functools.partial(reduce_kernel, bits, orders, parts, rows),
        in_specs=[vmem, vmem],
        out_specs=[vmem, vmem],
        out_shape=[jax.ShapeDtypeStruct((rows, width), F32), jax.ShapeDtypeStruct(vec.shape, F32)],
        scratch_shapes=[pltpu.VMEM(b, BF) for b in blocks] * 2
        + [pltpu.VMEM(b, F32) for b in blocks]
        + [
            pltpu.VMEM((2 * steps,) + vec.shape, F32), sems((steps, len(parts))), sems((steps, len(parts))),
            sems((steps,)), sems((steps,)),
        ],
        compiler_params=pltpu.CompilerParams(collective_id=1, has_side_effects=True, vmem_limit_bytes=LIMIT),
        name="reduce",
    )(grad.reshape(n_t * n_dp, rows, width), vec)


def to_pairs(grid, widths):
    n_t, n_dp, rows, _ = grid.shape
    grid = grid.reshape(n_t, n_dp * rows, -1)
    if n_t == 2:
        return grid
    out, at = [], 0
    for width in widths:
        part = grid[:, :, at : at + width].reshape(2, n_t // 2, D, width)
        out.append(part.transpose(0, 2, 1, 3).reshape(2, D, n_t // 2 * width))
        at += width
    return jnp.concatenate(out, axis=2)


def from_pairs(grid, widths, n_dp, n_t):
    if n_t != 2:
        out, at = [], 0
        for width in widths:
            full = width * n_t // 2
            part = grid[:, :, at : at + full].reshape(2, D, n_t // 2, width)
            out.append(part.transpose(0, 2, 1, 3).reshape(n_t, D, width))
            at += full
        grid = jnp.concatenate(out, axis=2)
    return grid.reshape(n_t, n_dp, D // n_dp, -1)


def own_sequences(values, lengths, tensor_count):
    micro, rows, width = values[0].shape
    t = lax.axis_index("tensor")
    if rows % SLOT == 0:
        per = rows // SLOT
        own = lax.dynamic_slice_in_dim(lengths, t * per, per, 1).reshape(-1)
        return [v.reshape(micro * per, SLOT, width) for v in values], own
    pieces = SLOT // rows
    assert micro == pieces
    groups = [[g * pieces + j for j in range(pieces)] for g in range(tensor_count // pieces)]
    out = [lax.all_to_all(v, "tensor", 0, 1, axis_index_groups=groups, tiled=True) for v in values]
    sequence = lax.dynamic_slice(lengths, (t % pieces, t // pieces), (1, 1))
    return out, sequence.reshape(-1)


def own_rows(values, shape, tensor_count):
    micro, rows, width = shape
    if rows % SLOT == 0:
        return [v.reshape(shape) for v in values]
    pieces = SLOT // rows
    groups = [[g * pieces + j for j in range(pieces)] for g in range(tensor_count // pieces)]
    return [
        lax.all_to_all(v, "tensor", 1, 0, axis_index_groups=groups, tiled=True).reshape(shape) for v in values
    ]


def core(x, lens, cot, row, w, ends, rest):
    const = {name: jnp.asarray(value) for name, value in constants().items()}
    count = x.shape[0]
    flat = (count * SLOT, D)
    n1, q, k, v, attn, low, lse = attention_forward(x, lens, row, w, ends, const)
    out, g1, grad_rest, mid_vec, gbup = middle(
        x.reshape(flat), attn.reshape(flat), cot.reshape(flat), rest, row, ends
    )
    dx, gqkv, pre_vec = attention_backward(
        x, lens, n1, q, k, v, attn, low, lse, g1.reshape(count, SLOT, D), row, w, rest, const
    )
    return out, dx, grad_rest, mid_vec, gbup, gqkv, pre_vec


def on_device(
    inputs, lengths, pre_gain, pre_shift, query_weight, key_weight, value_weight, query_bias, value_bias,
    output_weight, output_bias, mid_gain, mid_shift, up_weight, up_bias, down_weight, down_bias, cotangent,
):
    n_dp, n_t = lax.axis_size("dp"), lax.axis_size("tensor")
    t = lax.axis_index("tensor")
    (x, cot), lens = own_sequences([inputs, cotangent], lengths, n_t)

    n_q, n_f = query_weight.shape[1], up_weight.shape[1]
    vectors = (pre_gain, pre_shift, output_bias, mid_gain, mid_shift, down_bias, down_bias, down_bias)
    row = jnp.stack(vectors).astype(F32)
    first = jnp.concatenate([query_weight, key_weight, value_weight], axis=1)
    second = jnp.concatenate([output_weight.T, up_weight, down_weight.T], axis=1)
    ends = jnp.concatenate([query_bias, value_bias, up_bias])
    ends = jnp.pad(ends, (0, 2048 - ends.shape[0])).reshape(16, 128)
    w, ends = gather(first, ends, n_dp, n_t)
    w = to_pairs(w, (n_q,) * 3)
    rest = lax.all_gather(second, ("dp", "tensor"), axis=0, tiled=False)
    rest = rest.reshape(n_dp, n_t, D // n_dp, -1)
    if n_t != 2:
        rest = to_pairs(rest.transpose(1, 0, 2, 3), (n_q, n_f, n_f)).reshape(2, 16, 32, REST).transpose(1, 0, 2, 3)
        flat = ends.reshape(n_t, -1)
        parts = [flat[:, a : a + n].reshape(2, -1) for a, n in ((0, n_q), (n_q, n_q), (2 * n_q, n_f))]
        ends = jnp.concatenate(parts + [jnp.zeros((2, 512), ends.dtype)], axis=1).reshape(2, 16, 128)
    out, dx, grad_rest, mid_vec, gbup, gqkv, pre_vec = core(x, lens, cot, row, w, ends, rest)
    if n_t != 2:
        grad_rest = grad_rest.transpose(1, 0, 2, 3).reshape(2, D, REST)
        grad_rest = from_pairs(grad_rest, (n_q, n_f, n_f), n_dp, n_t).transpose(1, 0, 2, 3)
    grad_rest = grad_rest.reshape(n_dp * n_t, D // n_dp, -1)
    grad_rest = lax.psum_scatter(grad_rest, ("dp", "tensor"), scatter_dimension=0, tiled=False).astype(F32)
    vec = jnp.concatenate([pre_vec[:4], mid_vec[:4], gbup.reshape(4, D), jnp.zeros((4, D), F32)], axis=0)
    grad_first, vec = reduce(from_pairs(gqkv, (n_q,) * 3, n_dp, n_t), vec, n_dp, n_t)
    grad_q, grad_k, grad_v = (grad_first[:, n_q * j : n_q * j + n_q] for j in range(3))
    grad_o, grad_up, grad_down = grad_rest[:, :n_q].T, grad_rest[:, n_q : n_q + n_f], grad_rest[:, n_q + n_f :].T

    def mine(v):
        n = v.shape[0] // n_t
        return lax.dynamic_slice_in_dim(v, t * n, n, 0)

    out, dx = own_rows([out.reshape(x.shape), dx], inputs.shape, n_t)
    return (
        out, dx, vec[0], vec[1], grad_q, grad_k, grad_v, mine(vec[2]), mine(vec[3]), grad_o, vec[4], vec[5], vec[6],
        grad_up, mine(vec[8:12].reshape(-1)), grad_down, vec[7],
    )


def solution(mesh):
    rows = P(None, ("dp", "tensor"), None)
    by_row, by_column = P("dp", "tensor"), P("tensor", "dp")
    in_specs = (
        rows, P(None, "dp"), P(), P(), by_row, by_row, by_row, P("tensor"), P("tensor"), by_column, P(), P(), P(),
        by_row, P("tensor"), by_column, P(), rows,
    )
    out_specs = (
        rows, rows, P(), P(), by_row, by_row, by_row, P("tensor"), P("tensor"), by_column, P(), P(), P(),
        by_row, P("tensor"), by_column, P(),
    )
    return jax.shard_map(on_device, mesh=mesh, in_specs=in_specs, out_specs=out_specs, check_vma=False)
```

```python
import functools

import jax
import jax.numpy as jnp
import ml_dtypes
import numpy as np
from jax import lax
from jax.experimental import pallas as pl
from jax.experimental.pallas import tpu as pltpu
from jax.sharding import PartitionSpec as P

D = 512
HD = 64
FF = 2048
NR = 16
LEVELS = 6
SLOT = 1024
TILE = 128
TILES = SLOT // TILE
PAIRS = D // 128
HEADS = D // HD
HALF = D // 2
REST = HALF + FF
EPS = 1e-05
NEG = -1e30

BASE = (0, 1056, 1600, 1888, 2048, 2144)
CELL_ROWS = 2176
WIN_ROWS = (160, 96, 64, 32, 32, 16)
WIN_AT = (0, 160, 256, 320, 352, 384)
WIN = 400
COARSE = WIN - 160
LANE_AT = (0, 0, 0, 32, 48, 56)
SPLIT = WIN_AT[2]
BF = jnp.bfloat16
F32 = jnp.float32


def window_parts(i):
    two, four = i // 2, i // 4
    return (
        (128 * i, 160),
        (BASE[1] + 64 * i, 96),
        (BASE[2] + 32 * i, 64),
        (BASE[3] + 16 * i, 16),
        (BASE[3] + 16 * i + 32, 16),
        (BASE[4] + 16 * two, 16),
        (BASE[4] + 16 * two + 32, 16),
        (BASE[5] + 16 * (1 - four), 16),
    )


def mask_table():
    table = np.full((TILES, WIN, TILE), NEG, np.float32)
    for i in range(TILES):
        at = 0
        for start, count in window_parts(i):
            level = max(l for l in range(LEVELS) if WIN_AT[l] <= at)
            pad = 0 if level == 5 else 16
            cell = (start - BASE[level] - pad + np.arange(count))[:, None]
            here = TILE >> level
            query = (((128 * i) >> level) + np.arange(here))[None, :]
            good = np.abs(cell // 16 - query // 16) <= 1
            if level > 0:
                good &= np.abs((2 * cell) // 16 - (2 * query) // 16) > 1
            for head in range(1 if level == 0 else 2):
                lane = 64 * head + LANE_AT[level]
                table[i, at : at + count, lane : lane + here] = np.where(good, 0.0, NEG)
            at += count
    return table


def constants():
    t = np.arange(TILE)
    pool_q = np.zeros((TILE, TILE), np.float32)
    stat = np.zeros((2, 8, TILE), np.int32)
    expand = np.zeros((256, 256), np.float32)
    pool_k = np.zeros((256, 256), np.float32)
    t2 = np.arange(256)
    at = 0
    for level in range(1, LEVELS):
        width = 2**level
        half = 0 if level == 1 else 64
        pool_q[half + LANE_AT[level] + t // width, t] = 1.0 / width
        for head in range(2):
            stat[head, level - 1 :] = 64 * head + LANE_AT[level] + t // width
            expand[2 * half + 64 * head + LANE_AT[level] + t // width, 128 * head + t] = 1.0 / width
        pool_k[at + t2 // width, t2] = 1.0
        at += 256 // width
    half = ml_dtypes.bfloat16
    return {
        "mask": mask_table(),
        "pool_q": pool_q.astype(half),
        "stat": stat,
        "cell_rows": (pool_q > 0).astype(np.float32),
        "expand": expand.astype(half),
        "pool_k": pool_k.astype(half),
        "spread_k": pool_k.T.copy().astype(half),
    }


def mm(a, b):
    return lax.dot_general(a, b, (((1,), (0,)), ((), ())), preferred_element_type=F32)


def mm_nt(a, b):
    return lax.dot_general(a, b, (((1,), (1,)), ((), ())), preferred_element_type=F32)


def mm_tn(a, b):
    return lax.dot_general(a, b, (((0,), (0,)), ((), ())), preferred_element_type=F32)


def norm_parts(values):
    centre = values - jnp.mean(values, axis=-1, keepdims=True)
    spread = jnp.mean(centre * centre, axis=-1, keepdims=True)
    scale = lax.rsqrt(spread + EPS)
    return centre * scale, scale


def norm_back(grad, xhat, scale, gain):
    e = grad * gain
    return (e - jnp.mean(e, axis=-1, keepdims=True) - xhat * jnp.mean(e * xhat, axis=-1, keepdims=True)) * scale


def joined(ref, first, count):
    parts = [ref[t, r : r + 1, :].astype(F32) for t in range(2) for r in range(first, first + count)]
    return jnp.concatenate(parts, axis=1)


def column_sum(values):
    return jnp.sum(values, axis=0, keepdims=True)


def count_tables(length, bias_ref, inv_ref):
    length = length.astype(F32)
    for level in range(LEVELS):
        width = 2**level
        pad = 0 if level == 5 else 16
        count = SLOT // width + 2 * pad
        cell = lax.broadcasted_iota(jnp.int32, (count, 128), 0) - pad
        live = jnp.where(cell < 0, 0.0, length - (cell * width).astype(F32))
        rows = pl.ds(BASE[level], count)
        if level == 0:
            bias_ref[rows, :] = jnp.where(live > 0.0, 0.0, NEG)
        else:
            some = jnp.clip(live, 1.0, np.float32(width))
            bias_ref[rows, :] = jnp.where(live > 0.0, jnp.log(some), NEG)
            inv_ref[rows, :] = 1.0 / some


SKEW_F = 1
SKEW_B = 0
SKEW_P = 1
SKEW_E = 1
SKEW_M = 1


def interleave(chains, skew):
    live = dict(enumerate(chains))
    turn = 0
    while live:
        for j in sorted(live):
            if turn >= skew * j and next(live[j], live) is live:
                del live[j]
        turn += 1


def runs(touched, start, count):
    out = []
    for begin in range(start, start + count, 16):
        seen = begin in touched
        touched.add(begin)
        if out and out[-1][0] == seen:
            out[-1][2] += 16
        else:
            out.append([seen, begin, 16])
    return out


def window(ref, i, lanes):
    parts = []
    for start, count in window_parts(i):
        parts.append(ref[pl.ds(start, count), lanes])
    return jnp.concatenate(parts, axis=0)


def two_rows(block):
    first = lax.broadcasted_iota(jnp.int32, block.shape, 1) < 64
    zero = jnp.zeros_like(block)
    return jnp.concatenate([jnp.where(first, block, zero), jnp.where(first, zero, block)], axis=0)


def diagonal(block):
    n = block.shape[1] // 2
    return jnp.concatenate([block[:64, :n], block[64:, n:]], axis=0)


def four_rows(block):
    head = lax.broadcasted_iota(jnp.int32, block.shape, 1) // 64
    zero = jnp.zeros_like(block)
    return jnp.concatenate([jnp.where(head == j, block, zero) for j in range(4)], axis=0)


def corners(first, second):
    top = jnp.concatenate([first, jnp.zeros((first.shape[0], second.shape[1]), first.dtype)], axis=1)
    low = jnp.concatenate([jnp.zeros((second.shape[0], first.shape[1]), first.dtype), second], axis=1)
    return jnp.concatenate([top, low], axis=0)


def to_rows(level_one, others, index):
    row = lax.broadcasted_iota(jnp.int32, (8, TILE), 0)
    both = jnp.where(row == 0, jnp.broadcast_to(level_one, (8, TILE)), jnp.broadcast_to(others, (8, TILE)))
    return jnp.take_along_axis(both, index, axis=1)


def row_weights(weights, cell_rows):
    ones, rest = [], []
    for w in weights:
        wide = [jnp.broadcast_to(w[l : l + 1], (n, TILE)) for l, n in ((0, 64), (1, 32), (2, 16), (3, 8), (4, 8))]
        full = (jnp.concatenate(wide, axis=0) * cell_rows).astype(BF)
        ones.append(full[:64])
        rest.append(full[64:])
    return jnp.concatenate([corners(*ones), corners(*rest)], axis=0)


def keep_live(full, length, chunk, out_ref):
    row = lax.broadcasted_iota(jnp.int32, full.shape, 0) + 256 * chunk
    live = jnp.where(row < length, full, 0.0).astype(BF)
    out_ref[0, pl.ds(16 + 256 * chunk, 256), :] = live
    return live


def pack_cells(sums, chunk, out_ref, rough_ref, inv_ref):
    at = 0
    for level in range(1, LEVELS):
        count = 256 // 2**level
        pad = 0 if level == 5 else 16
        rows = pl.ds(BASE[level] + pad + count * chunk, count)
        cells = sums[at : at + count] * jnp.concatenate([inv_ref[rows, :]] * PAIRS, axis=1)
        if level == 5:
            rough_ref[pl.ds(8 * chunk, 8), :] = cells
        else:
            out_ref[0, rows, :] = cells.astype(BF)
        at += count


def forward_kernel(
    lens, x_ref, row_ref, w_ref, ends_ref,
    mask_ref, pool_q_ref, stat_ref, cell_rows_ref, pool_k_ref,
    n1_ref, q_ref, k_ref, v_ref, attn_ref, low_ref, lse_ref,
    bias_ref, inv_ref, rough_ref, tile_bias_ref,
):
    length = lens[pl.program_id(0)]
    count_tables(length, bias_ref, inv_ref)
    zeros = jnp.zeros((16, D), BF)
    for level in range(LEVELS - 1):
        cells = SLOT // 2**level
        for ref in (k_ref, v_ref):
            ref[0, pl.ds(BASE[level], 16), :] = zeros
            ref[0, pl.ds(BASE[level] + 16 + cells, 16), :] = zeros
    rough_k, rough_v = rough_ref.at[0], rough_ref.at[1]
    query_shift, value_shift = joined(ends_ref, 0, 2), joined(ends_ref, 2, 2)

    def project(chunk):
        rows = pl.ds(256 * chunk, 256)
        xhat, _ = norm_parts(x_ref[0, rows, :].astype(F32))
        n1 = (xhat * row_ref[0:1] + row_ref[1:2]).astype(BF)
        n1_ref[0, rows, :] = n1
        yield
        joint = [mm(n1, w_ref[t]) for t in range(2)]
        yield
        q, k, v = (jnp.concatenate([j[:, at : at + HALF] for j in joint], axis=1) for at in (0, HALF, 2 * HALF))
        q_ref[0, rows, :] = (q + query_shift).astype(BF) * BF(0.125)
        k = keep_live(k, length, chunk, k_ref)
        v = keep_live(v + value_shift, length, chunk, v_ref)
        yield
        k, v = mm(pool_k_ref[...], k), mm(pool_k_ref[...], v)
        yield
        pack_cells(k, chunk, k_ref, rough_k, inv_ref)
        pack_cells(v, chunk, v_ref, rough_v, inv_ref)
        yield

    interleave([project(chunk) for chunk in range(4)], SKEW_P)
    k_ref[0, pl.ds(BASE[5], 32), :] = rough_k[...].astype(BF)
    v_ref[0, pl.ds(BASE[5], 32), :] = rough_v[...].astype(BF)

    def tile(i, bias):
        rows = pl.ds(128 * i, 128)
        bias[...] = mask_ref[i] + window(bias_ref, i, slice(None))
        q = q_ref[0, rows, :]
        cells = mm(pool_q_ref[...], q).astype(BF)
        lse = {}

        def quad(u):
            lanes = slice(256 * u, 256 * u + 256)
            pairs = [slice(0, 128), slice(128, 256)]
            keys = window(k_ref.at[0], i, lanes)
            c_one, c_rest = four_rows(cells[:64, lanes]), four_rows(cells[64:, lanes])
            q_two = [two_rows(q[:, lanes][:, p]) for p in pairs]
            yield
            fine = [mm_nt(keys[:160, p], q_two[j]) for j, p in enumerate(pairs)]
            one, rest = mm_nt(keys[160:SPLIT], c_one), mm_nt(keys[SPLIT:], c_rest)
            yield
            one = [one[:, p] + bias[160:SPLIT] for p in pairs]
            rest = [rest[:, p] + bias[SPLIT:] for p in pairs]
            fine = [[f[:, p] + bias[:160] for p in pairs] for f in fine]
            top_one = [jnp.max(s, axis=0, keepdims=True) for s in one]
            top_rest = [jnp.max(s, axis=0, keepdims=True) for s in rest]
            top_fine = [[jnp.max(s, axis=0, keepdims=True) for s in f] for f in fine]
            yield
            one = [jnp.exp(s - top) for s, top in zip(one, top_one)]
            rest = [jnp.exp(s - top) for s, top in zip(rest, top_rest)]
            weights, shares, inverse = [], [], []
            row = lax.broadcasted_iota(jnp.int32, (8, TILE), 0)
            for j in range(2):
                sum_one = jnp.sum(one[j], axis=0, keepdims=True)
                sum_rest = jnp.sum(rest[j], axis=0, keepdims=True)
                pair_w, pair_p, pair_i = [], [], []
                for h in range(2):
                    tops = to_rows(top_one[j], top_rest[j], stat_ref[h])
                    sums = to_rows(sum_one, sum_rest, stat_ref[h])
                    top = jnp.maximum(top_fine[j][h], jnp.max(tops, axis=0, keepdims=True))
                    w = jnp.exp(tops - top).astype(BF).astype(F32)
                    p = jnp.exp(fine[j][h] - top)
                    total = jnp.sum(p, axis=0, keepdims=True)
                    total = total + jnp.sum(jnp.where(row < 5, w * sums, 0.0), axis=0, keepdims=True)
                    lse[4 * u + 2 * j + h] = top + jnp.log(total)
                    pair_w.append(w)
                    pair_p.append(p.astype(BF))
                    pair_i.append(1.0 / total)
                weights.append(row_weights(pair_w, cell_rows_ref[...]))
                shares.append(jnp.concatenate(pair_p, axis=1))
                inverse.append(jnp.concatenate(pair_i, axis=1))
            values = window(v_ref.at[0], i, lanes)
            v_fine = [values[:160, p].T for p in pairs]
            v_rough = [values[160:, p].T for p in pairs]
            yield
            mixed = [mm(v_rough[j], corners(one[j].astype(BF), rest[j].astype(BF))) for j in range(2)]
            out = [mm(v_fine[j], shares[j]) for j in range(2)]
            yield
            out = [out[j] + mm(mixed[j].astype(BF), weights[j]) for j in range(2)]
            yield
            for j in range(2):
                full = diagonal(out[j] * inverse[j]).T
                high = full.astype(BF)
                own = slice(256 * u + 128 * j, 256 * u + 128 * j + 128)
                attn_ref[0, rows, own] = high
                low_ref[0, rows, own] = (full - high.astype(F32)).astype(BF)
            if u == 1:
                lse_ref[0, :, rows] = jnp.concatenate([lse[h] for h in range(HEADS)], axis=0)
            yield

        return [quad(0), quad(1)]

    interleave([chain for i in range(TILES) for chain in tile(i, tile_bias_ref.at[i])], SKEW_F)


def middle_kernel(
    x_ref, attn_ref, cot_ref, w_ref, row_ref, ends_ref,
    out_ref, g1_ref, grad_ref, gvec_ref, gbup_ref,
    gwo_ref, gup_ref, gdown_ref,
):
    step = pl.program_id(0)

    @pl.when(step == 0)
    def _():
        gwo_ref[...] = jnp.zeros_like(gwo_ref)
        gup_ref[...] = jnp.zeros_like(gup_ref)
        gdown_ref[...] = jnp.zeros_like(gdown_ref)
        gvec_ref[...] = jnp.zeros_like(gvec_ref)
        gbup_ref[...] = jnp.zeros_like(gbup_ref)

    attn = attn_ref[...]
    cot = cot_ref[...]
    branch = sum(mm_nt(attn[:, HALF * t : HALF * t + HALF], w_ref[:, t, :, :HALF].reshape(D, HALF)) for t in range(2))
    y1 = x_ref[...].astype(F32) + (branch + row_ref[2:3])
    xhat, scale = norm_parts(y1)
    n2 = (xhat * row_ref[3:4] + row_ref[4:5]).astype(BF)
    up_shift = joined(ends_ref, 4, 8)
    n2_t = n2.T
    cot_t = cot.T
    total = [y1 + row_ref[5:6], jnp.zeros_like(y1)]
    c = np.float32(np.sqrt(2.0 / np.pi))

    def hidden(part):
        cols = slice(512 * part, 512 * part + 512)
        at = HALF + 512 * (part % 2)
        up = w_ref[:, part // 2, :, at : at + 512].reshape(D, 512)
        at += FF // 2
        down_t = w_ref[:, part // 2, :, at : at + 512].reshape(D, 512)
        u = mm(n2, up) + up_shift[:, cols]
        dh = mm(cot, down_t)
        yield
        u2 = u * u
        t = jnp.tanh(u * (c + (c * 0.044715) * u2))
        h = 0.5 + 0.5 * t
        hid = (u * h).astype(BF)
        slope = h + 2.0 * h * (1.0 - h) * u * (c + (3.0 * c * 0.044715) * u2)
        dhp = dh * slope
        dhp_b = dhp.astype(BF)
        gbup_ref[:, cols] += column_sum(dhp)
        yield
        total[0] = total[0] + mm_nt(hid, down_t)
        total[1] = total[1] + mm_nt(dhp_b, up)
        gdown_ref[:, cols] += mm(cot_t, hid)
        gup_ref[:, cols] += mm(n2_t, dhp_b)
        yield

    interleave([hidden(part) for part in range(4)], SKEW_M)
    out, dn2 = total
    out_ref[...] = out.astype(BF)
    cot_f = cot.astype(F32)
    dy1 = cot_f + norm_back(dn2, xhat, scale, row_ref[3:4])
    g1 = dy1.astype(BF)
    g1_ref[...] = g1
    gwo_ref[...] += mm(g1.T, attn)
    gvec_ref[...] += jnp.concatenate(
        [column_sum(g1.astype(F32)), column_sum(dn2 * xhat), column_sum(dn2), column_sum(cot_f), jnp.zeros((4, D), F32)],
        axis=0,
    )


    @pl.when(step == pl.num_programs(0) - 1)
    def _():
        rows = D // grad_ref.shape[0]
        for t in range(2):
            at = 0
            for ref, width in ((gwo_ref, HALF), (gup_ref, FF // 2), (gdown_ref, FF // 2)):
                part = ref[:, width * t : width * t + width].astype(BF)
                grad_ref[:, t, :, at : at + width] = part.reshape(grad_ref.shape[0], rows, width)
                at += width


def backward_kernel(
    lens, x_ref, n1_ref, q_ref, k_ref, v_ref, attn_ref, low_ref, lse_ref, g1_ref,
    row_ref, w_ref, wo_t_ref,
    mask_ref, pool_q_ref, stat_ref, cell_rows_ref, expand_ref, spread_k_ref,
    dx_ref, gqkv_ref, gvec_ref,
    bias_ref, inv_ref, tile_bias_ref, dk_ref, dv_ref, dqkv_ref,
):
    step = pl.program_id(0)

    @pl.when(step == 0)
    def _():
        gqkv_ref[...] = jnp.zeros_like(gqkv_ref)
        gvec_ref[...] = jnp.zeros_like(gvec_ref)

    length = lens[step]
    count_tables(length, bias_ref, inv_ref)
    touched = (set(), set())
    head_of = lax.broadcasted_iota(jnp.int32, (HEADS, D), 1) // HD
    heads = (head_of == lax.broadcasted_iota(jnp.int32, (HEADS, D), 0)).astype(BF)

    def tile(i, bias):
        rows = pl.ds(128 * i, 128)
        bias[...] = mask_ref[i] + window(bias_ref, i, slice(None))
        q = q_ref[0, rows, :]
        cells = mm(pool_q_ref[...], q).astype(BF)
        da = jnp.concatenate([mm(g1_ref[0, rows, :], wo_t_ref[:, t, :, :HALF].reshape(D, HALF)) for t in range(2)], axis=1)
        da = da.astype(BF)
        product = da.astype(F32) * (attn_ref[0, rows, :].astype(F32) + low_ref[0, rows, :].astype(F32))
        high = product.astype(BF)
        delta = mm_nt(heads, high) + mm_nt(heads, (product - high.astype(F32)).astype(BF))
        lse = lse_ref[0, :, rows]

        def quad(u):
            lanes = slice(256 * u, 256 * u + 256)
            pairs = [slice(0, 128), slice(128, 256)]
            keys = window(k_ref.at[0], i, lanes)
            values = window(v_ref.at[0], i, lanes)
            c_one, c_rest = four_rows(cells[:64, lanes]), four_rows(cells[64:, lanes])
            q_two = [two_rows(q[:, lanes][:, p]) for p in pairs]
            d_two = [two_rows(da[:, lanes][:, p]) for p in pairs]
            yield
            fine = [mm_nt(keys[:160, p], q_two[j]) for j, p in enumerate(pairs)]
            one, rest = mm_nt(keys[160:SPLIT], c_one), mm_nt(keys[SPLIT:], c_rest)
            dp = [mm_nt(values[:160, p], d_two[j]) for j, p in enumerate(pairs)]
            yield
            ones, rests, weights, shares, slopes, rows_delta = [], [], [], [], [], []
            for j, pair in enumerate(pairs):
                s_one, s_rest = one[:, pair] + bias[160:SPLIT], rest[:, pair] + bias[SPLIT:]
                top_one, top_rest = jnp.max(s_one, axis=0, keepdims=True), jnp.max(s_rest, axis=0, keepdims=True)
                ones.append(jnp.exp(s_one - top_one))
                rests.append(jnp.exp(s_rest - top_rest))
                pair_w, pair_p, pair_s = [], [], []
                for h, p in enumerate(pairs):
                    head = 4 * u + 2 * j + h
                    own_lse, own_delta = lse[head : head + 1], delta[head : head + 1]
                    pair_w.append(jnp.exp(to_rows(top_one, top_rest, stat_ref[h]) - own_lse))
                    share = jnp.exp(fine[j][:, p] + bias[:160] - own_lse)
                    pair_s.append((share * (dp[j][:, p] - own_delta)).astype(BF))
                    pair_p.append(share.astype(BF))
                weights.append(row_weights(pair_w, cell_rows_ref[...]))
                shares.append(jnp.concatenate(pair_p, axis=1))
                slopes.append(jnp.concatenate(pair_s, axis=1))
                head = 4 * u + 2 * j
                both = jnp.concatenate([delta[head : head + 1], delta[head + 1 : head + 2]], axis=1)
                top = both.astype(BF).astype(F32)
                rows_delta.append(jnp.concatenate([top, both - top, jnp.zeros((6, 256), F32)], axis=0).astype(BF))
            k_fine = [keys[:160, p].T for p in pairs]
            k_rough = [keys[160:, p].T for p in pairs]
            yield
            d_cells = [mm(weights[j], d_two[j]).astype(BF) for j in range(2)]
            delta_cells = [jnp.sum(mm_nt(rows_delta[j], weights[j]), axis=0, keepdims=True) for j in range(2)]
            dv_fine = [mm(shares[j], d_two[j]) for j in range(2)]
            yield
            d_one, d_rest = (corners(d_cells[0][a : a + 128], d_cells[1][a : a + 128]) for a in (0, 128))
            dp_one, dp_rest = mm_nt(values[160:SPLIT], d_one), mm_nt(values[SPLIT:], d_rest)
            dk_fine = [mm(slopes[j], q_two[j]) for j in range(2)]
            dq = [mm(k_fine[j], slopes[j]) for j in range(2)]
            yield
            s_one = [(ones[j] * (dp_one[:, p] - delta_cells[j][:, :128])).astype(BF) for j, p in enumerate(pairs)]
            s_rest = [(rests[j] * (dp_rest[:, p] - delta_cells[j][:, 128:])).astype(BF) for j, p in enumerate(pairs)]
            dv_one = mm(jnp.concatenate([e.astype(BF) for e in ones], axis=1), d_one)
            dv_rest = mm(jnp.concatenate([e.astype(BF) for e in rests], axis=1), d_rest)
            yield
            dq_cells = [mm(k_rough[j], corners(s_one[j], s_rest[j])).astype(BF) for j in range(2)]
            dk_one = mm(jnp.concatenate(s_one, axis=1), c_one)
            dk_rest = mm(jnp.concatenate(s_rest, axis=1), c_rest)
            yield
            dq = [diagonal(dq[j] + mm(dq_cells[j], expand_ref[...])) * 0.125 for j in range(2)]
            dk = jnp.concatenate([jnp.concatenate(dk_fine, axis=1), dk_one, dk_rest], axis=0)
            dv = jnp.concatenate([jnp.concatenate(dv_fine, axis=1), dv_one, dv_rest], axis=0)
            at = 0
            for start, count in window_parts(i):
                for seen, begin, n in runs(touched[u], start, count):
                    part = pl.ds(begin, n)
                    for ref, grad in ((dk_ref, dk), (dv_ref, dv)):
                        block = grad[at + begin - start : at + begin - start + n]
                        ref[part, lanes] = ref[part, lanes] + block if seen else block
                at += count
            yield
            for j in range(2):
                at = 3 * HALF * u + 128 * j
                dqkv_ref[rows, at : at + 128] = dq[j].T.astype(BF)
            yield

        return [quad(0), quad(1)]

    interleave([chain for i in range(TILES) for chain in tile(i, tile_bias_ref.at[i])], SKEW_B)

    sums = []

    def finish(chunk):
        rows = pl.ds(256 * chunk, 256)
        own = pl.ds(16 + 256 * chunk, 256)
        live = lax.broadcasted_iota(jnp.int32, (256, D), 0) + 256 * chunk < length
        wide = []
        for ref in (dk_ref, dv_ref):
            cells = []
            for level in range(1, LEVELS):
                count = 256 // 2**level
                pad = 0 if level == 5 else 16
                part = pl.ds(BASE[level] + pad + count * chunk, count)
                cells.append(ref[part, :] * jnp.concatenate([inv_ref[part, :]] * PAIRS, axis=1))
            cells.append(jnp.zeros((8, D), F32))
            wide.append(jnp.concatenate(cells, axis=0).astype(BF))
        yield
        wide = [mm(spread_k_ref[...], w) for w in wide]
        yield
        for ref, at, w in zip((dk_ref, dv_ref), (HALF, 2 * HALF), wide):
            grad = jnp.where(live, ref[own, :] + w, 0.0).astype(BF)
            dqkv_ref[rows, at : at + HALF] = grad[:, :HALF]
            dqkv_ref[rows, at + 3 * HALF : at + 4 * HALF] = grad[:, HALF:]
        yield
        parts = [dqkv_ref[rows, 3 * HALF * t : 3 * HALF * t + 3 * HALF] for t in range(2)]
        dn1 = mm_nt(parts[0], w_ref[0]) + mm_nt(parts[1], w_ref[1])
        xhat, scale = norm_parts(x_ref[0, rows, :].astype(F32))
        yield
        dx = g1_ref[0, rows, :].astype(F32) + norm_back(dn1, xhat, scale, row_ref[0:1])
        dx_ref[0, rows, :] = dx.astype(BF)
        col = [column_sum(part.astype(F32)) for part in parts]
        sums.append(
            jnp.concatenate(
                [
                    column_sum(dn1 * xhat), column_sum(dn1),
                    jnp.concatenate([c[:, :HALF] for c in col], axis=1),
                    jnp.concatenate([c[:, 2 * HALF :] for c in col], axis=1),
                    jnp.zeros((4, D), F32),
                ],
                axis=0,
            )
        )
        yield

    interleave([finish(chunk) for chunk in range(4)], SKEW_E)
    gvec_ref[...] += sums[0] + sums[1] + sums[2] + sums[3]
    n1_t = n1_ref[0].T
    for t in range(2):
        gqkv_ref[t] += mm(n1_t, dqkv_ref[:, 3 * HALF * t : 3 * HALF * t + 3 * HALF])


def whole(shape):
    return pl.BlockSpec(shape, lambda *_: (0,) * len(shape))


def per_sequence(*shape):
    return pl.BlockSpec((1,) + shape, lambda s, *_: (s,) + (0,) * len(shape))


LIMIT = 60 * 1024 * 1024


def attention_forward(x, lens, row, w, ends, const):
    count = x.shape[0]
    return pl.pallas_call(
        forward_kernel,
        grid_spec=pltpu.PrefetchScalarGridSpec(
            num_scalar_prefetch=1,
            grid=(count,),
            in_specs=[
                per_sequence(SLOT, D), whole((8, D)), whole((2, D, 3 * HALF)), whole((2, 16, 128)),
                whole((TILES, WIN, TILE)), whole((TILE, TILE)), whole((2, 8, TILE)), whole((TILE, TILE)), whole((256, 256)),
            ],
            out_specs=[
                per_sequence(SLOT, D), per_sequence(SLOT, D), per_sequence(CELL_ROWS, D), per_sequence(CELL_ROWS, D),
                per_sequence(SLOT, D), per_sequence(SLOT, D), per_sequence(HEADS, SLOT),
            ],
            scratch_shapes=[
                pltpu.VMEM((CELL_ROWS, 128), F32), pltpu.VMEM((CELL_ROWS, 128), F32), pltpu.VMEM((2, 32, D), F32),
                pltpu.VMEM((TILES, WIN, TILE), F32),
            ],
        ),
        out_shape=[
            jax.ShapeDtypeStruct((count, SLOT, D), BF), jax.ShapeDtypeStruct((count, SLOT, D), BF),
            jax.ShapeDtypeStruct((count, CELL_ROWS, D), BF), jax.ShapeDtypeStruct((count, CELL_ROWS, D), BF),
            jax.ShapeDtypeStruct((count, SLOT, D), BF), jax.ShapeDtypeStruct((count, SLOT, D), BF),
            jax.ShapeDtypeStruct((count, HEADS, SLOT), F32),
        ],
        compiler_params=pltpu.CompilerParams(vmem_limit_bytes=LIMIT),
        cost_estimate=pl.CostEstimate(flops=count * 30 * 10**9, bytes_accessed=count * 10**7, transcendentals=0),
        name="attention_forward",
    )(lens, x, row, w, ends, const["mask"], const["pool_q"], const["stat"], const["cell_rows"], const["pool_k"])


ROWS = 512


def middle(x, attn, cot, w, row, ends):
    total = x.shape[0]
    rows = pl.BlockSpec((ROWS, D), lambda s: (s, 0))
    return pl.pallas_call(
        middle_kernel,
        grid=(total // ROWS,),
        in_specs=[
            rows, rows, rows, whole(w.shape), whole((8, D)), whole((2, 16, 128)),
        ],
        out_specs=[rows, rows, whole(w.shape), whole((8, D)), whole((1, FF))],
        scratch_shapes=[pltpu.VMEM((D, D), F32), pltpu.VMEM((D, FF), F32), pltpu.VMEM((D, FF), F32)],
        out_shape=[
            jax.ShapeDtypeStruct((total, D), BF), jax.ShapeDtypeStruct((total, D), BF), jax.ShapeDtypeStruct(w.shape, BF),
            jax.ShapeDtypeStruct((8, D), F32), jax.ShapeDtypeStruct((1, FF), F32),
        ],
        compiler_params=pltpu.CompilerParams(vmem_limit_bytes=LIMIT),
        name="middle",
    )(x, attn, cot, w, row, ends)


def attention_backward(x, lens, n1, q, k, v, attn, low, lse, g1, row, w, rest, const):
    count = x.shape[0]
    wo_t = pl.BlockSpec(rest.shape[:3] + (HALF,), lambda *_: (0, 0, 0, 0))
    return pl.pallas_call(
        backward_kernel,
        grid_spec=pltpu.PrefetchScalarGridSpec(
            num_scalar_prefetch=1,
            grid=(count,),
            in_specs=[
                per_sequence(SLOT, D), per_sequence(SLOT, D), per_sequence(SLOT, D),
                per_sequence(CELL_ROWS, D), per_sequence(CELL_ROWS, D), per_sequence(SLOT, D), per_sequence(SLOT, D),
                per_sequence(HEADS, SLOT), per_sequence(SLOT, D),
                whole((8, D)), whole((2, D, 3 * HALF)), wo_t,
                whole((TILES, WIN, TILE)), whole((TILE, TILE)), whole((2, 8, TILE)), whole((TILE, TILE)),
                whole((256, 256)), whole((256, 256)),
            ],
            out_specs=[per_sequence(SLOT, D), whole((2, D, 3 * HALF)), whole((8, D))],
            scratch_shapes=[
                pltpu.VMEM((CELL_ROWS, 128), F32), pltpu.VMEM((CELL_ROWS, 128), F32), pltpu.VMEM((TILES, WIN, TILE), F32),
                pltpu.VMEM((CELL_ROWS, D), F32), pltpu.VMEM((CELL_ROWS, D), F32), pltpu.VMEM((SLOT, 3 * D), BF),
            ],
        ),
        out_shape=[
            jax.ShapeDtypeStruct((count, SLOT, D), BF), jax.ShapeDtypeStruct((2, D, 3 * HALF), F32),
            jax.ShapeDtypeStruct((8, D), F32),
        ],
        compiler_params=pltpu.CompilerParams(vmem_limit_bytes=LIMIT),
        cost_estimate=pl.CostEstimate(flops=count * 40 * 10**9, bytes_accessed=count * 10**7, transcendentals=0),
        name="attention_backward",
    )(
        lens, x, n1, q, k, v, attn, low, lse, g1, row, w, rest,
        const["mask"], const["pool_q"], const["stat"], const["cell_rows"], const["expand"], const["spread_k"],
    )


def bits_of(count):
    return count.bit_length() - 1


def all_bits(n_dp, n_t):
    return [("tensor", b) for b in reversed(range(bits_of(n_t)))] + [("dp", b) for b in reversed(range(bits_of(n_dp)))]


def gather_orders(n_dp, n_t):
    far = [("dp", b) for b in reversed(range(2, bits_of(n_dp)))]
    near = [("dp", 1)]
    side = [("tensor", b) for b in reversed(range(bits_of(n_t)))]
    core_bit = [("dp", 0)]
    return far + near + side + core_bit, far + side + near + core_bit


def own_bit(bit):
    axis, b = bit
    return (lax.axis_index(axis) // 2**b) % 2


def partner(bit):
    axis, b = bit
    return {axis: lax.axis_index(axis) + (1 - 2 * own_bit(bit)) * 2**b}


def meet(bits):
    barrier = pltpu.get_barrier_semaphore()
    for bit in bits:
        pl.semaphore_signal(barrier, inc=1, device_id=partner(bit), device_id_type=pl.DeviceIdType.MESH)
    pl.semaphore_wait(barrier, len(bits))


def halves(width):
    if width % 256:
        return [(0, width)]
    return [(0, width // 2), (width // 2, width // 2)]


def gather_kernel(
    bits, orders, parts, shard_ref, ends_ref, out_ref, all_ends_ref, own_sem, send_sems, recv_sems, ends_own_sem, ends_sems
):
    own = pltpu.make_async_copy(shard_ref, out_ref.at[tuple(own_bit(bit) for bit in bits)], own_sem)
    own.start()
    side = [bit for bit in bits if bit[0] == "tensor"]
    own_ends = pltpu.make_async_copy(ends_ref, all_ends_ref.at[tuple(own_bit(bit) for bit in side)], ends_own_sem)
    own_ends.start()
    meet(bits)
    pending = []
    own_ends.wait()

    def ends_copy(step):
        place = all_ends_ref.at[tuple(slice(None) if j < step else own_bit(bit) for j, bit in enumerate(side))]
        return pltpu.make_async_remote_copy(
            src_ref=place, dst_ref=place, send_sem=ends_sems.at[0, step], recv_sem=ends_sems.at[1, step],
            device_id=partner(side[step]), device_id_type=pl.DeviceIdType.MESH,
        )

    if side:
        ends_copy(0).start()
    for step in range(len(bits)):
        for part, (at, width) in enumerate(parts):
            order = orders[part]
            done = order[:step]
            index = tuple(slice(None) if bit in done else own_bit(bit) for bit in bits)
            place = out_ref.at[index + (slice(None), pl.ds(at, width))]
            source = shard_ref.at[:, pl.ds(at, width)] if step == 0 else place
            if step > 0:
                pending[(step - 1) * len(parts) + part].wait_recv()
            copy = pltpu.make_async_remote_copy(
                src_ref=source, dst_ref=place,
                send_sem=send_sems.at[step, part], recv_sem=recv_sems.at[step, part],
                device_id=partner(order[step]), device_id_type=pl.DeviceIdType.MESH,
            )
            if step == 1 and part == 0:
                own.wait()
            copy.start()
            pending.append(copy)
    for copy in pending[-len(parts) :]:
        copy.wait_recv()
    for step in range(len(side)):
        ends_copy(step).wait_recv()
        if step + 1 < len(side):
            ends_copy(step + 1).start()
    for step in range(len(side)):
        ends_copy(step).wait_send()
    for copy in pending:
        copy.wait_send()


def gather(shard, ends, n_dp, n_t):
    rows, width = shard.shape
    bits, orders, parts = all_bits(n_dp, n_t), gather_orders(n_dp, n_t), halves(width)
    side = bits_of(n_t)
    anywhere = pl.BlockSpec(memory_space=pl.ANY)
    out, all_ends = pl.pallas_call(
        functools.partial(gather_kernel, bits, orders, parts),
        in_specs=[anywhere, anywhere],
        out_specs=[anywhere, anywhere],
        out_shape=[
            jax.ShapeDtypeStruct((2,) * len(bits) + (rows, width), shard.dtype),
            jax.ShapeDtypeStruct((2,) * side + ends.shape, ends.dtype),
        ],
        scratch_shapes=[
            pltpu.SemaphoreType.DMA, pltpu.SemaphoreType.DMA((len(bits), len(parts))),
            pltpu.SemaphoreType.DMA((len(bits), len(parts))), pltpu.SemaphoreType.DMA,
            pltpu.SemaphoreType.DMA((2, max(side, 1))),
        ],
        compiler_params=pltpu.CompilerParams(collective_id=0, has_side_effects=True),
        name="gather",
    )(shard, ends)
    return out.reshape(n_t, n_dp, rows, width), all_ends.reshape((n_t,) + ends.shape)


def reduce_kernel(bits, orders, parts, rows, grad_ref, vec_ref, out_ref, vec_out_ref, *scratch):
    steps, count = len(bits), len(parts)
    sends, recvs, sums = (scratch[j * steps * count : (j + 1) * steps * count] for j in range(3))
    vec_recv, send_sems, recv_sems, vec_send_sems, vec_recv_sems = scratch[3 * steps * count :]
    meet(bits)
    vec_out_ref[...] = vec_ref[...]

    def vec_copy(step):
        return pltpu.make_async_remote_copy(
            src_ref=vec_recv.at[2 * step], dst_ref=vec_recv.at[2 * step + 1],
            send_sem=vec_send_sems.at[step], recv_sem=vec_recv_sems.at[step],
            device_id=partner(orders[0][steps - 1 - step]), device_id_type=pl.DeviceIdType.MESH,
        )

    def copy_of(step, part):
        j = step * count + part
        return pltpu.make_async_remote_copy(
            src_ref=sends[j], dst_ref=recvs[j], send_sem=send_sems.at[step, part], recv_sem=recv_sems.at[step, part],
            device_id=partner(orders[part][steps - 1 - step]), device_id_type=pl.DeviceIdType.MESH,
        )

    def pieces(step, part):
        order = orders[part][::-1]
        left = [bit for bit in bits if bit not in order[:step]]
        j = left.index(order[step])
        low = 2 ** (len(left) - 1 - j)
        mine = own_bit(order[step])
        out = []
        for a in range(2**j):
            for c in range(low):
                out.append(((a * 2 + 1 - mine) * low + c, (a * 2 + mine) * low + c, a * low + c))
        at, width = parts[part]
        source = sums[(step - 1) * count + part] if step else grad_ref.at[:, :, pl.ds(at, width)]
        return out, source

    for step in range(steps):
        vec_recv[2 * step] = vec_out_ref[...]
        vec_copy(step).start()
        for part in range(count):
            blocks, source = pieces(step, part)
            for away, _, to in blocks:
                sends[step * count + part][to] = source[away].astype(BF)
            copy_of(step, part).start()
        for part in range(count):
            copy_of(step, part).wait_recv()
            blocks, source = pieces(step, part)
            for _, keep, to in blocks:
                total = source[keep] + recvs[step * count + part][to].astype(F32)
                if step == steps - 1:
                    at, width = parts[part]
                    out_ref[:, at : at + width] = total
                else:
                    sums[step * count + part][to] = total
        vec_copy(step).wait_recv()
        vec_out_ref[...] += vec_recv[2 * step + 1]
    for step in range(steps):
        vec_copy(step).wait_send()
        for part in range(count):
            copy_of(step, part).wait_send()


def reduce(grad, vec, n_dp, n_t):
    rows, width = grad.shape[2:]
    bits, orders, parts = all_bits(n_dp, n_t), gather_orders(n_dp, n_t), halves(width)
    steps = len(bits)
    blocks = [(2 ** (steps - 1 - step), rows, w) for step in range(steps) for _, w in parts]
    sems = pltpu.SemaphoreType.DMA
    vmem = pl.BlockSpec(memory_space=pltpu.VMEM)
    return pl.pallas_call(
        functools.partial(reduce_kernel, bits, orders, parts, rows),
        in_specs=[vmem, vmem],
        out_specs=[vmem, vmem],
        out_shape=[jax.ShapeDtypeStruct((rows, width), F32), jax.ShapeDtypeStruct(vec.shape, F32)],
        scratch_shapes=[pltpu.VMEM(b, BF) for b in blocks] * 2
        + [pltpu.VMEM(b, F32) for b in blocks]
        + [
            pltpu.VMEM((2 * steps,) + vec.shape, F32), sems((steps, len(parts))), sems((steps, len(parts))),
            sems((steps,)), sems((steps,)),
        ],
        compiler_params=pltpu.CompilerParams(collective_id=1, has_side_effects=True, vmem_limit_bytes=LIMIT),
        name="reduce",
    )(grad.reshape(n_t * n_dp, rows, width), vec)


def to_pairs(grid, widths):
    n_t, n_dp, rows, _ = grid.shape
    grid = grid.reshape(n_t, n_dp * rows, -1)
    if n_t == 2:
        return grid
    out, at = [], 0
    for width in widths:
        part = grid[:, :, at : at + width].reshape(2, n_t // 2, D, width)
        out.append(part.transpose(0, 2, 1, 3).reshape(2, D, n_t // 2 * width))
        at += width
    return jnp.concatenate(out, axis=2)


def from_pairs(grid, widths, n_dp, n_t):
    if n_t != 2:
        out, at = [], 0
        for width in widths:
            full = width * n_t // 2
            part = grid[:, :, at : at + full].reshape(2, D, n_t // 2, width)
            out.append(part.transpose(0, 2, 1, 3).reshape(n_t, D, width))
            at += full
        grid = jnp.concatenate(out, axis=2)
    return grid.reshape(n_t, n_dp, D // n_dp, -1)


def own_sequences(values, lengths, tensor_count):
    micro, rows, width = values[0].shape
    t = lax.axis_index("tensor")
    if rows % SLOT == 0:
        per = rows // SLOT
        own = lax.dynamic_slice_in_dim(lengths, t * per, per, 1).reshape(-1)
        return [v.reshape(micro * per, SLOT, width) for v in values], own
    pieces = SLOT // rows
    assert micro == pieces
    groups = [[g * pieces + j for j in range(pieces)] for g in range(tensor_count // pieces)]
    out = [lax.all_to_all(v, "tensor", 0, 1, axis_index_groups=groups, tiled=True) for v in values]
    sequence = lax.dynamic_slice(lengths, (t % pieces, t // pieces), (1, 1))
    return out, sequence.reshape(-1)


def own_rows(values, shape, tensor_count):
    micro, rows, width = shape
    if rows % SLOT == 0:
        return [v.reshape(shape) for v in values]
    pieces = SLOT // rows
    groups = [[g * pieces + j for j in range(pieces)] for g in range(tensor_count // pieces)]
    return [
        lax.all_to_all(v, "tensor", 1, 0, axis_index_groups=groups, tiled=True).reshape(shape) for v in values
    ]


def core(x, lens, cot, row, w, ends, rest):
    const = {name: jnp.asarray(value) for name, value in constants().items()}
    count = x.shape[0]
    flat = (count * SLOT, D)
    n1, q, k, v, attn, low, lse = attention_forward(x, lens, row, w, ends, const)
    out, g1, grad_rest, mid_vec, gbup = middle(
        x.reshape(flat), attn.reshape(flat), cot.reshape(flat), rest, row, ends
    )
    dx, gqkv, pre_vec = attention_backward(
        x, lens, n1, q, k, v, attn, low, lse, g1.reshape(count, SLOT, D), row, w, rest, const
    )
    return out, dx, grad_rest, mid_vec, gbup, gqkv, pre_vec


def on_device(
    inputs, lengths, pre_gain, pre_shift, query_weight, key_weight, value_weight, query_bias, value_bias,
    output_weight, output_bias, mid_gain, mid_shift, up_weight, up_bias, down_weight, down_bias, cotangent,
):
    n_dp, n_t = lax.axis_size("dp"), lax.axis_size("tensor")
    t = lax.axis_index("tensor")
    (x, cot), lens = own_sequences([inputs, cotangent], lengths, n_t)

    n_q, n_f = query_weight.shape[1], up_weight.shape[1]
    vectors = (pre_gain, pre_shift, output_bias, mid_gain, mid_shift, down_bias, down_bias, down_bias)
    row = jnp.stack(vectors).astype(F32)
    first = jnp.concatenate([query_weight, key_weight, value_weight], axis=1)
    second = jnp.concatenate([output_weight.T, up_weight, down_weight.T], axis=1)
    ends = jnp.concatenate([query_bias, value_bias, up_bias])
    ends = jnp.pad(ends, (0, 2048 - ends.shape[0])).reshape(16, 128)
    w, ends = gather(first, ends, n_dp, n_t)
    w = to_pairs(w, (n_q,) * 3)
    rest = lax.all_gather(second, ("dp", "tensor"), axis=0, tiled=False)
    rest = rest.reshape(n_dp, n_t, D // n_dp, -1)
    if n_t != 2:
        rest = to_pairs(rest.transpose(1, 0, 2, 3), (n_q, n_f, n_f)).reshape(2, 16, 32, REST).transpose(1, 0, 2, 3)
        flat = ends.reshape(n_t, -1)
        parts = [flat[:, a : a + n].reshape(2, -1) for a, n in ((0, n_q), (n_q, n_q), (2 * n_q, n_f))]
        ends = jnp.concatenate(parts + [jnp.zeros((2, 512), ends.dtype)], axis=1).reshape(2, 16, 128)
    out, dx, grad_rest, mid_vec, gbup, gqkv, pre_vec = core(x, lens, cot, row, w, ends, rest)
    if n_t != 2:
        grad_rest = grad_rest.transpose(1, 0, 2, 3).reshape(2, D, REST)
        grad_rest = from_pairs(grad_rest, (n_q, n_f, n_f), n_dp, n_t).transpose(1, 0, 2, 3)
    grad_rest = grad_rest.reshape(n_dp * n_t, D // n_dp, -1)
    grad_rest = lax.psum_scatter(grad_rest, ("dp", "tensor"), scatter_dimension=0, tiled=False).astype(F32)
    vec = jnp.concatenate([pre_vec[:4], mid_vec[:4], gbup.reshape(4, D), jnp.zeros((4, D), F32)], axis=0)
    grad_first, vec = reduce(from_pairs(gqkv, (n_q,) * 3, n_dp, n_t), vec, n_dp, n_t)
    grad_q, grad_k, grad_v = (grad_first[:, n_q * j : n_q * j + n_q] for j in range(3))
    grad_o, grad_up, grad_down = grad_rest[:, :n_q].T, grad_rest[:, n_q : n_q + n_f], grad_rest[:, n_q + n_f :].T

    def mine(v):
        n = v.shape[0] // n_t
        return lax.dynamic_slice_in_dim(v, t * n, n, 0)

    out, dx = own_rows([out.reshape(x.shape), dx], inputs.shape, n_t)
    return (
        out, dx, vec[0], vec[1], grad_q, grad_k, grad_v, mine(vec[2]), mine(vec[3]), grad_o, vec[4], vec[5], vec[6],
        grad_up, mine(vec[8:12].reshape(-1)), grad_down, vec[7],
    )


def solution(mesh):
    rows = P(None, ("dp", "tensor"), None)
    by_row, by_column = P("dp", "tensor"), P("tensor", "dp")
    in_specs = (
        rows, P(None, "dp"), P(), P(), by_row, by_row, by_row, P("tensor"), P("tensor"), by_column, P(), P(), P(),
        by_row, P("tensor"), by_column, P(), rows,
    )
    out_specs = (
        rows, rows, P(), P(), by_row, by_row, by_row, P("tensor"), P("tensor"), by_column, P(), P(), P(),
        by_row, P("tensor"), by_column, P(),
    )
    return jax.shard_map(on_device, mesh=mesh, in_specs=in_specs, out_specs=out_specs, check_vma=False)
```

```python
import functools

import jax
import jax.numpy as jnp
import ml_dtypes
import numpy as np
from jax import lax
from jax.experimental import pallas as pl
from jax.experimental.pallas import tpu as pltpu
from jax.sharding import PartitionSpec as P

D = 512
HD = 64
FF = 2048
NR = 16
LEVELS = 6
SLOT = 1024
TILE = 128
TILES = SLOT // TILE
PAIRS = D // 128
HEADS = D // HD
HALF = D // 2
REST = HALF + FF
SMALL = 40
EPS = 1e-05
NEG = -1e30

BASE = (0, 1056, 1600, 1888, 2048, 2144)
CELL_ROWS = 2176
WIN_ROWS = (160, 96, 64, 32, 32, 16)
WIN_AT = (0, 160, 256, 320, 352, 384)
WIN = 400
COARSE = WIN - 160
LANE_AT = (0, 0, 0, 32, 48, 56)
SPLIT = WIN_AT[2]
BF = jnp.bfloat16
F32 = jnp.float32


def window_parts(i):
    two, four = i // 2, i // 4
    return (
        (128 * i, 160),
        (BASE[1] + 64 * i, 96),
        (BASE[2] + 32 * i, 64),
        (BASE[3] + 16 * i, 16),
        (BASE[3] + 16 * i + 32, 16),
        (BASE[4] + 16 * two, 16),
        (BASE[4] + 16 * two + 32, 16),
        (BASE[5] + 16 * (1 - four), 16),
    )


def mask_table():
    table = np.full((TILES, WIN, TILE), NEG, np.float32)
    for i in range(TILES):
        at = 0
        for start, count in window_parts(i):
            level = max(l for l in range(LEVELS) if WIN_AT[l] <= at)
            pad = 0 if level == 5 else 16
            cell = (start - BASE[level] - pad + np.arange(count))[:, None]
            here = TILE >> level
            query = (((128 * i) >> level) + np.arange(here))[None, :]
            good = np.abs(cell // 16 - query // 16) <= 1
            if level > 0:
                good &= np.abs((2 * cell) // 16 - (2 * query) // 16) > 1
            for head in range(1 if level == 0 else 2):
                lane = 64 * head + LANE_AT[level]
                table[i, at : at + count, lane : lane + here] = np.where(good, 0.0, NEG)
            at += count
    return table


def constants():
    t = np.arange(TILE)
    pool_q = np.zeros((TILE, TILE), np.float32)
    stat = np.zeros((2, 8, TILE), np.int32)
    expand = np.zeros((256, 256), np.float32)
    pool_k = np.zeros((256, 256), np.float32)
    t2 = np.arange(256)
    at = 0
    for level in range(1, LEVELS):
        width = 2**level
        half = 0 if level == 1 else 64
        pool_q[half + LANE_AT[level] + t // width, t] = 1.0 / width
        for head in range(2):
            stat[head, level - 1 :] = 64 * head + LANE_AT[level] + t // width
            expand[2 * half + 64 * head + LANE_AT[level] + t // width, 128 * head + t] = 1.0 / width
        pool_k[at + t2 // width, t2] = 1.0
        at += 256 // width
    half = ml_dtypes.bfloat16
    return {
        "mask": mask_table(),
        "pool_q": pool_q.astype(half),
        "stat": stat,
        "cell_rows": (pool_q > 0).astype(np.float32),
        "expand": expand.astype(half),
        "pool_k": pool_k.astype(half),
        "spread_k": pool_k.T.copy().astype(half),
    }


def mm(a, b):
    return lax.dot_general(a, b, (((1,), (0,)), ((), ())), preferred_element_type=F32)


def mm_nt(a, b):
    return lax.dot_general(a, b, (((1,), (1,)), ((), ())), preferred_element_type=F32)


def mm_tn(a, b):
    return lax.dot_general(a, b, (((0,), (0,)), ((), ())), preferred_element_type=F32)


def norm_parts(values):
    centre = values - jnp.mean(values, axis=-1, keepdims=True)
    spread = jnp.mean(centre * centre, axis=-1, keepdims=True)
    scale = lax.rsqrt(spread + EPS)
    return centre * scale, scale


def norm_back(grad, xhat, scale, gain):
    e = grad * gain
    return (e - jnp.mean(e, axis=-1, keepdims=True) - xhat * jnp.mean(e * xhat, axis=-1, keepdims=True)) * scale


def joined(ref, first, count):
    parts = [ref[t, r : r + 1, :].astype(F32) for t in range(2) for r in range(first, first + count)]
    return jnp.concatenate(parts, axis=1)


def vector(ref, j):
    return jnp.concatenate([ref[16 + 4 * j + r : 17 + 4 * j + r, :].astype(F32) for r in range(4)], axis=1)


def column_sum(values):
    return jnp.sum(values, axis=0, keepdims=True)


def count_tables(length, bias_ref, inv_ref):
    length = length.astype(F32)
    for level in range(LEVELS):
        width = 2**level
        pad = 0 if level == 5 else 16
        count = SLOT // width + 2 * pad
        cell = lax.broadcasted_iota(jnp.int32, (count, 128), 0) - pad
        live = jnp.where(cell < 0, 0.0, length - (cell * width).astype(F32))
        rows = pl.ds(BASE[level], count)
        if level == 0:
            bias_ref[rows, :] = jnp.where(live > 0.0, 0.0, NEG)
        else:
            some = jnp.clip(live, 1.0, np.float32(width))
            bias_ref[rows, :] = jnp.where(live > 0.0, jnp.log(some), NEG)
            inv_ref[rows, :] = 1.0 / some


SKEW_F = 1
SKEW_B = 0
SKEW_P = 1
SKEW_E = 1
SKEW_M = 1


def interleave(chains, skew):
    live = dict(enumerate(chains))
    turn = 0
    while live:
        for j in sorted(live):
            if turn >= skew * j and next(live[j], live) is live:
                del live[j]
        turn += 1


def runs(touched, start, count):
    out = []
    for begin in range(start, start + count, 16):
        seen = begin in touched
        touched.add(begin)
        if out and out[-1][0] == seen:
            out[-1][2] += 16
        else:
            out.append([seen, begin, 16])
    return out


def window(ref, i, lanes):
    parts = []
    for start, count in window_parts(i):
        parts.append(ref[pl.ds(start, count), lanes])
    return jnp.concatenate(parts, axis=0)


def two_rows(block):
    first = lax.broadcasted_iota(jnp.int32, block.shape, 1) < 64
    zero = jnp.zeros_like(block)
    return jnp.concatenate([jnp.where(first, block, zero), jnp.where(first, zero, block)], axis=0)


def diagonal(block):
    n = block.shape[1] // 2
    return jnp.concatenate([block[:64, :n], block[64:, n:]], axis=0)


def four_rows(block):
    head = lax.broadcasted_iota(jnp.int32, block.shape, 1) // 64
    zero = jnp.zeros_like(block)
    return jnp.concatenate([jnp.where(head == j, block, zero) for j in range(4)], axis=0)


def corners(first, second):
    top = jnp.concatenate([first, jnp.zeros((first.shape[0], second.shape[1]), first.dtype)], axis=1)
    low = jnp.concatenate([jnp.zeros((second.shape[0], first.shape[1]), first.dtype), second], axis=1)
    return jnp.concatenate([top, low], axis=0)


def to_rows(level_one, others, index):
    row = lax.broadcasted_iota(jnp.int32, (8, TILE), 0)
    both = jnp.where(row == 0, jnp.broadcast_to(level_one, (8, TILE)), jnp.broadcast_to(others, (8, TILE)))
    return jnp.take_along_axis(both, index, axis=1)


def row_weights(weights, cell_rows):
    ones, rest = [], []
    for w in weights:
        wide = [jnp.broadcast_to(w[l : l + 1], (n, TILE)) for l, n in ((0, 64), (1, 32), (2, 16), (3, 8), (4, 8))]
        full = (jnp.concatenate(wide, axis=0) * cell_rows).astype(BF)
        ones.append(full[:64])
        rest.append(full[64:])
    return jnp.concatenate([corners(*ones), corners(*rest)], axis=0)


def keep_live(full, length, chunk, out_ref):
    row = lax.broadcasted_iota(jnp.int32, full.shape, 0) + 256 * chunk
    live = jnp.where(row < length, full, 0.0).astype(BF)
    out_ref[0, pl.ds(16 + 256 * chunk, 256), :] = live
    return live


def pack_cells(sums, chunk, out_ref, rough_ref, inv_ref):
    at = 0
    for level in range(1, LEVELS):
        count = 256 // 2**level
        pad = 0 if level == 5 else 16
        rows = pl.ds(BASE[level] + pad + count * chunk, count)
        cells = sums[at : at + count] * jnp.concatenate([inv_ref[rows, :]] * PAIRS, axis=1)
        if level == 5:
            rough_ref[pl.ds(8 * chunk, 8), :] = cells
        else:
            out_ref[0, rows, :] = cells.astype(BF)
        at += count


def forward_kernel(
    lens, x_ref, row_ref, w_ref, ends_ref,
    mask_ref, pool_q_ref, stat_ref, cell_rows_ref, pool_k_ref,
    n1_ref, q_ref, k_ref, v_ref, attn_ref, low_ref, lse_ref,
    bias_ref, inv_ref, rough_ref, tile_bias_ref,
):
    length = lens[pl.program_id(0)]
    count_tables(length, bias_ref, inv_ref)
    zeros = jnp.zeros((16, D), BF)
    for level in range(LEVELS - 1):
        cells = SLOT // 2**level
        for ref in (k_ref, v_ref):
            ref[0, pl.ds(BASE[level], 16), :] = zeros
            ref[0, pl.ds(BASE[level] + 16 + cells, 16), :] = zeros
    rough_k, rough_v = rough_ref.at[0], rough_ref.at[1]
    pre_gain, pre_shift = vector(row_ref, 0), vector(row_ref, 1)
    query_shift, value_shift = joined(ends_ref, 0, 2), joined(ends_ref, 2, 2)

    def project(chunk):
        rows = pl.ds(256 * chunk, 256)
        xhat, _ = norm_parts(x_ref[0, rows, :].astype(F32))
        n1 = (xhat * pre_gain + pre_shift).astype(BF)
        n1_ref[0, rows, :] = n1
        yield
        joint = [mm(n1, w_ref[t]) for t in range(2)]
        yield
        q, k, v = (jnp.concatenate([j[:, at : at + HALF] for j in joint], axis=1) for at in (0, HALF, 2 * HALF))
        q_ref[0, rows, :] = (q + query_shift).astype(BF) * BF(0.125)
        k = keep_live(k, length, chunk, k_ref)
        v = keep_live(v + value_shift, length, chunk, v_ref)
        yield
        k, v = mm(pool_k_ref[...], k), mm(pool_k_ref[...], v)
        yield
        pack_cells(k, chunk, k_ref, rough_k, inv_ref)
        pack_cells(v, chunk, v_ref, rough_v, inv_ref)
        yield

    interleave([project(chunk) for chunk in range(4)], SKEW_P)
    k_ref[0, pl.ds(BASE[5], 32), :] = rough_k[...].astype(BF)
    v_ref[0, pl.ds(BASE[5], 32), :] = rough_v[...].astype(BF)

    def tile(i, bias):
        rows = pl.ds(128 * i, 128)
        bias[...] = mask_ref[i] + window(bias_ref, i, slice(None))
        q = q_ref[0, rows, :]
        cells = mm(pool_q_ref[...], q).astype(BF)
        lse = {}

        def quad(u):
            lanes = slice(256 * u, 256 * u + 256)
            pairs = [slice(0, 128), slice(128, 256)]
            keys = window(k_ref.at[0], i, lanes)
            c_one, c_rest = four_rows(cells[:64, lanes]), four_rows(cells[64:, lanes])
            q_two = [two_rows(q[:, lanes][:, p]) for p in pairs]
            yield
            fine = [mm_nt(keys[:160, p], q_two[j]) for j, p in enumerate(pairs)]
            one, rest = mm_nt(keys[160:SPLIT], c_one), mm_nt(keys[SPLIT:], c_rest)
            yield
            one = [one[:, p] + bias[160:SPLIT] for p in pairs]
            rest = [rest[:, p] + bias[SPLIT:] for p in pairs]
            fine = [[f[:, p] + bias[:160] for p in pairs] for f in fine]
            top_one = [jnp.max(s, axis=0, keepdims=True) for s in one]
            top_rest = [jnp.max(s, axis=0, keepdims=True) for s in rest]
            top_fine = [[jnp.max(s, axis=0, keepdims=True) for s in f] for f in fine]
            yield
            one = [jnp.exp(s - top) for s, top in zip(one, top_one)]
            rest = [jnp.exp(s - top) for s, top in zip(rest, top_rest)]
            weights, shares, inverse = [], [], []
            row = lax.broadcasted_iota(jnp.int32, (8, TILE), 0)
            for j in range(2):
                sum_one = jnp.sum(one[j], axis=0, keepdims=True)
                sum_rest = jnp.sum(rest[j], axis=0, keepdims=True)
                pair_w, pair_p, pair_i = [], [], []
                for h in range(2):
                    tops = to_rows(top_one[j], top_rest[j], stat_ref[h])
                    sums = to_rows(sum_one, sum_rest, stat_ref[h])
                    top = jnp.maximum(top_fine[j][h], jnp.max(tops, axis=0, keepdims=True))
                    w = jnp.exp(tops - top).astype(BF).astype(F32)
                    p = jnp.exp(fine[j][h] - top)
                    total = jnp.sum(p, axis=0, keepdims=True)
                    total = total + jnp.sum(jnp.where(row < 5, w * sums, 0.0), axis=0, keepdims=True)
                    lse[4 * u + 2 * j + h] = top + jnp.log(total)
                    pair_w.append(w)
                    pair_p.append(p.astype(BF))
                    pair_i.append(1.0 / total)
                weights.append(row_weights(pair_w, cell_rows_ref[...]))
                shares.append(jnp.concatenate(pair_p, axis=1))
                inverse.append(jnp.concatenate(pair_i, axis=1))
            values = window(v_ref.at[0], i, lanes)
            v_fine = [values[:160, p].T for p in pairs]
            v_rough = [values[160:, p].T for p in pairs]
            yield
            mixed = [mm(v_rough[j], corners(one[j].astype(BF), rest[j].astype(BF))) for j in range(2)]
            out = [mm(v_fine[j], shares[j]) for j in range(2)]
            yield
            out = [out[j] + mm(mixed[j].astype(BF), weights[j]) for j in range(2)]
            yield
            for j in range(2):
                full = diagonal(out[j] * inverse[j]).T
                high = full.astype(BF)
                own = slice(256 * u + 128 * j, 256 * u + 128 * j + 128)
                attn_ref[0, rows, own] = high
                low_ref[0, rows, own] = (full - high.astype(F32)).astype(BF)
            if u == 1:
                lse_ref[0, :, rows] = jnp.concatenate([lse[h] for h in range(HEADS)], axis=0)
            yield

        return [quad(0), quad(1)]

    interleave([chain for i in range(TILES) for chain in tile(i, tile_bias_ref.at[i])], SKEW_F)


def middle_kernel(
    x_ref, attn_ref, cot_ref, w_ref, row_ref, ends_ref,
    out_ref, g1_ref, grad_ref, gvec_ref, gbup_ref,
    gwo_ref, gup_ref, gdown_ref,
):
    step = pl.program_id(0)

    @pl.when(step == 0)
    def _():
        gwo_ref[...] = jnp.zeros_like(gwo_ref)
        gup_ref[...] = jnp.zeros_like(gup_ref)
        gdown_ref[...] = jnp.zeros_like(gdown_ref)
        gvec_ref[...] = jnp.zeros_like(gvec_ref)
        gbup_ref[...] = jnp.zeros_like(gbup_ref)

    attn = attn_ref[...]
    cot = cot_ref[...]
    branch = sum(mm_nt(attn[:, HALF * t : HALF * t + HALF], w_ref[:, t, :, :HALF].reshape(D, HALF)) for t in range(2))
    y1 = x_ref[...].astype(F32) + (branch + vector(row_ref, 2))
    xhat, scale = norm_parts(y1)
    mid_gain = vector(row_ref, 3)
    n2 = (xhat * mid_gain + vector(row_ref, 4)).astype(BF)
    up_shift = joined(ends_ref, 4, 8)
    n2_t = n2.T
    cot_t = cot.T
    total = [y1 + vector(row_ref, 5), jnp.zeros_like(y1)]
    c = np.float32(np.sqrt(2.0 / np.pi))

    def hidden(part):
        cols = slice(512 * part, 512 * part + 512)
        at = HALF + 512 * (part % 2)
        up = w_ref[:, part // 2, :, at : at + 512].reshape(D, 512)
        at += FF // 2
        down_t = w_ref[:, part // 2, :, at : at + 512].reshape(D, 512)
        u = mm(n2, up) + up_shift[:, cols]
        dh = mm(cot, down_t)
        yield
        u2 = u * u
        t = jnp.tanh(u * (c + (c * 0.044715) * u2))
        h = 0.5 + 0.5 * t
        hid = (u * h).astype(BF)
        slope = h + 2.0 * h * (1.0 - h) * u * (c + (3.0 * c * 0.044715) * u2)
        dhp = dh * slope
        dhp_b = dhp.astype(BF)
        gbup_ref[:, cols] += column_sum(dhp)
        yield
        total[0] = total[0] + mm_nt(hid, down_t)
        total[1] = total[1] + mm_nt(dhp_b, up)
        gdown_ref[:, cols] += mm(cot_t, hid)
        gup_ref[:, cols] += mm(n2_t, dhp_b)
        yield

    interleave([hidden(part) for part in range(4)], SKEW_M)
    out, dn2 = total
    out_ref[...] = out.astype(BF)
    cot_f = cot.astype(F32)
    dy1 = cot_f + norm_back(dn2, xhat, scale, mid_gain)
    g1 = dy1.astype(BF)
    g1_ref[...] = g1
    gwo_ref[...] += mm(g1.T, attn)
    gvec_ref[...] += jnp.concatenate(
        [column_sum(g1.astype(F32)), column_sum(dn2 * xhat), column_sum(dn2), column_sum(cot_f), jnp.zeros((4, D), F32)],
        axis=0,
    )


    @pl.when(step == pl.num_programs(0) - 1)
    def _():
        rows = D // grad_ref.shape[0]
        for t in range(2):
            at = 0
            for ref, width in ((gwo_ref, HALF), (gup_ref, FF // 2), (gdown_ref, FF // 2)):
                part = ref[:, width * t : width * t + width].astype(BF)
                grad_ref[:, t, :, at : at + width] = part.reshape(grad_ref.shape[0], rows, width)
                at += width


def backward_kernel(
    lens, x_ref, n1_ref, q_ref, k_ref, v_ref, attn_ref, low_ref, lse_ref, g1_ref,
    row_ref, w_ref, wo_t_ref,
    mask_ref, pool_q_ref, stat_ref, cell_rows_ref, expand_ref, spread_k_ref,
    dx_ref, gqkv_ref, gvec_ref,
    bias_ref, inv_ref, tile_bias_ref, dk_ref, dv_ref, dqkv_ref,
):
    step = pl.program_id(0)

    @pl.when(step == 0)
    def _():
        gqkv_ref[...] = jnp.zeros_like(gqkv_ref)
        gvec_ref[...] = jnp.zeros_like(gvec_ref)

    length = lens[step]
    count_tables(length, bias_ref, inv_ref)
    touched = (set(), set())
    head_of = lax.broadcasted_iota(jnp.int32, (HEADS, D), 1) // HD
    heads = (head_of == lax.broadcasted_iota(jnp.int32, (HEADS, D), 0)).astype(BF)

    def tile(i, bias):
        rows = pl.ds(128 * i, 128)
        bias[...] = mask_ref[i] + window(bias_ref, i, slice(None))
        q = q_ref[0, rows, :]
        cells = mm(pool_q_ref[...], q).astype(BF)
        da = jnp.concatenate([mm(g1_ref[0, rows, :], wo_t_ref[:, t, :, :HALF].reshape(D, HALF)) for t in range(2)], axis=1)
        da = da.astype(BF)
        product = da.astype(F32) * (attn_ref[0, rows, :].astype(F32) + low_ref[0, rows, :].astype(F32))
        high = product.astype(BF)
        delta = mm_nt(heads, high) + mm_nt(heads, (product - high.astype(F32)).astype(BF))
        lse = lse_ref[0, :, rows]

        def quad(u):
            lanes = slice(256 * u, 256 * u + 256)
            pairs = [slice(0, 128), slice(128, 256)]
            keys = window(k_ref.at[0], i, lanes)
            values = window(v_ref.at[0], i, lanes)
            c_one, c_rest = four_rows(cells[:64, lanes]), four_rows(cells[64:, lanes])
            q_two = [two_rows(q[:, lanes][:, p]) for p in pairs]
            d_two = [two_rows(da[:, lanes][:, p]) for p in pairs]
            yield
            fine = [mm_nt(keys[:160, p], q_two[j]) for j, p in enumerate(pairs)]
            one, rest = mm_nt(keys[160:SPLIT], c_one), mm_nt(keys[SPLIT:], c_rest)
            dp = [mm_nt(values[:160, p], d_two[j]) for j, p in enumerate(pairs)]
            yield
            ones, rests, weights, shares, slopes, rows_delta = [], [], [], [], [], []
            for j, pair in enumerate(pairs):
                s_one, s_rest = one[:, pair] + bias[160:SPLIT], rest[:, pair] + bias[SPLIT:]
                top_one, top_rest = jnp.max(s_one, axis=0, keepdims=True), jnp.max(s_rest, axis=0, keepdims=True)
                ones.append(jnp.exp(s_one - top_one))
                rests.append(jnp.exp(s_rest - top_rest))
                pair_w, pair_p, pair_s = [], [], []
                for h, p in enumerate(pairs):
                    head = 4 * u + 2 * j + h
                    own_lse, own_delta = lse[head : head + 1], delta[head : head + 1]
                    pair_w.append(jnp.exp(to_rows(top_one, top_rest, stat_ref[h]) - own_lse))
                    share = jnp.exp(fine[j][:, p] + bias[:160] - own_lse)
                    pair_s.append((share * (dp[j][:, p] - own_delta)).astype(BF))
                    pair_p.append(share.astype(BF))
                weights.append(row_weights(pair_w, cell_rows_ref[...]))
                shares.append(jnp.concatenate(pair_p, axis=1))
                slopes.append(jnp.concatenate(pair_s, axis=1))
                head = 4 * u + 2 * j
                both = jnp.concatenate([delta[head : head + 1], delta[head + 1 : head + 2]], axis=1)
                top = both.astype(BF).astype(F32)
                rows_delta.append(jnp.concatenate([top, both - top, jnp.zeros((6, 256), F32)], axis=0).astype(BF))
            k_fine = [keys[:160, p].T for p in pairs]
            k_rough = [keys[160:, p].T for p in pairs]
            yield
            d_cells = [mm(weights[j], d_two[j]).astype(BF) for j in range(2)]
            delta_cells = [jnp.sum(mm_nt(rows_delta[j], weights[j]), axis=0, keepdims=True) for j in range(2)]
            dv_fine = [mm(shares[j], d_two[j]) for j in range(2)]
            yield
            d_one, d_rest = (corners(d_cells[0][a : a + 128], d_cells[1][a : a + 128]) for a in (0, 128))
            dp_one, dp_rest = mm_nt(values[160:SPLIT], d_one), mm_nt(values[SPLIT:], d_rest)
            dk_fine = [mm(slopes[j], q_two[j]) for j in range(2)]
            dq = [mm(k_fine[j], slopes[j]) for j in range(2)]
            yield
            s_one = [(ones[j] * (dp_one[:, p] - delta_cells[j][:, :128])).astype(BF) for j, p in enumerate(pairs)]
            s_rest = [(rests[j] * (dp_rest[:, p] - delta_cells[j][:, 128:])).astype(BF) for j, p in enumerate(pairs)]
            dv_one = mm(jnp.concatenate([e.astype(BF) for e in ones], axis=1), d_one)
            dv_rest = mm(jnp.concatenate([e.astype(BF) for e in rests], axis=1), d_rest)
            yield
            dq_cells = [mm(k_rough[j], corners(s_one[j], s_rest[j])).astype(BF) for j in range(2)]
            dk_one = mm(jnp.concatenate(s_one, axis=1), c_one)
            dk_rest = mm(jnp.concatenate(s_rest, axis=1), c_rest)
            yield
            dq = [diagonal(dq[j] + mm(dq_cells[j], expand_ref[...])) * 0.125 for j in range(2)]
            dk = jnp.concatenate([jnp.concatenate(dk_fine, axis=1), dk_one, dk_rest], axis=0)
            dv = jnp.concatenate([jnp.concatenate(dv_fine, axis=1), dv_one, dv_rest], axis=0)
            at = 0
            for start, count in window_parts(i):
                for seen, begin, n in runs(touched[u], start, count):
                    part = pl.ds(begin, n)
                    for ref, grad in ((dk_ref, dk), (dv_ref, dv)):
                        block = grad[at + begin - start : at + begin - start + n]
                        ref[part, lanes] = ref[part, lanes] + block if seen else block
                at += count
            yield
            for j in range(2):
                at = 3 * HALF * u + 128 * j
                dqkv_ref[rows, at : at + 128] = dq[j].T.astype(BF)
            yield

        return [quad(0), quad(1)]

    interleave([chain for i in range(TILES) for chain in tile(i, tile_bias_ref.at[i])], SKEW_B)

    sums = []
    pre_gain = vector(row_ref, 0)

    def finish(chunk):
        rows = pl.ds(256 * chunk, 256)
        own = pl.ds(16 + 256 * chunk, 256)
        live = lax.broadcasted_iota(jnp.int32, (256, D), 0) + 256 * chunk < length
        wide = []
        for ref in (dk_ref, dv_ref):
            cells = []
            for level in range(1, LEVELS):
                count = 256 // 2**level
                pad = 0 if level == 5 else 16
                part = pl.ds(BASE[level] + pad + count * chunk, count)
                cells.append(ref[part, :] * jnp.concatenate([inv_ref[part, :]] * PAIRS, axis=1))
            cells.append(jnp.zeros((8, D), F32))
            wide.append(jnp.concatenate(cells, axis=0).astype(BF))
        yield
        wide = [mm(spread_k_ref[...], w) for w in wide]
        yield
        for ref, at, w in zip((dk_ref, dv_ref), (HALF, 2 * HALF), wide):
            grad = jnp.where(live, ref[own, :] + w, 0.0).astype(BF)
            dqkv_ref[rows, at : at + HALF] = grad[:, :HALF]
            dqkv_ref[rows, at + 3 * HALF : at + 4 * HALF] = grad[:, HALF:]
        yield
        parts = [dqkv_ref[rows, 3 * HALF * t : 3 * HALF * t + 3 * HALF] for t in range(2)]
        dn1 = mm_nt(parts[0], w_ref[0]) + mm_nt(parts[1], w_ref[1])
        xhat, scale = norm_parts(x_ref[0, rows, :].astype(F32))
        yield
        dx = g1_ref[0, rows, :].astype(F32) + norm_back(dn1, xhat, scale, pre_gain)
        dx_ref[0, rows, :] = dx.astype(BF)
        col = [column_sum(part.astype(F32)) for part in parts]
        sums.append(
            jnp.concatenate(
                [
                    column_sum(dn1 * xhat), column_sum(dn1),
                    jnp.concatenate([c[:, :HALF] for c in col], axis=1),
                    jnp.concatenate([c[:, 2 * HALF :] for c in col], axis=1),
                    jnp.zeros((4, D), F32),
                ],
                axis=0,
            )
        )
        yield

    interleave([finish(chunk) for chunk in range(4)], SKEW_E)
    gvec_ref[...] += sums[0] + sums[1] + sums[2] + sums[3]
    n1_t = n1_ref[0].T
    for t in range(2):
        gqkv_ref[t] += mm(n1_t, dqkv_ref[:, 3 * HALF * t : 3 * HALF * t + 3 * HALF])


def whole(shape):
    return pl.BlockSpec(shape, lambda *_: (0,) * len(shape))


def per_sequence(*shape):
    return pl.BlockSpec((1,) + shape, lambda s, *_: (s,) + (0,) * len(shape))


LIMIT = 60 * 1024 * 1024


def attention_forward(x, lens, row, w, ends, const):
    count = x.shape[0]
    return pl.pallas_call(
        forward_kernel,
        grid_spec=pltpu.PrefetchScalarGridSpec(
            num_scalar_prefetch=1,
            grid=(count,),
            in_specs=[
                per_sequence(SLOT, D), whole((SMALL, 128)), whole((2, D, 3 * HALF)), whole((2, 16, 128)),
                whole((TILES, WIN, TILE)), whole((TILE, TILE)), whole((2, 8, TILE)), whole((TILE, TILE)), whole((256, 256)),
            ],
            out_specs=[
                per_sequence(SLOT, D), per_sequence(SLOT, D), per_sequence(CELL_ROWS, D), per_sequence(CELL_ROWS, D),
                per_sequence(SLOT, D), per_sequence(SLOT, D), per_sequence(HEADS, SLOT),
            ],
            scratch_shapes=[
                pltpu.VMEM((CELL_ROWS, 128), F32), pltpu.VMEM((CELL_ROWS, 128), F32), pltpu.VMEM((2, 32, D), F32),
                pltpu.VMEM((TILES, WIN, TILE), F32),
            ],
        ),
        out_shape=[
            jax.ShapeDtypeStruct((count, SLOT, D), BF), jax.ShapeDtypeStruct((count, SLOT, D), BF),
            jax.ShapeDtypeStruct((count, CELL_ROWS, D), BF), jax.ShapeDtypeStruct((count, CELL_ROWS, D), BF),
            jax.ShapeDtypeStruct((count, SLOT, D), BF), jax.ShapeDtypeStruct((count, SLOT, D), BF),
            jax.ShapeDtypeStruct((count, HEADS, SLOT), F32),
        ],
        compiler_params=pltpu.CompilerParams(vmem_limit_bytes=LIMIT),
        cost_estimate=pl.CostEstimate(flops=count * 30 * 10**9, bytes_accessed=count * 10**7, transcendentals=0),
        name="attention_forward",
    )(lens, x, row, w, ends, const["mask"], const["pool_q"], const["stat"], const["cell_rows"], const["pool_k"])


ROWS = 512


def middle(x, attn, cot, w, row, ends):
    total = x.shape[0]
    rows = pl.BlockSpec((ROWS, D), lambda s: (s, 0))
    return pl.pallas_call(
        middle_kernel,
        grid=(total // ROWS,),
        in_specs=[
            rows, rows, rows, whole(w.shape), whole((SMALL, 128)), whole((2, 16, 128)),
        ],
        out_specs=[rows, rows, whole(w.shape), whole((8, D)), whole((1, FF))],
        scratch_shapes=[pltpu.VMEM((D, D), F32), pltpu.VMEM((D, FF), F32), pltpu.VMEM((D, FF), F32)],
        out_shape=[
            jax.ShapeDtypeStruct((total, D), BF), jax.ShapeDtypeStruct((total, D), BF), jax.ShapeDtypeStruct(w.shape, BF),
            jax.ShapeDtypeStruct((8, D), F32), jax.ShapeDtypeStruct((1, FF), F32),
        ],
        compiler_params=pltpu.CompilerParams(vmem_limit_bytes=LIMIT),
        name="middle",
    )(x, attn, cot, w, row, ends)


def attention_backward(x, lens, n1, q, k, v, attn, low, lse, g1, row, w, rest, const):
    count = x.shape[0]
    wo_t = pl.BlockSpec(rest.shape[:3] + (HALF,), lambda *_: (0, 0, 0, 0))
    return pl.pallas_call(
        backward_kernel,
        grid_spec=pltpu.PrefetchScalarGridSpec(
            num_scalar_prefetch=1,
            grid=(count,),
            in_specs=[
                per_sequence(SLOT, D), per_sequence(SLOT, D), per_sequence(SLOT, D),
                per_sequence(CELL_ROWS, D), per_sequence(CELL_ROWS, D), per_sequence(SLOT, D), per_sequence(SLOT, D),
                per_sequence(HEADS, SLOT), per_sequence(SLOT, D),
                whole((SMALL, 128)), whole((2, D, 3 * HALF)), wo_t,
                whole((TILES, WIN, TILE)), whole((TILE, TILE)), whole((2, 8, TILE)), whole((TILE, TILE)),
                whole((256, 256)), whole((256, 256)),
            ],
            out_specs=[per_sequence(SLOT, D), whole((2, D, 3 * HALF)), whole((8, D))],
            scratch_shapes=[
                pltpu.VMEM((CELL_ROWS, 128), F32), pltpu.VMEM((CELL_ROWS, 128), F32), pltpu.VMEM((TILES, WIN, TILE), F32),
                pltpu.VMEM((CELL_ROWS, D), F32), pltpu.VMEM((CELL_ROWS, D), F32), pltpu.VMEM((SLOT, 3 * D), BF),
            ],
        ),
        out_shape=[
            jax.ShapeDtypeStruct((count, SLOT, D), BF), jax.ShapeDtypeStruct((2, D, 3 * HALF), F32),
            jax.ShapeDtypeStruct((8, D), F32),
        ],
        compiler_params=pltpu.CompilerParams(vmem_limit_bytes=LIMIT),
        cost_estimate=pl.CostEstimate(flops=count * 40 * 10**9, bytes_accessed=count * 10**7, transcendentals=0),
        name="attention_backward",
    )(
        lens, x, n1, q, k, v, attn, low, lse, g1, row, w, rest,
        const["mask"], const["pool_q"], const["stat"], const["cell_rows"], const["expand"], const["spread_k"],
    )


def bits_of(count):
    return count.bit_length() - 1


def all_bits(n_dp, n_t):
    return [("tensor", b) for b in reversed(range(bits_of(n_t)))] + [("dp", b) for b in reversed(range(bits_of(n_dp)))]


def gather_orders(n_dp, n_t):
    far = [("dp", b) for b in reversed(range(2, bits_of(n_dp)))]
    near = [("dp", 1)]
    side = [("tensor", b) for b in reversed(range(bits_of(n_t)))]
    core_bit = [("dp", 0)]
    return far + near + side + core_bit, far + side + near + core_bit


def own_bit(bit):
    axis, b = bit
    return (lax.axis_index(axis) // 2**b) % 2


def partner(bit):
    axis, b = bit
    return {axis: lax.axis_index(axis) + (1 - 2 * own_bit(bit)) * 2**b}


def meet(bits):
    barrier = pltpu.get_barrier_semaphore()
    for bit in bits:
        pl.semaphore_signal(barrier, inc=1, device_id=partner(bit), device_id_type=pl.DeviceIdType.MESH)
    pl.semaphore_wait(barrier, len(bits))


def halves(width):
    if width % 256:
        return [(0, width)]
    return [(0, width // 2), (width // 2, width // 2)]


def gather_kernel(
    bits, orders, parts, *refs
):
    *shard_refs, ends_ref, out_ref, all_ends_ref, own_sems, send_sems, recv_sems, ends_own_sem, ends_sems = refs
    slot = out_ref.at[tuple(own_bit(bit) for bit in bits)]
    width = shard_refs[0].shape[1]
    own = [
        pltpu.make_async_copy(ref, slot.at[:, pl.ds(width * j, width)], own_sems.at[j]) for j, ref in enumerate(shard_refs)
    ]
    for copy in own:
        copy.start()
    side = [bit for bit in bits if bit[0] == "tensor"]
    own_ends = pltpu.make_async_copy(ends_ref.at[pl.ds(0, 16)], all_ends_ref.at[tuple(own_bit(bit) for bit in side)], ends_own_sem)
    own_ends.start()
    meet(bits)
    pending = []
    own_ends.wait()
    for copy in own:
        copy.wait()

    def ends_copy(step):
        place = all_ends_ref.at[tuple(slice(None) if j < step else own_bit(bit) for j, bit in enumerate(side))]
        return pltpu.make_async_remote_copy(
            src_ref=place, dst_ref=place, send_sem=ends_sems.at[0, step], recv_sem=ends_sems.at[1, step],
            device_id=partner(side[step]), device_id_type=pl.DeviceIdType.MESH,
        )

    if side:
        ends_copy(0).start()
    for step in range(len(bits)):
        for part, (at, width) in enumerate(parts):
            order = orders[part]
            done = order[:step]
            index = tuple(slice(None) if bit in done else own_bit(bit) for bit in bits)
            place = out_ref.at[index + (slice(None), pl.ds(at, width))]
            if step > 0:
                pending[(step - 1) * len(parts) + part].wait_recv()
            copy = pltpu.make_async_remote_copy(
                src_ref=place, dst_ref=place,
                send_sem=send_sems.at[step, part], recv_sem=recv_sems.at[step, part],
                device_id=partner(order[step]), device_id_type=pl.DeviceIdType.MESH,
            )
            copy.start()
            pending.append(copy)
    for copy in pending[-len(parts) :]:
        copy.wait_recv()
    for step in range(len(side)):
        ends_copy(step).wait_recv()
        if step + 1 < len(side):
            ends_copy(step + 1).start()
    for step in range(len(side)):
        ends_copy(step).wait_send()
    for copy in pending:
        copy.wait_send()


def gather(shards, ends, n_dp, n_t):
    rows, width = shards[0].shape[0], len(shards) * shards[0].shape[1]
    bits, orders, parts = all_bits(n_dp, n_t), gather_orders(n_dp, n_t), halves(width)
    side = bits_of(n_t)
    anywhere = pl.BlockSpec(memory_space=pl.ANY)
    out, all_ends = pl.pallas_call(
        functools.partial(gather_kernel, bits, orders, parts),
        in_specs=[anywhere] * (len(shards) + 1),
        out_specs=[anywhere, anywhere],
        out_shape=[
            jax.ShapeDtypeStruct((2,) * len(bits) + (rows, width), BF),
            jax.ShapeDtypeStruct((2,) * side + (16, 128), BF),
        ],
        scratch_shapes=[
            pltpu.SemaphoreType.DMA((len(shards),)), pltpu.SemaphoreType.DMA((len(bits), len(parts))),
            pltpu.SemaphoreType.DMA((len(bits), len(parts))), pltpu.SemaphoreType.DMA,
            pltpu.SemaphoreType.DMA((2, max(side, 1))),
        ],
        compiler_params=pltpu.CompilerParams(collective_id=0, has_side_effects=True),
        name="gather",
    )(*shards, ends)
    return out.reshape(n_t, n_dp, rows, width), all_ends.reshape(n_t, 16, 128)


def reduce_kernel(bits, orders, parts, n_t, grad_ref, pre_ref, mid_ref, up_ref, out_ref, own_ref, *scratch):
    steps, count = len(bits), len(parts)
    sends, recvs, sums = (scratch[j * steps * count : (j + 1) * steps * count] for j in range(3))
    vec_out_ref, vec_recv, send_sems, recv_sems, vec_send_sems, vec_recv_sems = scratch[3 * steps * count :]
    meet(bits)
    vec_out_ref[0:4, :] = pre_ref[0:4, :]
    vec_out_ref[4:8, :] = mid_ref[0:4, :]
    for r in range(4):
        vec_out_ref[8 + r : 9 + r, :] = up_ref[:, D * r : D * r + D]
    vec_out_ref[12:16, :] = jnp.zeros((4, D), F32)

    def vec_copy(step):
        return pltpu.make_async_remote_copy(
            src_ref=vec_recv.at[2 * step], dst_ref=vec_recv.at[2 * step + 1],
            send_sem=vec_send_sems.at[step], recv_sem=vec_recv_sems.at[step],
            device_id=partner(orders[0][steps - 1 - step]), device_id_type=pl.DeviceIdType.MESH,
        )

    def copy_of(step, part):
        j = step * count + part
        return pltpu.make_async_remote_copy(
            src_ref=sends[j], dst_ref=recvs[j], send_sem=send_sems.at[step, part], recv_sem=recv_sems.at[step, part],
            device_id=partner(orders[part][steps - 1 - step]), device_id_type=pl.DeviceIdType.MESH,
        )

    def pieces(step, part):
        order = orders[part][::-1]
        left = [bit for bit in bits if bit not in order[:step]]
        j = left.index(order[step])
        low = 2 ** (len(left) - 1 - j)
        mine = own_bit(order[step])
        out = []
        for a in range(2**j):
            for c in range(low):
                out.append(((a * 2 + 1 - mine) * low + c, (a * 2 + mine) * low + c, a * low + c))
        at, width = parts[part]
        source = sums[(step - 1) * count + part] if step else grad_ref.at[:, :, pl.ds(at, width)]
        return out, source

    for step in range(steps):
        vec_recv[2 * step] = vec_out_ref[...]
        vec_copy(step).start()
        for part in range(count):
            blocks, source = pieces(step, part)
            for away, _, to in blocks:
                sends[step * count + part][to] = source[away].astype(BF)
            copy_of(step, part).start()
        for part in range(count):
            copy_of(step, part).wait_recv()
            blocks, source = pieces(step, part)
            for _, keep, to in blocks:
                total = source[keep] + recvs[step * count + part][to].astype(F32)
                if step == steps - 1:
                    at, width = parts[part]
                    out_ref[:, at : at + width] = total
                else:
                    sums[step * count + part][to] = total
        vec_copy(step).wait_recv()
        vec_out_ref[...] += vec_recv[2 * step + 1]
    own_ref[0:8, :] = vec_out_ref[0:8, :]
    t = lax.axis_index("tensor")
    for row in (2, 3):
        n = D // n_t
        full = vec_out_ref[row : row + 1, :]
        mine = full[:, :n]
        for j in range(1, n_t):
            mine = jnp.where(t == j, full[:, n * j : n * j + n], mine)
        own_ref[row : row + 1, 0:n] = mine
    n = FF // n_t
    full = jnp.concatenate([vec_out_ref[8 + r : 9 + r, :] for r in range(4)], axis=1)
    mine = full[:, :n]
    for j in range(1, n_t):
        mine = jnp.where(t == j, full[:, n * j : n * j + n], mine)
    piece = min(n, D)
    own_ref[8:16, :] = jnp.zeros((8, D), F32)
    for r in range(n // piece):
        own_ref[8 + r : 9 + r, 0:piece] = mine[:, piece * r : piece * r + piece]
    for step in range(steps):
        vec_copy(step).wait_send()
        for part in range(count):
            copy_of(step, part).wait_send()


def reduce(grad, pre, mid, up, n_dp, n_t):
    rows, width = grad.shape[2:]
    bits, orders, parts = all_bits(n_dp, n_t), gather_orders(n_dp, n_t), halves(width)
    steps = len(bits)
    blocks = [(2 ** (steps - 1 - step), rows, w) for step in range(steps) for _, w in parts]
    sems = pltpu.SemaphoreType.DMA
    vmem = pl.BlockSpec(memory_space=pltpu.VMEM)
    return pl.pallas_call(
        functools.partial(reduce_kernel, bits, orders, parts, n_t),
        in_specs=[vmem] * 4,
        out_specs=[vmem, vmem],
        out_shape=[jax.ShapeDtypeStruct((rows, width), F32), jax.ShapeDtypeStruct((16, D), F32)],
        scratch_shapes=[pltpu.VMEM(b, BF) for b in blocks] * 2
        + [pltpu.VMEM(b, F32) for b in blocks]
        + [
            pltpu.VMEM((16, D), F32), pltpu.VMEM((2 * steps, 16, D), F32), sems((steps, len(parts))), sems((steps, len(parts))),
            sems((steps,)), sems((steps,)),
        ],
        compiler_params=pltpu.CompilerParams(collective_id=1, has_side_effects=True, vmem_limit_bytes=LIMIT),
        name="reduce",
    )(grad.reshape(n_t * n_dp, rows, width), pre, mid, up)


def to_pairs(grid, widths):
    n_t, n_dp, rows, _ = grid.shape
    grid = grid.reshape(n_t, n_dp * rows, -1)
    if n_t == 2:
        return grid
    out, at = [], 0
    for width in widths:
        part = grid[:, :, at : at + width].reshape(2, n_t // 2, D, width)
        out.append(part.transpose(0, 2, 1, 3).reshape(2, D, n_t // 2 * width))
        at += width
    return jnp.concatenate(out, axis=2)


def from_pairs(grid, widths, n_dp, n_t):
    if n_t != 2:
        out, at = [], 0
        for width in widths:
            full = width * n_t // 2
            part = grid[:, :, at : at + full].reshape(2, D, n_t // 2, width)
            out.append(part.transpose(0, 2, 1, 3).reshape(n_t, D, width))
            at += full
        grid = jnp.concatenate(out, axis=2)
    return grid.reshape(n_t, n_dp, D // n_dp, -1)


def own_sequences(values, lengths, tensor_count):
    micro, rows, width = values[0].shape
    t = lax.axis_index("tensor")
    if rows % SLOT == 0:
        per = rows // SLOT
        own = lax.dynamic_slice_in_dim(lengths, t * per, per, 1).reshape(-1)
        return [v.reshape(micro * per, SLOT, width) for v in values], own
    pieces = SLOT // rows
    assert micro == pieces
    groups = [[g * pieces + j for j in range(pieces)] for g in range(tensor_count // pieces)]
    out = [lax.all_to_all(v, "tensor", 0, 1, axis_index_groups=groups, tiled=True) for v in values]
    sequence = lax.dynamic_slice(lengths, (t % pieces, t // pieces), (1, 1))
    return out, sequence.reshape(-1)


def own_rows(values, shape, tensor_count):
    micro, rows, width = shape
    if rows % SLOT == 0:
        return [v.reshape(shape) for v in values]
    pieces = SLOT // rows
    groups = [[g * pieces + j for j in range(pieces)] for g in range(tensor_count // pieces)]
    return [
        lax.all_to_all(v, "tensor", 1, 0, axis_index_groups=groups, tiled=True).reshape(shape) for v in values
    ]


def core(x, lens, cot, row, w, ends, rest):
    const = {name: jnp.asarray(value) for name, value in constants().items()}
    count = x.shape[0]
    flat = (count * SLOT, D)
    n1, q, k, v, attn, low, lse = attention_forward(x, lens, row, w, ends, const)
    out, g1, grad_rest, mid_vec, gbup = middle(
        x.reshape(flat), attn.reshape(flat), cot.reshape(flat), rest, row, ends
    )
    dx, gqkv, pre_vec = attention_backward(
        x, lens, n1, q, k, v, attn, low, lse, g1.reshape(count, SLOT, D), row, w, rest, const
    )
    return out, dx, grad_rest, mid_vec, gbup, gqkv, pre_vec


def on_device(
    inputs, lengths, pre_gain, pre_shift, query_weight, key_weight, value_weight, query_bias, value_bias,
    output_weight, output_bias, mid_gain, mid_shift, up_weight, up_bias, down_weight, down_bias, cotangent,
):
    n_dp, n_t = lax.axis_size("dp"), lax.axis_size("tensor")
    t = lax.axis_index("tensor")
    (x, cot), lens = own_sequences([inputs, cotangent], lengths, n_t)

    n_q, n_f = query_weight.shape[1], up_weight.shape[1]
    second = jnp.concatenate([output_weight.T, up_weight, down_weight.T], axis=1)
    small = ((query_bias, 0), (value_bias, n_q), (up_bias, 2 * n_q))
    vectors = (pre_gain, pre_shift, output_bias, mid_gain, mid_shift, down_bias)
    small += tuple((v, 2048 + D * j) for j, v in enumerate(vectors))
    row = sum(lax.pad(v, jnp.zeros((), BF), [(at, SMALL * 128 - at - v.shape[0], 0)]) for v, at in small)
    row = row.reshape(SMALL, 128)
    first = (query_weight, key_weight, value_weight)
    if n_q % 128:
        first = (jnp.concatenate(first, axis=1),)
    w, ends = gather(first, row, n_dp, n_t)
    w = to_pairs(w, (n_q,) * 3)
    rest = lax.all_gather(second, ("dp", "tensor"), axis=0, tiled=False)
    rest = rest.reshape(n_dp, n_t, D // n_dp, -1)
    if n_t != 2:
        rest = to_pairs(rest.transpose(1, 0, 2, 3), (n_q, n_f, n_f)).reshape(2, 16, 32, REST).transpose(1, 0, 2, 3)
        flat = ends.reshape(n_t, -1)
        parts = [flat[:, a : a + n].reshape(2, -1) for a, n in ((0, n_q), (n_q, n_q), (2 * n_q, n_f))]
        ends = jnp.concatenate(parts + [jnp.zeros((2, 512), ends.dtype)], axis=1).reshape(2, 16, 128)
    out, dx, grad_rest, mid_vec, gbup, gqkv, pre_vec = core(x, lens, cot, row, w, ends, rest)
    if n_t != 2:
        grad_rest = grad_rest.transpose(1, 0, 2, 3).reshape(2, D, REST)
        grad_rest = from_pairs(grad_rest, (n_q, n_f, n_f), n_dp, n_t).transpose(1, 0, 2, 3)
    grad_rest = grad_rest.reshape(n_dp * n_t, D // n_dp, -1)
    grad_rest = lax.psum_scatter(grad_rest, ("dp", "tensor"), scatter_dimension=0, tiled=False).astype(F32)
    grad_first, vec = reduce(from_pairs(gqkv, (n_q,) * 3, n_dp, n_t), pre_vec, mid_vec, gbup, n_dp, n_t)
    grad_q, grad_k, grad_v = (grad_first[:, n_q * j : n_q * j + n_q] for j in range(3))
    grad_o, grad_up, grad_down = grad_rest[:, :n_q].T, grad_rest[:, n_q : n_q + n_f], grad_rest[:, n_q + n_f :].T

    out, dx = own_rows([out.reshape(x.shape), dx], inputs.shape, n_t)
    return (
        out, dx, vec[0], vec[1], grad_q, grad_k, grad_v, vec[2, :n_q], vec[3, :n_q], grad_o, vec[4], vec[5], vec[6],
        grad_up, vec[8:].reshape(-1)[:n_f], grad_down, vec[7],
    )


def solution(mesh):
    rows = P(None, ("dp", "tensor"), None)
    by_row, by_column = P("dp", "tensor"), P("tensor", "dp")
    in_specs = (
        rows, P(None, "dp"), P(), P(), by_row, by_row, by_row, P("tensor"), P("tensor"), by_column, P(), P(), P(),
        by_row, P("tensor"), by_column, P(), rows,
    )
    out_specs = (
        rows, rows, P(), P(), by_row, by_row, by_row, P("tensor"), P("tensor"), by_column, P(), P(), P(),
        by_row, P("tensor"), by_column, P(),
    )
    return jax.shard_map(on_device, mesh=mesh, in_specs=in_specs, out_specs=out_specs, check_vma=False)
```

```python
import functools

import jax
import jax.numpy as jnp
import ml_dtypes
import numpy as np
from jax import lax
from jax.experimental import pallas as pl
from jax.experimental.pallas import tpu as pltpu
from jax.sharding import PartitionSpec as P

D = 512
HD = 64
FF = 2048
NR = 16
LEVELS = 6
SLOT = 1024
TILE = 128
TILES = SLOT // TILE
PAIRS = D // 128
HEADS = D // HD
HALF = D // 2
REST = HALF + FF
SMALL = 40
EPS = 1e-05
NEG = -1e30

BASE = (0, 1056, 1600, 1888, 2048, 2144)
CELL_ROWS = 2176
WIN_ROWS = (160, 96, 64, 32, 32, 16)
WIN_AT = (0, 160, 256, 320, 352, 384)
WIN = 400
COARSE = WIN - 160
LANE_AT = (0, 0, 0, 32, 48, 56)
SPLIT = WIN_AT[2]
BF = jnp.bfloat16
F32 = jnp.float32


def window_parts(i):
    two, four = i // 2, i // 4
    return (
        (128 * i, 160),
        (BASE[1] + 64 * i, 96),
        (BASE[2] + 32 * i, 64),
        (BASE[3] + 16 * i, 16),
        (BASE[3] + 16 * i + 32, 16),
        (BASE[4] + 16 * two, 16),
        (BASE[4] + 16 * two + 32, 16),
        (BASE[5] + 16 * (1 - four), 16),
    )


def mask_table():
    table = np.full((TILES, WIN, TILE), NEG, np.float32)
    for i in range(TILES):
        at = 0
        for start, count in window_parts(i):
            level = max(l for l in range(LEVELS) if WIN_AT[l] <= at)
            pad = 0 if level == 5 else 16
            cell = (start - BASE[level] - pad + np.arange(count))[:, None]
            here = TILE >> level
            query = (((128 * i) >> level) + np.arange(here))[None, :]
            good = np.abs(cell // 16 - query // 16) <= 1
            if level > 0:
                good &= np.abs((2 * cell) // 16 - (2 * query) // 16) > 1
            for head in range(1 if level == 0 else 2):
                lane = 64 * head + LANE_AT[level]
                table[i, at : at + count, lane : lane + here] = np.where(good, 0.0, NEG)
            at += count
    return table


def constants():
    t = np.arange(TILE)
    pool_q = np.zeros((TILE, TILE), np.float32)
    stat = np.zeros((2, 8, TILE), np.int32)
    expand = np.zeros((256, 256), np.float32)
    pool_k = np.zeros((256, 256), np.float32)
    t2 = np.arange(256)
    at = 0
    for level in range(1, LEVELS):
        width = 2**level
        half = 0 if level == 1 else 64
        pool_q[half + LANE_AT[level] + t // width, t] = 1.0 / width
        for head in range(2):
            stat[head, level - 1 :] = 64 * head + LANE_AT[level] + t // width
            expand[2 * half + 64 * head + LANE_AT[level] + t // width, 128 * head + t] = 1.0 / width
        pool_k[at + t2 // width, t2] = 1.0
        at += 256 // width
    half = ml_dtypes.bfloat16
    return {
        "mask": mask_table(),
        "pool_q": pool_q.astype(half),
        "stat": stat,
        "cell_rows": (pool_q > 0).astype(np.float32),
        "expand": expand.astype(half),
        "pool_k": pool_k.astype(half),
        "spread_k": pool_k.T.copy().astype(half),
    }


def mm(a, b):
    return lax.dot_general(a, b, (((1,), (0,)), ((), ())), preferred_element_type=F32)


def mm_nt(a, b):
    return lax.dot_general(a, b, (((1,), (1,)), ((), ())), preferred_element_type=F32)


def mm_tn(a, b):
    return lax.dot_general(a, b, (((0,), (0,)), ((), ())), preferred_element_type=F32)


def norm_parts(values):
    centre = values - jnp.mean(values, axis=-1, keepdims=True)
    spread = jnp.mean(centre * centre, axis=-1, keepdims=True)
    scale = lax.rsqrt(spread + EPS)
    return centre * scale, scale


def norm_back(grad, xhat, scale, gain):
    e = grad * gain
    return (e - jnp.mean(e, axis=-1, keepdims=True) - xhat * jnp.mean(e * xhat, axis=-1, keepdims=True)) * scale


def joined(ref, first, count):
    parts = [ref[t, r : r + 1, :].astype(F32) for t in range(2) for r in range(first, first + count)]
    return jnp.concatenate(parts, axis=1)


def vector(ref, j):
    return jnp.concatenate([ref[16 + 4 * j + r : 17 + 4 * j + r, :].astype(F32) for r in range(4)], axis=1)


def column_sum(values):
    return jnp.sum(values, axis=0, keepdims=True)


def count_tables(length, bias_ref, inv_ref):
    length = length.astype(F32)
    for level in range(LEVELS):
        width = 2**level
        pad = 0 if level == 5 else 16
        count = SLOT // width + 2 * pad
        cell = lax.broadcasted_iota(jnp.int32, (count, 128), 0) - pad
        live = jnp.where(cell < 0, 0.0, length - (cell * width).astype(F32))
        rows = pl.ds(BASE[level], count)
        if level == 0:
            bias_ref[rows, :] = jnp.where(live > 0.0, 0.0, NEG)
        else:
            some = jnp.clip(live, 1.0, np.float32(width))
            bias_ref[rows, :] = jnp.where(live > 0.0, jnp.log(some), NEG)
            inv_ref[rows, :] = 1.0 / some


SKEW_F = 1
SKEW_B = 0
SKEW_P = 1
SKEW_E = 1
SKEW_M = 0


def interleave(chains, skew):
    live = dict(enumerate(chains))
    turn = 0
    while live:
        for j in sorted(live):
            if turn >= skew * j and next(live[j], live) is live:
                del live[j]
        turn += 1


def runs(touched, start, count):
    out = []
    for begin in range(start, start + count, 16):
        seen = begin in touched
        touched.add(begin)
        if out and out[-1][0] == seen:
            out[-1][2] += 16
        else:
            out.append([seen, begin, 16])
    return out


def window(ref, i, lanes):
    parts = []
    for start, count in window_parts(i):
        parts.append(ref[pl.ds(start, count), lanes])
    return jnp.concatenate(parts, axis=0)


def two_rows(block):
    first = lax.broadcasted_iota(jnp.int32, block.shape, 1) < 64
    zero = jnp.zeros_like(block)
    return jnp.concatenate([jnp.where(first, block, zero), jnp.where(first, zero, block)], axis=0)


def diagonal(block):
    n = block.shape[1] // 2
    return jnp.concatenate([block[:64, :n], block[64:, n:]], axis=0)


def four_rows(block):
    head = lax.broadcasted_iota(jnp.int32, block.shape, 1) // 64
    zero = jnp.zeros_like(block)
    return jnp.concatenate([jnp.where(head == j, block, zero) for j in range(4)], axis=0)


def corners(first, second):
    top = jnp.concatenate([first, jnp.zeros((first.shape[0], second.shape[1]), first.dtype)], axis=1)
    low = jnp.concatenate([jnp.zeros((second.shape[0], first.shape[1]), first.dtype), second], axis=1)
    return jnp.concatenate([top, low], axis=0)


def to_rows(level_one, others, index):
    row = lax.broadcasted_iota(jnp.int32, (8, TILE), 0)
    both = jnp.where(row == 0, jnp.broadcast_to(level_one, (8, TILE)), jnp.broadcast_to(others, (8, TILE)))
    return jnp.take_along_axis(both, index, axis=1)


def row_weights(weights, cell_rows):
    ones, rest = [], []
    for w in weights:
        wide = [jnp.broadcast_to(w[l : l + 1], (n, TILE)) for l, n in ((0, 64), (1, 32), (2, 16), (3, 8), (4, 8))]
        full = (jnp.concatenate(wide, axis=0) * cell_rows).astype(BF)
        ones.append(full[:64])
        rest.append(full[64:])
    return jnp.concatenate([corners(*ones), corners(*rest)], axis=0)


def keep_live(full, length, chunk, out_ref):
    row = lax.broadcasted_iota(jnp.int32, full.shape, 0) + 256 * chunk
    live = jnp.where(row < length, full, 0.0).astype(BF)
    out_ref[0, pl.ds(16 + 256 * chunk, 256), :] = live
    return live


def pack_cells(sums, chunk, out_ref, rough_ref, inv_ref):
    at = 0
    for level in range(1, LEVELS):
        count = 256 // 2**level
        pad = 0 if level == 5 else 16
        rows = pl.ds(BASE[level] + pad + count * chunk, count)
        cells = sums[at : at + count] * jnp.concatenate([inv_ref[rows, :]] * PAIRS, axis=1)
        if level == 5:
            rough_ref[pl.ds(8 * chunk, 8), :] = cells
        else:
            out_ref[0, rows, :] = cells.astype(BF)
        at += count


def forward_kernel(
    lens, x_ref, row_ref, w_ref, ends_ref,
    mask_ref, pool_q_ref, stat_ref, cell_rows_ref, pool_k_ref,
    n1_ref, q_ref, k_ref, v_ref, attn_ref, low_ref, lse_ref,
    bias_ref, inv_ref, rough_ref, tile_bias_ref,
):
    length = lens[pl.program_id(0)]
    count_tables(length, bias_ref, inv_ref)
    zeros = jnp.zeros((16, D), BF)
    for level in range(LEVELS - 1):
        cells = SLOT // 2**level
        for ref in (k_ref, v_ref):
            ref[0, pl.ds(BASE[level], 16), :] = zeros
            ref[0, pl.ds(BASE[level] + 16 + cells, 16), :] = zeros
    rough_k, rough_v = rough_ref.at[0], rough_ref.at[1]
    pre_gain, pre_shift = vector(row_ref, 0), vector(row_ref, 1)
    query_shift, value_shift = joined(ends_ref, 0, 2), joined(ends_ref, 2, 2)

    def project(chunk):
        rows = pl.ds(256 * chunk, 256)
        xhat, _ = norm_parts(x_ref[0, rows, :].astype(F32))
        n1 = (xhat * pre_gain + pre_shift).astype(BF)
        n1_ref[0, rows, :] = n1
        yield
        joint = [mm(n1, w_ref[t]) for t in range(2)]
        yield
        q, k, v = (jnp.concatenate([j[:, at : at + HALF] for j in joint], axis=1) for at in (0, HALF, 2 * HALF))
        q_ref[0, rows, :] = (q + query_shift).astype(BF) * BF(0.125)
        k = keep_live(k, length, chunk, k_ref)
        v = keep_live(v + value_shift, length, chunk, v_ref)
        yield
        k, v = mm(pool_k_ref[...], k), mm(pool_k_ref[...], v)
        yield
        pack_cells(k, chunk, k_ref, rough_k, inv_ref)
        pack_cells(v, chunk, v_ref, rough_v, inv_ref)
        yield

    interleave([project(chunk) for chunk in range(4)], SKEW_P)
    k_ref[0, pl.ds(BASE[5], 32), :] = rough_k[...].astype(BF)
    v_ref[0, pl.ds(BASE[5], 32), :] = rough_v[...].astype(BF)

    def tile(i, bias):
        rows = pl.ds(128 * i, 128)
        bias[...] = mask_ref[i] + window(bias_ref, i, slice(None))
        q = q_ref[0, rows, :]
        cells = mm(pool_q_ref[...], q).astype(BF)
        lse = {}

        def quad(u):
            lanes = slice(256 * u, 256 * u + 256)
            pairs = [slice(0, 128), slice(128, 256)]
            keys = window(k_ref.at[0], i, lanes)
            c_one, c_rest = four_rows(cells[:64, lanes]), four_rows(cells[64:, lanes])
            q_two = [two_rows(q[:, lanes][:, p]) for p in pairs]
            yield
            fine = [mm_nt(keys[:160, p], q_two[j]) for j, p in enumerate(pairs)]
            one, rest = mm_nt(keys[160:SPLIT], c_one), mm_nt(keys[SPLIT:], c_rest)
            yield
            one = [one[:, p] + bias[160:SPLIT] for p in pairs]
            rest = [rest[:, p] + bias[SPLIT:] for p in pairs]
            fine = [[f[:, p] + bias[:160] for p in pairs] for f in fine]
            top_one = [jnp.max(s, axis=0, keepdims=True) for s in one]
            top_rest = [jnp.max(s, axis=0, keepdims=True) for s in rest]
            top_fine = [[jnp.max(s, axis=0, keepdims=True) for s in f] for f in fine]
            yield
            one = [jnp.exp(s - top) for s, top in zip(one, top_one)]
            rest = [jnp.exp(s - top) for s, top in zip(rest, top_rest)]
            weights, shares, inverse = [], [], []
            row = lax.broadcasted_iota(jnp.int32, (8, TILE), 0)
            for j in range(2):
                sum_one = jnp.sum(one[j], axis=0, keepdims=True)
                sum_rest = jnp.sum(rest[j], axis=0, keepdims=True)
                pair_w, pair_p, pair_i = [], [], []
                for h in range(2):
                    tops = to_rows(top_one[j], top_rest[j], stat_ref[h])
                    sums = to_rows(sum_one, sum_rest, stat_ref[h])
                    top = jnp.maximum(top_fine[j][h], jnp.max(tops, axis=0, keepdims=True))
                    w = jnp.exp(tops - top).astype(BF).astype(F32)
                    p = jnp.exp(fine[j][h] - top)
                    total = jnp.sum(p, axis=0, keepdims=True)
                    total = total + jnp.sum(jnp.where(row < 5, w * sums, 0.0), axis=0, keepdims=True)
                    lse[4 * u + 2 * j + h] = top + jnp.log(total)
                    pair_w.append(w)
                    pair_p.append(p.astype(BF))
                    pair_i.append(1.0 / total)
                weights.append(row_weights(pair_w, cell_rows_ref[...]))
                shares.append(jnp.concatenate(pair_p, axis=1))
                inverse.append(jnp.concatenate(pair_i, axis=1))
            values = window(v_ref.at[0], i, lanes)
            v_fine = [values[:160, p].T for p in pairs]
            v_rough = [values[160:, p].T for p in pairs]
            yield
            mixed = [mm(v_rough[j], corners(one[j].astype(BF), rest[j].astype(BF))) for j in range(2)]
            out = [mm(v_fine[j], shares[j]) for j in range(2)]
            yield
            out = [out[j] + mm(mixed[j].astype(BF), weights[j]) for j in range(2)]
            yield
            for j in range(2):
                full = diagonal(out[j] * inverse[j]).T
                high = full.astype(BF)
                own = slice(256 * u + 128 * j, 256 * u + 128 * j + 128)
                attn_ref[0, rows, own] = high
                low_ref[0, rows, own] = (full - high.astype(F32)).astype(BF)
            if u == 1:
                lse_ref[0, :, rows] = jnp.concatenate([lse[h] for h in range(HEADS)], axis=0)
            yield

        return [quad(0), quad(1)]

    interleave([chain for i in range(TILES) for chain in tile(i, tile_bias_ref.at[i])], SKEW_F)


def middle_kernel(
    x_ref, attn_ref, cot_ref, w_ref, row_ref, ends_ref,
    out_ref, g1_ref, grad_ref, gvec_ref, gbup_ref,
    gwo_ref, gup_ref, gdown_ref,
):
    step = pl.program_id(0)

    @pl.when(step == 0)
    def _():
        gwo_ref[...] = jnp.zeros_like(gwo_ref)
        gup_ref[...] = jnp.zeros_like(gup_ref)
        gdown_ref[...] = jnp.zeros_like(gdown_ref)
        gvec_ref[...] = jnp.zeros_like(gvec_ref)
        gbup_ref[...] = jnp.zeros_like(gbup_ref)

    attn = attn_ref[...]
    cot = cot_ref[...]
    branch = sum(mm_nt(attn[:, HALF * t : HALF * t + HALF], w_ref[:, t, :, :HALF].reshape(D, HALF)) for t in range(2))
    y1 = x_ref[...].astype(F32) + (branch + vector(row_ref, 2))
    xhat, scale = norm_parts(y1)
    mid_gain = vector(row_ref, 3)
    n2 = (xhat * mid_gain + vector(row_ref, 4)).astype(BF)
    up_shift = joined(ends_ref, 4, 8)
    n2_t = n2.T
    cot_t = cot.T
    total = [y1 + vector(row_ref, 5), jnp.zeros_like(y1)]
    c = np.float32(np.sqrt(2.0 / np.pi))

    def hidden(part):
        cols = slice(256 * part, 256 * part + 256)
        at = HALF + 256 * (part % 4)
        up = w_ref[:, part // 4, :, at : at + 256].reshape(D, 256)
        at += FF // 2
        down_t = w_ref[:, part // 4, :, at : at + 256].reshape(D, 256)
        u = mm(n2, up) + up_shift[:, cols]
        dh = mm(cot, down_t)
        yield
        u2 = u * u
        t = jnp.tanh(u * (c + (c * 0.044715) * u2))
        h = 0.5 + 0.5 * t
        hid = (u * h).astype(BF)
        slope = h + 2.0 * h * (1.0 - h) * u * (c + (3.0 * c * 0.044715) * u2)
        dhp = dh * slope
        dhp_b = dhp.astype(BF)
        gbup_ref[:, cols] += column_sum(dhp)
        yield
        total[0] = total[0] + mm_nt(hid, down_t)
        total[1] = total[1] + mm_nt(dhp_b, up)
        gdown_ref[:, cols] += mm(cot_t, hid)
        gup_ref[:, cols] += mm(n2_t, dhp_b)
        yield

    interleave([hidden(part) for part in range(8)], SKEW_M)
    out, dn2 = total
    out_ref[...] = out.astype(BF)
    cot_f = cot.astype(F32)
    dy1 = cot_f + norm_back(dn2, xhat, scale, mid_gain)
    g1 = dy1.astype(BF)
    g1_ref[...] = g1
    gwo_ref[...] += mm(g1.T, attn)
    gvec_ref[...] += jnp.concatenate(
        [column_sum(g1.astype(F32)), column_sum(dn2 * xhat), column_sum(dn2), column_sum(cot_f), jnp.zeros((4, D), F32)],
        axis=0,
    )


    @pl.when(step == pl.num_programs(0) - 1)
    def _():
        rows = D // grad_ref.shape[0]
        for t in range(2):
            at = 0
            for ref, width in ((gwo_ref, HALF), (gup_ref, FF // 2), (gdown_ref, FF // 2)):
                part = ref[:, width * t : width * t + width].astype(BF)
                grad_ref[:, t, :, at : at + width] = part.reshape(grad_ref.shape[0], rows, width)
                at += width


def backward_kernel(
    lens, x_ref, n1_ref, q_ref, k_ref, v_ref, attn_ref, low_ref, lse_ref, g1_ref,
    row_ref, w_ref, wo_t_ref,
    mask_ref, pool_q_ref, stat_ref, cell_rows_ref, expand_ref, spread_k_ref,
    dx_ref, gqkv_ref, gvec_ref,
    bias_ref, inv_ref, tile_bias_ref, dk_ref, dv_ref, dqkv_ref,
):
    step = pl.program_id(0)

    @pl.when(step == 0)
    def _():
        gqkv_ref[...] = jnp.zeros_like(gqkv_ref)
        gvec_ref[...] = jnp.zeros_like(gvec_ref)

    length = lens[step]
    count_tables(length, bias_ref, inv_ref)
    touched = (set(), set())
    head_of = lax.broadcasted_iota(jnp.int32, (HEADS, D), 1) // HD
    heads = (head_of == lax.broadcasted_iota(jnp.int32, (HEADS, D), 0)).astype(BF)

    def tile(i, bias):
        rows = pl.ds(128 * i, 128)
        bias[...] = mask_ref[i] + window(bias_ref, i, slice(None))
        q = q_ref[0, rows, :]
        cells = mm(pool_q_ref[...], q).astype(BF)
        da = jnp.concatenate([mm(g1_ref[0, rows, :], wo_t_ref[:, t, :, :HALF].reshape(D, HALF)) for t in range(2)], axis=1)
        da = da.astype(BF)
        product = da.astype(F32) * (attn_ref[0, rows, :].astype(F32) + low_ref[0, rows, :].astype(F32))
        high = product.astype(BF)
        delta = mm_nt(heads, high) + mm_nt(heads, (product - high.astype(F32)).astype(BF))
        lse = lse_ref[0, :, rows]

        def quad(u):
            lanes = slice(256 * u, 256 * u + 256)
            pairs = [slice(0, 128), slice(128, 256)]
            keys = window(k_ref.at[0], i, lanes)
            values = window(v_ref.at[0], i, lanes)
            c_one, c_rest = four_rows(cells[:64, lanes]), four_rows(cells[64:, lanes])
            q_two = [two_rows(q[:, lanes][:, p]) for p in pairs]
            d_two = [two_rows(da[:, lanes][:, p]) for p in pairs]
            yield
            fine = [mm_nt(keys[:160, p], q_two[j]) for j, p in enumerate(pairs)]
            one, rest = mm_nt(keys[160:SPLIT], c_one), mm_nt(keys[SPLIT:], c_rest)
            dp = [mm_nt(values[:160, p], d_two[j]) for j, p in enumerate(pairs)]
            yield
            ones, rests, weights, shares, slopes, rows_delta = [], [], [], [], [], []
            for j, pair in enumerate(pairs):
                s_one, s_rest = one[:, pair] + bias[160:SPLIT], rest[:, pair] + bias[SPLIT:]
                top_one, top_rest = jnp.max(s_one, axis=0, keepdims=True), jnp.max(s_rest, axis=0, keepdims=True)
                ones.append(jnp.exp(s_one - top_one))
                rests.append(jnp.exp(s_rest - top_rest))
                pair_w, pair_p, pair_s = [], [], []
                for h, p in enumerate(pairs):
                    head = 4 * u + 2 * j + h
                    own_lse, own_delta = lse[head : head + 1], delta[head : head + 1]
                    pair_w.append(jnp.exp(to_rows(top_one, top_rest, stat_ref[h]) - own_lse))
                    share = jnp.exp(fine[j][:, p] + bias[:160] - own_lse)
                    pair_s.append((share * (dp[j][:, p] - own_delta)).astype(BF))
                    pair_p.append(share.astype(BF))
                weights.append(row_weights(pair_w, cell_rows_ref[...]))
                shares.append(jnp.concatenate(pair_p, axis=1))
                slopes.append(jnp.concatenate(pair_s, axis=1))
                head = 4 * u + 2 * j
                both = jnp.concatenate([delta[head : head + 1], delta[head + 1 : head + 2]], axis=1)
                top = both.astype(BF).astype(F32)
                rows_delta.append(jnp.concatenate([top, both - top, jnp.zeros((6, 256), F32)], axis=0).astype(BF))
            k_fine = [keys[:160, p].T for p in pairs]
            k_rough = [keys[160:, p].T for p in pairs]
            yield
            d_cells = [mm(weights[j], d_two[j]).astype(BF) for j in range(2)]
            delta_cells = [jnp.sum(mm_nt(rows_delta[j], weights[j]), axis=0, keepdims=True) for j in range(2)]
            dv_fine = [mm(shares[j], d_two[j]) for j in range(2)]
            yield
            d_one, d_rest = (corners(d_cells[0][a : a + 128], d_cells[1][a : a + 128]) for a in (0, 128))
            dp_one, dp_rest = mm_nt(values[160:SPLIT], d_one), mm_nt(values[SPLIT:], d_rest)
            dk_fine = [mm(slopes[j], q_two[j]) for j in range(2)]
            dq = [mm(k_fine[j], slopes[j]) for j in range(2)]
            yield
            s_one = [(ones[j] * (dp_one[:, p] - delta_cells[j][:, :128])).astype(BF) for j, p in enumerate(pairs)]
            s_rest = [(rests[j] * (dp_rest[:, p] - delta_cells[j][:, 128:])).astype(BF) for j, p in enumerate(pairs)]
            dv_one = mm(jnp.concatenate([e.astype(BF) for e in ones], axis=1), d_one)
            dv_rest = mm(jnp.concatenate([e.astype(BF) for e in rests], axis=1), d_rest)
            yield
            dq_cells = [mm(k_rough[j], corners(s_one[j], s_rest[j])).astype(BF) for j in range(2)]
            dk_one = mm(jnp.concatenate(s_one, axis=1), c_one)
            dk_rest = mm(jnp.concatenate(s_rest, axis=1), c_rest)
            yield
            dq = [diagonal(dq[j] + mm(dq_cells[j], expand_ref[...])) * 0.125 for j in range(2)]
            dk = jnp.concatenate([jnp.concatenate(dk_fine, axis=1), dk_one, dk_rest], axis=0)
            dv = jnp.concatenate([jnp.concatenate(dv_fine, axis=1), dv_one, dv_rest], axis=0)
            at = 0
            for start, count in window_parts(i):
                for seen, begin, n in runs(touched[u], start, count):
                    part = pl.ds(begin, n)
                    for ref, grad in ((dk_ref, dk), (dv_ref, dv)):
                        block = grad[at + begin - start : at + begin - start + n]
                        ref[part, lanes] = ref[part, lanes] + block if seen else block
                at += count
            yield
            for j in range(2):
                at = 3 * HALF * u + 128 * j
                dqkv_ref[rows, at : at + 128] = dq[j].T.astype(BF)
            yield

        return [quad(0), quad(1)]

    interleave([chain for i in range(TILES) for chain in tile(i, tile_bias_ref.at[i])], SKEW_B)

    sums = []
    pre_gain = vector(row_ref, 0)

    def finish(chunk):
        rows = pl.ds(256 * chunk, 256)
        own = pl.ds(16 + 256 * chunk, 256)
        live = lax.broadcasted_iota(jnp.int32, (256, D), 0) + 256 * chunk < length
        wide = []
        for ref in (dk_ref, dv_ref):
            cells = []
            for level in range(1, LEVELS):
                count = 256 // 2**level
                pad = 0 if level == 5 else 16
                part = pl.ds(BASE[level] + pad + count * chunk, count)
                cells.append(ref[part, :] * jnp.concatenate([inv_ref[part, :]] * PAIRS, axis=1))
            cells.append(jnp.zeros((8, D), F32))
            wide.append(jnp.concatenate(cells, axis=0).astype(BF))
        yield
        wide = [mm(spread_k_ref[...], w) for w in wide]
        yield
        for ref, at, w in zip((dk_ref, dv_ref), (HALF, 2 * HALF), wide):
            grad = jnp.where(live, ref[own, :] + w, 0.0).astype(BF)
            dqkv_ref[rows, at : at + HALF] = grad[:, :HALF]
            dqkv_ref[rows, at + 3 * HALF : at + 4 * HALF] = grad[:, HALF:]
        yield
        parts = [dqkv_ref[rows, 3 * HALF * t : 3 * HALF * t + 3 * HALF] for t in range(2)]
        dn1 = mm_nt(parts[0], w_ref[0]) + mm_nt(parts[1], w_ref[1])
        xhat, scale = norm_parts(x_ref[0, rows, :].astype(F32))
        yield
        dx = g1_ref[0, rows, :].astype(F32) + norm_back(dn1, xhat, scale, pre_gain)
        dx_ref[0, rows, :] = dx.astype(BF)
        col = [column_sum(part.astype(F32)) for part in parts]
        sums.append(
            jnp.concatenate(
                [
                    column_sum(dn1 * xhat), column_sum(dn1),
                    jnp.concatenate([c[:, :HALF] for c in col], axis=1),
                    jnp.concatenate([c[:, 2 * HALF :] for c in col], axis=1),
                    jnp.zeros((4, D), F32),
                ],
                axis=0,
            )
        )
        yield

    interleave([finish(chunk) for chunk in range(4)], SKEW_E)
    gvec_ref[...] += sums[0] + sums[1] + sums[2] + sums[3]
    n1_t = n1_ref[0].T
    for t in range(2):
        gqkv_ref[t] += mm(n1_t, dqkv_ref[:, 3 * HALF * t : 3 * HALF * t + 3 * HALF])


def whole(shape):
    return pl.BlockSpec(shape, lambda *_: (0,) * len(shape))


def per_sequence(*shape):
    return pl.BlockSpec((1,) + shape, lambda s, *_: (s,) + (0,) * len(shape))


LIMIT = 60 * 1024 * 1024


def attention_forward(x, lens, row, w, ends, const):
    count = x.shape[0]
    return pl.pallas_call(
        forward_kernel,
        grid_spec=pltpu.PrefetchScalarGridSpec(
            num_scalar_prefetch=1,
            grid=(count,),
            in_specs=[
                per_sequence(SLOT, D), whole((SMALL, 128)), whole((2, D, 3 * HALF)), whole((2, 16, 128)),
                whole((TILES, WIN, TILE)), whole((TILE, TILE)), whole((2, 8, TILE)), whole((TILE, TILE)), whole((256, 256)),
            ],
            out_specs=[
                per_sequence(SLOT, D), per_sequence(SLOT, D), per_sequence(CELL_ROWS, D), per_sequence(CELL_ROWS, D),
                per_sequence(SLOT, D), per_sequence(SLOT, D), per_sequence(HEADS, SLOT),
            ],
            scratch_shapes=[
                pltpu.VMEM((CELL_ROWS, 128), F32), pltpu.VMEM((CELL_ROWS, 128), F32), pltpu.VMEM((2, 32, D), F32),
                pltpu.VMEM((TILES, WIN, TILE), F32),
            ],
        ),
        out_shape=[
            jax.ShapeDtypeStruct((count, SLOT, D), BF), jax.ShapeDtypeStruct((count, SLOT, D), BF),
            jax.ShapeDtypeStruct((count, CELL_ROWS, D), BF), jax.ShapeDtypeStruct((count, CELL_ROWS, D), BF),
            jax.ShapeDtypeStruct((count, SLOT, D), BF), jax.ShapeDtypeStruct((count, SLOT, D), BF),
            jax.ShapeDtypeStruct((count, HEADS, SLOT), F32),
        ],
        compiler_params=pltpu.CompilerParams(vmem_limit_bytes=LIMIT),
        cost_estimate=pl.CostEstimate(flops=count * 30 * 10**9, bytes_accessed=count * 10**7, transcendentals=0),
        name="attention_forward",
    )(lens, x, row, w, ends, const["mask"], const["pool_q"], const["stat"], const["cell_rows"], const["pool_k"])


ROWS = 512


def middle(x, attn, cot, w, row, ends):
    total = x.shape[0]
    rows = pl.BlockSpec((ROWS, D), lambda s: (s, 0))
    return pl.pallas_call(
        middle_kernel,
        grid=(total // ROWS,),
        in_specs=[
            rows, rows, rows, whole(w.shape), whole((SMALL, 128)), whole((2, 16, 128)),
        ],
        out_specs=[rows, rows, whole(w.shape), whole((8, D)), whole((1, FF))],
        scratch_shapes=[pltpu.VMEM((D, D), F32), pltpu.VMEM((D, FF), F32), pltpu.VMEM((D, FF), F32)],
        out_shape=[
            jax.ShapeDtypeStruct((total, D), BF), jax.ShapeDtypeStruct((total, D), BF), jax.ShapeDtypeStruct(w.shape, BF),
            jax.ShapeDtypeStruct((8, D), F32), jax.ShapeDtypeStruct((1, FF), F32),
        ],
        compiler_params=pltpu.CompilerParams(vmem_limit_bytes=LIMIT),
        name="middle",
    )(x, attn, cot, w, row, ends)


def attention_backward(x, lens, n1, q, k, v, attn, low, lse, g1, row, w, rest, const):
    count = x.shape[0]
    wo_t = pl.BlockSpec(rest.shape[:3] + (HALF,), lambda *_: (0, 0, 0, 0))
    return pl.pallas_call(
        backward_kernel,
        grid_spec=pltpu.PrefetchScalarGridSpec(
            num_scalar_prefetch=1,
            grid=(count,),
            in_specs=[
                per_sequence(SLOT, D), per_sequence(SLOT, D), per_sequence(SLOT, D),
                per_sequence(CELL_ROWS, D), per_sequence(CELL_ROWS, D), per_sequence(SLOT, D), per_sequence(SLOT, D),
                per_sequence(HEADS, SLOT), per_sequence(SLOT, D),
                whole((SMALL, 128)), whole((2, D, 3 * HALF)), wo_t,
                whole((TILES, WIN, TILE)), whole((TILE, TILE)), whole((2, 8, TILE)), whole((TILE, TILE)),
                whole((256, 256)), whole((256, 256)),
            ],
            out_specs=[per_sequence(SLOT, D), whole((2, D, 3 * HALF)), whole((8, D))],
            scratch_shapes=[
                pltpu.VMEM((CELL_ROWS, 128), F32), pltpu.VMEM((CELL_ROWS, 128), F32), pltpu.VMEM((TILES, WIN, TILE), F32),
                pltpu.VMEM((CELL_ROWS, D), F32), pltpu.VMEM((CELL_ROWS, D), F32), pltpu.VMEM((SLOT, 3 * D), BF),
            ],
        ),
        out_shape=[
            jax.ShapeDtypeStruct((count, SLOT, D), BF), jax.ShapeDtypeStruct((2, D, 3 * HALF), F32),
            jax.ShapeDtypeStruct((8, D), F32),
        ],
        compiler_params=pltpu.CompilerParams(vmem_limit_bytes=LIMIT),
        cost_estimate=pl.CostEstimate(flops=count * 40 * 10**9, bytes_accessed=count * 10**7, transcendentals=0),
        name="attention_backward",
    )(
        lens, x, n1, q, k, v, attn, low, lse, g1, row, w, rest,
        const["mask"], const["pool_q"], const["stat"], const["cell_rows"], const["expand"], const["spread_k"],
    )


def bits_of(count):
    return count.bit_length() - 1


def all_bits(n_dp, n_t):
    return [("tensor", b) for b in reversed(range(bits_of(n_t)))] + [("dp", b) for b in reversed(range(bits_of(n_dp)))]


def gather_orders(n_dp, n_t):
    far = [("dp", b) for b in reversed(range(2, bits_of(n_dp)))]
    near = [("dp", 1)]
    side = [("tensor", b) for b in reversed(range(bits_of(n_t)))]
    core_bit = [("dp", 0)]
    return far + near + side + core_bit, far + side + near + core_bit


def own_bit(bit):
    axis, b = bit
    return (lax.axis_index(axis) // 2**b) % 2


def partner(bit):
    axis, b = bit
    return {axis: lax.axis_index(axis) + (1 - 2 * own_bit(bit)) * 2**b}


def meet(bits):
    barrier = pltpu.get_barrier_semaphore()
    for bit in bits:
        pl.semaphore_signal(barrier, inc=1, device_id=partner(bit), device_id_type=pl.DeviceIdType.MESH)
    pl.semaphore_wait(barrier, len(bits))


def halves(width):
    if width % 256:
        return [(0, width)]
    return [(0, width // 2), (width // 2, width // 2)]


def gather_kernel(
    bits, orders, parts, *refs
):
    *shard_refs, ends_ref, out_ref, all_ends_ref, own_sems, send_sems, recv_sems, ends_own_sem, ends_sems = refs
    slot = out_ref.at[tuple(own_bit(bit) for bit in bits)]
    width = shard_refs[0].shape[1]
    own = [
        pltpu.make_async_copy(ref, slot.at[:, pl.ds(width * j, width)], own_sems.at[j]) for j, ref in enumerate(shard_refs)
    ]
    for copy in own:
        copy.start()
    side = [bit for bit in bits if bit[0] == "tensor"]
    own_ends = pltpu.make_async_copy(ends_ref.at[pl.ds(0, 16)], all_ends_ref.at[tuple(own_bit(bit) for bit in side)], ends_own_sem)
    own_ends.start()
    meet(bits)
    pending = []
    own_ends.wait()
    for copy in own:
        copy.wait()

    def ends_copy(step):
        place = all_ends_ref.at[tuple(slice(None) if j < step else own_bit(bit) for j, bit in enumerate(side))]
        return pltpu.make_async_remote_copy(
            src_ref=place, dst_ref=place, send_sem=ends_sems.at[0, step], recv_sem=ends_sems.at[1, step],
            device_id=partner(side[step]), device_id_type=pl.DeviceIdType.MESH,
        )

    if side:
        ends_copy(0).start()
    for step in range(len(bits)):
        for part, (at, width) in enumerate(parts):
            order = orders[part]
            done = order[:step]
            index = tuple(slice(None) if bit in done else own_bit(bit) for bit in bits)
            place = out_ref.at[index + (slice(None), pl.ds(at, width))]
            if step > 0:
                pending[(step - 1) * len(parts) + part].wait_recv()
            copy = pltpu.make_async_remote_copy(
                src_ref=place, dst_ref=place,
                send_sem=send_sems.at[step, part], recv_sem=recv_sems.at[step, part],
                device_id=partner(order[step]), device_id_type=pl.DeviceIdType.MESH,
            )
            copy.start()
            pending.append(copy)
    for copy in pending[-len(parts) :]:
        copy.wait_recv()
    for step in range(len(side)):
        ends_copy(step).wait_recv()
        if step + 1 < len(side):
            ends_copy(step + 1).start()
    for step in range(len(side)):
        ends_copy(step).wait_send()
    for copy in pending:
        copy.wait_send()


def gather(shards, ends, n_dp, n_t):
    rows, width = shards[0].shape[0], len(shards) * shards[0].shape[1]
    bits, orders, parts = all_bits(n_dp, n_t), gather_orders(n_dp, n_t), halves(width)
    side = bits_of(n_t)
    anywhere = pl.BlockSpec(memory_space=pl.ANY)
    out, all_ends = pl.pallas_call(
        functools.partial(gather_kernel, bits, orders, parts),
        in_specs=[anywhere] * (len(shards) + 1),
        out_specs=[anywhere, anywhere],
        out_shape=[
            jax.ShapeDtypeStruct((2,) * len(bits) + (rows, width), BF),
            jax.ShapeDtypeStruct((2,) * side + (16, 128), BF),
        ],
        scratch_shapes=[
            pltpu.SemaphoreType.DMA((len(shards),)), pltpu.SemaphoreType.DMA((len(bits), len(parts))),
            pltpu.SemaphoreType.DMA((len(bits), len(parts))), pltpu.SemaphoreType.DMA,
            pltpu.SemaphoreType.DMA((2, max(side, 1))),
        ],
        compiler_params=pltpu.CompilerParams(collective_id=0, has_side_effects=True),
        name="gather",
    )(*shards, ends)
    return out.reshape(n_t, n_dp, rows, width), all_ends.reshape(n_t, 16, 128)


def reduce_kernel(bits, orders, parts, n_t, grad_ref, pre_ref, mid_ref, up_ref, out_ref, own_ref, *scratch):
    steps, count = len(bits), len(parts)
    sends, recvs, sums = (scratch[j * steps * count : (j + 1) * steps * count] for j in range(3))
    vec_out_ref, vec_recv, send_sems, recv_sems, vec_send_sems, vec_recv_sems = scratch[3 * steps * count :]
    meet(bits)
    vec_out_ref[0:4, :] = pre_ref[0:4, :]
    vec_out_ref[4:8, :] = mid_ref[0:4, :]
    for r in range(4):
        vec_out_ref[8 + r : 9 + r, :] = up_ref[:, D * r : D * r + D]
    vec_out_ref[12:16, :] = jnp.zeros((4, D), F32)

    def vec_copy(step):
        return pltpu.make_async_remote_copy(
            src_ref=vec_recv.at[2 * step], dst_ref=vec_recv.at[2 * step + 1],
            send_sem=vec_send_sems.at[step], recv_sem=vec_recv_sems.at[step],
            device_id=partner(orders[0][steps - 1 - step]), device_id_type=pl.DeviceIdType.MESH,
        )

    def copy_of(step, part):
        j = step * count + part
        return pltpu.make_async_remote_copy(
            src_ref=sends[j], dst_ref=recvs[j], send_sem=send_sems.at[step, part], recv_sem=recv_sems.at[step, part],
            device_id=partner(orders[part][steps - 1 - step]), device_id_type=pl.DeviceIdType.MESH,
        )

    def pieces(step, part):
        order = orders[part][::-1]
        left = [bit for bit in bits if bit not in order[:step]]
        j = left.index(order[step])
        low = 2 ** (len(left) - 1 - j)
        mine = own_bit(order[step])
        out = []
        for a in range(2**j):
            for c in range(low):
                out.append(((a * 2 + 1 - mine) * low + c, (a * 2 + mine) * low + c, a * low + c))
        at, width = parts[part]
        source = sums[(step - 1) * count + part] if step else grad_ref.at[:, :, pl.ds(at, width)]
        return out, source

    for step in range(steps):
        vec_recv[2 * step] = vec_out_ref[...]
        vec_copy(step).start()
        for part in range(count):
            blocks, source = pieces(step, part)
            for away, _, to in blocks:
                sends[step * count + part][to] = source[away].astype(BF)
            copy_of(step, part).start()
        for part in range(count):
            copy_of(step, part).wait_recv()
            blocks, source = pieces(step, part)
            for _, keep, to in blocks:
                total = source[keep] + recvs[step * count + part][to].astype(F32)
                if step == steps - 1:
                    at, width = parts[part]
                    out_ref[:, at : at + width] = total
                else:
                    sums[step * count + part][to] = total
        vec_copy(step).wait_recv()
        vec_out_ref[...] += vec_recv[2 * step + 1]
    own_ref[...] = jnp.zeros_like(own_ref)
    own_ref[0:8, 0:D] = vec_out_ref[0:8, :]
    t = lax.axis_index("tensor")
    for row in (2, 3):
        n = D // n_t
        full = vec_out_ref[row : row + 1, :]
        mine = full[:, :n]
        for j in range(1, n_t):
            mine = jnp.where(t == j, full[:, n * j : n * j + n], mine)
        own_ref[row : row + 1, 0:n] = mine
    n = FF // n_t
    full = jnp.concatenate([vec_out_ref[8 + r : 9 + r, :] for r in range(4)], axis=1)
    mine = full[:, :n]
    for j in range(1, n_t):
        mine = jnp.where(t == j, full[:, n * j : n * j + n], mine)
    own_ref[8:9, 0:n] = mine
    for step in range(steps):
        vec_copy(step).wait_send()
        for part in range(count):
            copy_of(step, part).wait_send()


def reduce(grad, pre, mid, up, n_dp, n_t):
    rows, width = grad.shape[2:]
    bits, orders, parts = all_bits(n_dp, n_t), gather_orders(n_dp, n_t), halves(width)
    steps = len(bits)
    blocks = [(2 ** (steps - 1 - step), rows, w) for step in range(steps) for _, w in parts]
    sems = pltpu.SemaphoreType.DMA
    vmem = pl.BlockSpec(memory_space=pltpu.VMEM)
    return pl.pallas_call(
        functools.partial(reduce_kernel, bits, orders, parts, n_t),
        in_specs=[vmem] * 4,
        out_specs=[vmem, vmem],
        out_shape=[jax.ShapeDtypeStruct((rows, width), F32), jax.ShapeDtypeStruct((16, max(D, FF // n_t)), F32)],
        scratch_shapes=[pltpu.VMEM(b, BF) for b in blocks] * 2
        + [pltpu.VMEM(b, F32) for b in blocks]
        + [
            pltpu.VMEM((16, D), F32), pltpu.VMEM((2 * steps, 16, D), F32), sems((steps, len(parts))), sems((steps, len(parts))),
            sems((steps,)), sems((steps,)),
        ],
        compiler_params=pltpu.CompilerParams(collective_id=1, has_side_effects=True, vmem_limit_bytes=LIMIT),
        name="reduce",
    )(grad.reshape(n_t * n_dp, rows, width), pre, mid, up)


def to_pairs(grid, widths):
    n_t, n_dp, rows, _ = grid.shape
    grid = grid.reshape(n_t, n_dp * rows, -1)
    if n_t == 2:
        return grid
    out, at = [], 0
    for width in widths:
        part = grid[:, :, at : at + width].reshape(2, n_t // 2, D, width)
        out.append(part.transpose(0, 2, 1, 3).reshape(2, D, n_t // 2 * width))
        at += width
    return jnp.concatenate(out, axis=2)


def from_pairs(grid, widths, n_dp, n_t):
    if n_t != 2:
        out, at = [], 0
        for width in widths:
            full = width * n_t // 2
            part = grid[:, :, at : at + full].reshape(2, D, n_t // 2, width)
            out.append(part.transpose(0, 2, 1, 3).reshape(n_t, D, width))
            at += full
        grid = jnp.concatenate(out, axis=2)
    return grid.reshape(n_t, n_dp, D // n_dp, -1)


def own_sequences(values, lengths, tensor_count):
    micro, rows, width = values[0].shape
    t = lax.axis_index("tensor")
    if rows % SLOT == 0:
        per = rows // SLOT
        own = lax.dynamic_slice_in_dim(lengths, t * per, per, 1).reshape(-1)
        return [v.reshape(micro * per, SLOT, width) for v in values], own
    pieces = SLOT // rows
    assert micro == pieces
    groups = [[g * pieces + j for j in range(pieces)] for g in range(tensor_count // pieces)]
    out = [lax.all_to_all(v, "tensor", 0, 1, axis_index_groups=groups, tiled=True) for v in values]
    sequence = lax.dynamic_slice(lengths, (t % pieces, t // pieces), (1, 1))
    return out, sequence.reshape(-1)


def own_rows(values, shape, tensor_count):
    micro, rows, width = shape
    if rows % SLOT == 0:
        return [v.reshape(shape) for v in values]
    pieces = SLOT // rows
    groups = [[g * pieces + j for j in range(pieces)] for g in range(tensor_count // pieces)]
    return [
        lax.all_to_all(v, "tensor", 1, 0, axis_index_groups=groups, tiled=True).reshape(shape) for v in values
    ]


def core(x, lens, cot, row, w, ends, rest):
    const = {name: jnp.asarray(value) for name, value in constants().items()}
    count = x.shape[0]
    flat = (count * SLOT, D)
    n1, q, k, v, attn, low, lse = attention_forward(x, lens, row, w, ends, const)
    out, g1, grad_rest, mid_vec, gbup = middle(
        x.reshape(flat), attn.reshape(flat), cot.reshape(flat), rest, row, ends
    )
    dx, gqkv, pre_vec = attention_backward(
        x, lens, n1, q, k, v, attn, low, lse, g1.reshape(count, SLOT, D), row, w, rest, const
    )
    return out, dx, grad_rest, mid_vec, gbup, gqkv, pre_vec


def on_device(
    inputs, lengths, pre_gain, pre_shift, query_weight, key_weight, value_weight, query_bias, value_bias,
    output_weight, output_bias, mid_gain, mid_shift, up_weight, up_bias, down_weight, down_bias, cotangent,
):
    n_dp, n_t = lax.axis_size("dp"), lax.axis_size("tensor")
    t = lax.axis_index("tensor")
    (x, cot), lens = own_sequences([inputs, cotangent], lengths, n_t)

    n_q, n_f = query_weight.shape[1], up_weight.shape[1]
    second = jnp.concatenate([output_weight.T, up_weight, down_weight.T], axis=1)
    small = ((query_bias, 0), (value_bias, n_q), (up_bias, 2 * n_q))
    vectors = (pre_gain, pre_shift, output_bias, mid_gain, mid_shift, down_bias)
    small += tuple((v, 2048 + D * j) for j, v in enumerate(vectors))
    row = sum(lax.pad(v, jnp.zeros((), BF), [(at, SMALL * 128 - at - v.shape[0], 0)]) for v, at in small)
    row = row.reshape(SMALL, 128)
    first = (query_weight, key_weight, value_weight)
    if n_q % 128:
        first = (jnp.concatenate(first, axis=1),)
    w, ends = gather(first, row, n_dp, n_t)
    w = to_pairs(w, (n_q,) * 3)
    rest = lax.all_gather(second, ("dp", "tensor"), axis=0, tiled=False)
    rest = rest.reshape(n_dp, n_t, D // n_dp, -1)
    if n_t != 2:
        rest = to_pairs(rest.transpose(1, 0, 2, 3), (n_q, n_f, n_f)).reshape(2, 16, 32, REST).transpose(1, 0, 2, 3)
        flat = ends.reshape(n_t, -1)
        parts = [flat[:, a : a + n].reshape(2, -1) for a, n in ((0, n_q), (n_q, n_q), (2 * n_q, n_f))]
        ends = jnp.concatenate(parts + [jnp.zeros((2, 512), ends.dtype)], axis=1).reshape(2, 16, 128)
    out, dx, grad_rest, mid_vec, gbup, gqkv, pre_vec = core(x, lens, cot, row, w, ends, rest)
    if n_t != 2:
        grad_rest = grad_rest.transpose(1, 0, 2, 3).reshape(2, D, REST)
        grad_rest = from_pairs(grad_rest, (n_q, n_f, n_f), n_dp, n_t).transpose(1, 0, 2, 3)
    grad_rest = grad_rest.reshape(n_dp * n_t, D // n_dp, -1)
    grad_rest = lax.psum_scatter(grad_rest, ("dp", "tensor"), scatter_dimension=0, tiled=False).astype(F32)
    grad_first, vec = reduce(from_pairs(gqkv, (n_q,) * 3, n_dp, n_t), pre_vec, mid_vec, gbup, n_dp, n_t)
    grad_q, grad_k, grad_v = (grad_first[:, n_q * j : n_q * j + n_q] for j in range(3))
    grad_o, grad_up, grad_down = grad_rest[:, :n_q].T, grad_rest[:, n_q : n_q + n_f], grad_rest[:, n_q + n_f :].T

    out, dx = own_rows([out.reshape(x.shape), dx], inputs.shape, n_t)
    each = [vec[j, :D] for j in range(8)]
    return (
        out, dx, each[0], each[1], grad_q, grad_k, grad_v, vec[2, :n_q], vec[3, :n_q], grad_o, each[4], each[5], each[6],
        grad_up, vec[8, :n_f], grad_down, each[7],
    )


def solution(mesh):
    rows = P(None, ("dp", "tensor"), None)
    by_row, by_column = P("dp", "tensor"), P("tensor", "dp")
    in_specs = (
        rows, P(None, "dp"), P(), P(), by_row, by_row, by_row, P("tensor"), P("tensor"), by_column, P(), P(), P(),
        by_row, P("tensor"), by_column, P(), rows,
    )
    out_specs = (
        rows, rows, P(), P(), by_row, by_row, by_row, P("tensor"), P("tensor"), by_column, P(), P(), P(),
        by_row, P("tensor"), by_column, P(),
    )
    return jax.shard_map(on_device, mesh=mesh, in_specs=in_specs, out_specs=out_specs, check_vma=False)
```

```python
import functools

import jax
import jax.numpy as jnp
import ml_dtypes
import numpy as np
from jax import lax
from jax.experimental import pallas as pl
from jax.experimental.pallas import tpu as pltpu
from jax.sharding import PartitionSpec as P

D = 512
HD = 64
FF = 2048
NR = 16
LEVELS = 6
SLOT = 1024
TILE = 128
TILES = SLOT // TILE
PAIRS = D // 128
HEADS = D // HD
HALF = D // 2
REST = HALF + FF
SMALL = 40
EPS = 1e-05
NEG = -1e30

BASE = (0, 1056, 1600, 1888, 2048, 2144)
CELL_ROWS = 2176
WIN_ROWS = (160, 96, 64, 32, 32, 16)
WIN_AT = (0, 160, 256, 320, 352, 384)
WIN = 400
COARSE = WIN - 160
LANE_AT = (0, 0, 0, 32, 48, 56)
SPLIT = WIN_AT[2]
BF = jnp.bfloat16
F32 = jnp.float32


def window_parts(i):
    two, four = i // 2, i // 4
    return (
        (128 * i, 160),
        (BASE[1] + 64 * i, 96),
        (BASE[2] + 32 * i, 64),
        (BASE[3] + 16 * i, 16),
        (BASE[3] + 16 * i + 32, 16),
        (BASE[4] + 16 * two, 16),
        (BASE[4] + 16 * two + 32, 16),
        (BASE[5] + 16 * (1 - four), 16),
    )


def mask_table():
    table = np.full((TILES, WIN, TILE), NEG, np.float32)
    for i in range(TILES):
        at = 0
        for start, count in window_parts(i):
            level = max(l for l in range(LEVELS) if WIN_AT[l] <= at)
            pad = 0 if level == 5 else 16
            cell = (start - BASE[level] - pad + np.arange(count))[:, None]
            here = TILE >> level
            query = (((128 * i) >> level) + np.arange(here))[None, :]
            good = np.abs(cell // 16 - query // 16) <= 1
            if level > 0:
                good &= np.abs((2 * cell) // 16 - (2 * query) // 16) > 1
            for head in range(1 if level == 0 else 2):
                lane = 64 * head + LANE_AT[level]
                table[i, at : at + count, lane : lane + here] = np.where(good, 0.0, NEG)
            at += count
    return table


def constants():
    t = np.arange(TILE)
    pool_q = np.zeros((TILE, TILE), np.float32)
    stat = np.zeros((2, 8, TILE), np.int32)
    expand = np.zeros((256, 256), np.float32)
    pool_k = np.zeros((256, 256), np.float32)
    t2 = np.arange(256)
    at = 0
    for level in range(1, LEVELS):
        width = 2**level
        half = 0 if level == 1 else 64
        pool_q[half + LANE_AT[level] + t // width, t] = 1.0 / width
        for head in range(2):
            stat[head, level - 1 :] = 64 * head + LANE_AT[level] + t // width
            expand[2 * half + 64 * head + LANE_AT[level] + t // width, 128 * head + t] = 1.0 / width
        pool_k[at + t2 // width, t2] = 1.0
        at += 256 // width
    half = ml_dtypes.bfloat16
    return {
        "mask": mask_table(),
        "pool_q": pool_q.astype(half),
        "stat": stat,
        "cell_rows": (pool_q > 0).astype(np.float32),
        "expand": expand.astype(half),
        "pool_k": pool_k.astype(half),
        "spread_k": pool_k.T.copy().astype(half),
    }


def mm(a, b):
    return lax.dot_general(a, b, (((1,), (0,)), ((), ())), preferred_element_type=F32)


def mm_nt(a, b):
    return lax.dot_general(a, b, (((1,), (1,)), ((), ())), preferred_element_type=F32)


def mm_tn(a, b):
    return lax.dot_general(a, b, (((0,), (0,)), ((), ())), preferred_element_type=F32)


def norm_parts(values):
    centre = values - jnp.mean(values, axis=-1, keepdims=True)
    spread = jnp.mean(centre * centre, axis=-1, keepdims=True)
    scale = lax.rsqrt(spread + EPS)
    return centre * scale, scale


def norm_back(grad, xhat, scale, gain):
    e = grad * gain
    return (e - jnp.mean(e, axis=-1, keepdims=True) - xhat * jnp.mean(e * xhat, axis=-1, keepdims=True)) * scale


def joined(ref, first, count):
    parts = [ref[t, r : r + 1, :].astype(F32) for t in range(2) for r in range(first, first + count)]
    return jnp.concatenate(parts, axis=1)


def vector(ref, j):
    return jnp.concatenate([ref[16 + 4 * j + r : 17 + 4 * j + r, :].astype(F32) for r in range(4)], axis=1)


def column_sum(values):
    return jnp.sum(values, axis=0, keepdims=True)


def count_tables(length, bias_ref, inv_ref):
    length = length.astype(F32)
    for level in range(LEVELS):
        width = 2**level
        pad = 0 if level == 5 else 16
        count = SLOT // width + 2 * pad
        cell = lax.broadcasted_iota(jnp.int32, (count, 128), 0) - pad
        live = jnp.where(cell < 0, 0.0, length - (cell * width).astype(F32))
        rows = pl.ds(BASE[level], count)
        if level == 0:
            bias_ref[rows, :] = jnp.where(live > 0.0, 0.0, NEG)
        else:
            some = jnp.clip(live, 1.0, np.float32(width))
            bias_ref[rows, :] = jnp.where(live > 0.0, jnp.log(some), NEG)
            inv_ref[rows, :] = 1.0 / some


SKEW_F = 1
SKEW_B = 0
SKEW_P = 1
SKEW_E = 0
SKEW_M = 0


def interleave(chains, skew):
    live = dict(enumerate(chains))
    turn = 0
    while live:
        for j in sorted(live):
            if turn >= skew * j and next(live[j], live) is live:
                del live[j]
        turn += 1


def runs(touched, start, count):
    out = []
    for begin in range(start, start + count, 16):
        seen = begin in touched
        touched.add(begin)
        if out and out[-1][0] == seen:
            out[-1][2] += 16
        else:
            out.append([seen, begin, 16])
    return out


def window(ref, i, lanes):
    parts = []
    for start, count in window_parts(i):
        parts.append(ref[pl.ds(start, count), lanes])
    return jnp.concatenate(parts, axis=0)


def two_rows(block):
    first = lax.broadcasted_iota(jnp.int32, block.shape, 1) < 64
    zero = jnp.zeros_like(block)
    return jnp.concatenate([jnp.where(first, block, zero), jnp.where(first, zero, block)], axis=0)


def diagonal(block):
    n = block.shape[1] // 2
    return jnp.concatenate([block[:64, :n], block[64:, n:]], axis=0)


def four_rows(block):
    head = lax.broadcasted_iota(jnp.int32, block.shape, 1) // 64
    zero = jnp.zeros_like(block)
    return jnp.concatenate([jnp.where(head == j, block, zero) for j in range(4)], axis=0)


def corners(first, second):
    top = jnp.concatenate([first, jnp.zeros((first.shape[0], second.shape[1]), first.dtype)], axis=1)
    low = jnp.concatenate([jnp.zeros((second.shape[0], first.shape[1]), first.dtype), second], axis=1)
    return jnp.concatenate([top, low], axis=0)


def to_rows(level_one, others, index):
    row = lax.broadcasted_iota(jnp.int32, (8, TILE), 0)
    both = jnp.where(row == 0, jnp.broadcast_to(level_one, (8, TILE)), jnp.broadcast_to(others, (8, TILE)))
    return jnp.take_along_axis(both, index, axis=1)


def row_weights(weights, cell_rows):
    ones, rest = [], []
    for w in weights:
        wide = [jnp.broadcast_to(w[l : l + 1], (n, TILE)) for l, n in ((0, 64), (1, 32), (2, 16), (3, 8), (4, 8))]
        full = (jnp.concatenate(wide, axis=0) * cell_rows).astype(BF)
        ones.append(full[:64])
        rest.append(full[64:])
    return jnp.concatenate([corners(*ones), corners(*rest)], axis=0)


def keep_live(full, length, chunk, out_ref):
    row = lax.broadcasted_iota(jnp.int32, full.shape, 0) + 256 * chunk
    live = jnp.where(row < length, full, 0.0).astype(BF)
    out_ref[0, pl.ds(16 + 256 * chunk, 256), :] = live
    return live


def pack_cells(sums, chunk, out_ref, rough_ref, inv_ref):
    at = 0
    for level in range(1, LEVELS):
        count = 256 // 2**level
        pad = 0 if level == 5 else 16
        rows = pl.ds(BASE[level] + pad + count * chunk, count)
        cells = sums[at : at + count] * jnp.concatenate([inv_ref[rows, :]] * PAIRS, axis=1)
        if level == 5:
            rough_ref[pl.ds(8 * chunk, 8), :] = cells
        else:
            out_ref[0, rows, :] = cells.astype(BF)
        at += count


def forward_kernel(
    lens, x_ref, row_ref, w_ref, ends_ref,
    mask_ref, pool_q_ref, stat_ref, cell_rows_ref, pool_k_ref,
    n1_ref, q_ref, k_ref, v_ref, attn_ref, low_ref, lse_ref,
    bias_ref, inv_ref, rough_ref, tile_bias_ref,
):
    length = lens[pl.program_id(0)]
    count_tables(length, bias_ref, inv_ref)
    zeros = jnp.zeros((16, D), BF)
    for level in range(LEVELS - 1):
        cells = SLOT // 2**level
        for ref in (k_ref, v_ref):
            ref[0, pl.ds(BASE[level], 16), :] = zeros
            ref[0, pl.ds(BASE[level] + 16 + cells, 16), :] = zeros
    rough_k, rough_v = rough_ref.at[0], rough_ref.at[1]
    pre_gain, pre_shift = vector(row_ref, 0), vector(row_ref, 1)
    query_shift, value_shift = joined(ends_ref, 0, 2), joined(ends_ref, 2, 2)

    def project(chunk):
        rows = pl.ds(256 * chunk, 256)
        xhat, _ = norm_parts(x_ref[0, rows, :].astype(F32))
        n1 = (xhat * pre_gain + pre_shift).astype(BF)
        n1_ref[0, rows, :] = n1
        yield
        joint = [mm(n1, w_ref[t]) for t in range(2)]
        yield
        q, k, v = (jnp.concatenate([j[:, at : at + HALF] for j in joint], axis=1) for at in (0, HALF, 2 * HALF))
        q_ref[0, rows, :] = (q + query_shift).astype(BF) * BF(0.125)
        k = keep_live(k, length, chunk, k_ref)
        v = keep_live(v + value_shift, length, chunk, v_ref)
        yield
        k, v = mm(pool_k_ref[...], k), mm(pool_k_ref[...], v)
        yield
        pack_cells(k, chunk, k_ref, rough_k, inv_ref)
        pack_cells(v, chunk, v_ref, rough_v, inv_ref)
        yield

    interleave([project(chunk) for chunk in range(4)], SKEW_P)
    k_ref[0, pl.ds(BASE[5], 32), :] = rough_k[...].astype(BF)
    v_ref[0, pl.ds(BASE[5], 32), :] = rough_v[...].astype(BF)

    def tile(i, bias):
        rows = pl.ds(128 * i, 128)
        bias[...] = mask_ref[i] + window(bias_ref, i, slice(None))
        q = q_ref[0, rows, :]
        cells = mm(pool_q_ref[...], q).astype(BF)
        lse = {}

        def quad(u):
            lanes = slice(256 * u, 256 * u + 256)
            pairs = [slice(0, 128), slice(128, 256)]
            keys = window(k_ref.at[0], i, lanes)
            c_one, c_rest = four_rows(cells[:64, lanes]), four_rows(cells[64:, lanes])
            q_two = [two_rows(q[:, lanes][:, p]) for p in pairs]
            yield
            fine = [mm_nt(keys[:160, p], q_two[j]) for j, p in enumerate(pairs)]
            one, rest = mm_nt(keys[160:SPLIT], c_one), mm_nt(keys[SPLIT:], c_rest)
            yield
            one = [one[:, p] + bias[160:SPLIT] for p in pairs]
            rest = [rest[:, p] + bias[SPLIT:] for p in pairs]
            fine = [[f[:, p] + bias[:160] for p in pairs] for f in fine]
            top_one = [jnp.max(s, axis=0, keepdims=True) for s in one]
            top_rest = [jnp.max(s, axis=0, keepdims=True) for s in rest]
            top_fine = [[jnp.max(s, axis=0, keepdims=True) for s in f] for f in fine]
            yield
            one = [jnp.exp(s - top) for s, top in zip(one, top_one)]
            rest = [jnp.exp(s - top) for s, top in zip(rest, top_rest)]
            weights, shares, inverse = [], [], []
            row = lax.broadcasted_iota(jnp.int32, (8, TILE), 0)
            for j in range(2):
                sum_one = jnp.sum(one[j], axis=0, keepdims=True)
                sum_rest = jnp.sum(rest[j], axis=0, keepdims=True)
                pair_w, pair_p, pair_i = [], [], []
                for h in range(2):
                    tops = to_rows(top_one[j], top_rest[j], stat_ref[h])
                    sums = to_rows(sum_one, sum_rest, stat_ref[h])
                    top = jnp.maximum(top_fine[j][h], jnp.max(tops, axis=0, keepdims=True))
                    w = jnp.exp(tops - top).astype(BF).astype(F32)
                    p = jnp.exp(fine[j][h] - top)
                    total = jnp.sum(p, axis=0, keepdims=True)
                    total = total + jnp.sum(jnp.where(row < 5, w * sums, 0.0), axis=0, keepdims=True)
                    lse[4 * u + 2 * j + h] = top + jnp.log(total)
                    pair_w.append(w)
                    pair_p.append(p.astype(BF))
                    pair_i.append(1.0 / total)
                weights.append(row_weights(pair_w, cell_rows_ref[...]))
                shares.append(jnp.concatenate(pair_p, axis=1))
                inverse.append(jnp.concatenate(pair_i, axis=1))
            values = window(v_ref.at[0], i, lanes)
            v_fine = [values[:160, p].T for p in pairs]
            v_rough = [values[160:, p].T for p in pairs]
            yield
            mixed = [mm(v_rough[j], corners(one[j].astype(BF), rest[j].astype(BF))) for j in range(2)]
            out = [mm(v_fine[j], shares[j]) for j in range(2)]
            yield
            out = [out[j] + mm(mixed[j].astype(BF), weights[j]) for j in range(2)]
            yield
            for j in range(2):
                full = diagonal(out[j] * inverse[j]).T
                high = full.astype(BF)
                own = slice(256 * u + 128 * j, 256 * u + 128 * j + 128)
                attn_ref[0, rows, own] = high
                low_ref[0, rows, own] = (full - high.astype(F32)).astype(BF)
            if u == 1:
                lse_ref[0, :, rows] = jnp.concatenate([lse[h] for h in range(HEADS)], axis=0)
            yield

        return [quad(0), quad(1)]

    interleave([chain for i in range(TILES) for chain in tile(i, tile_bias_ref.at[i])], SKEW_F)


def middle_kernel(
    x_ref, attn_ref, cot_ref, w_ref, row_ref, ends_ref,
    out_ref, g1_ref, grad_ref, gvec_ref, gbup_ref,
    gwo_ref, gup_ref, gdown_ref,
):
    step = pl.program_id(0)

    @pl.when(step == 0)
    def _():
        gwo_ref[...] = jnp.zeros_like(gwo_ref)
        gup_ref[...] = jnp.zeros_like(gup_ref)
        gdown_ref[...] = jnp.zeros_like(gdown_ref)
        gvec_ref[...] = jnp.zeros_like(gvec_ref)
        gbup_ref[...] = jnp.zeros_like(gbup_ref)

    attn = attn_ref[...]
    cot = cot_ref[...]
    branch = sum(mm_nt(attn[:, HALF * t : HALF * t + HALF], w_ref[:, t, :, :HALF].reshape(D, HALF)) for t in range(2))
    y1 = x_ref[...].astype(F32) + (branch + vector(row_ref, 2))
    xhat, scale = norm_parts(y1)
    mid_gain = vector(row_ref, 3)
    n2 = (xhat * mid_gain + vector(row_ref, 4)).astype(BF)
    up_shift = joined(ends_ref, 4, 8)
    n2_t = n2.T
    cot_t = cot.T
    total = [y1 + vector(row_ref, 5), jnp.zeros_like(y1)]
    c = np.float32(np.sqrt(2.0 / np.pi))

    def hidden(part):
        cols = slice(256 * part, 256 * part + 256)
        at = HALF + 256 * (part % 4)
        up = w_ref[:, part // 4, :, at : at + 256].reshape(D, 256)
        at += FF // 2
        down_t = w_ref[:, part // 4, :, at : at + 256].reshape(D, 256)
        u = mm(n2, up) + up_shift[:, cols]
        dh = mm(cot, down_t)
        yield
        u2 = u * u
        t = jnp.tanh(u * (c + (c * 0.044715) * u2))
        h = 0.5 + 0.5 * t
        hid = (u * h).astype(BF)
        slope = h + (h - h * h) * (u * (2.0 * c + (6.0 * c * 0.044715) * u2))
        dhp = dh * slope
        dhp_b = dhp.astype(BF)
        gbup_ref[:, cols] += column_sum(dhp)
        yield
        total[0] = total[0] + mm_nt(hid, down_t)
        total[1] = total[1] + mm_nt(dhp_b, up)
        yield
        gdown_ref[:, cols] += mm(cot_t, hid)
        gup_ref[:, cols] += mm(n2_t, dhp_b)
        yield

    interleave([hidden(part) for part in range(8)], SKEW_M)
    out, dn2 = total
    out_ref[...] = out.astype(BF)
    cot_f = cot.astype(F32)
    dy1 = cot_f + norm_back(dn2, xhat, scale, mid_gain)
    g1 = dy1.astype(BF)
    g1_ref[...] = g1
    gwo_ref[...] += mm(g1.T, attn)
    gvec_ref[...] += jnp.concatenate(
        [column_sum(g1.astype(F32)), column_sum(dn2 * xhat), column_sum(dn2), column_sum(cot_f), jnp.zeros((4, D), F32)],
        axis=0,
    )


    @pl.when(step == pl.num_programs(0) - 1)
    def _():
        rows = D // grad_ref.shape[0]
        for t in range(2):
            at = 0
            for ref, width in ((gwo_ref, HALF), (gup_ref, FF // 2), (gdown_ref, FF // 2)):
                part = ref[:, width * t : width * t + width].astype(BF)
                grad_ref[:, t, :, at : at + width] = part.reshape(grad_ref.shape[0], rows, width)
                at += width


def backward_kernel(
    lens, x_ref, n1_ref, q_ref, k_ref, v_ref, attn_ref, low_ref, lse_ref, g1_ref,
    row_ref, w_ref, wo_t_ref,
    mask_ref, pool_q_ref, stat_ref, cell_rows_ref, expand_ref, spread_k_ref,
    dx_ref, gqkv_ref, gvec_ref,
    bias_ref, inv_ref, tile_bias_ref, dk_ref, dv_ref, dqkv_ref,
):
    step = pl.program_id(0)

    @pl.when(step == 0)
    def _():
        gqkv_ref[...] = jnp.zeros_like(gqkv_ref)
        gvec_ref[...] = jnp.zeros_like(gvec_ref)

    length = lens[step]
    count_tables(length, bias_ref, inv_ref)
    touched = (set(), set())
    head_of = lax.broadcasted_iota(jnp.int32, (HEADS, D), 1) // HD
    heads = (head_of == lax.broadcasted_iota(jnp.int32, (HEADS, D), 0)).astype(BF)

    def tile(i, bias):
        rows = pl.ds(128 * i, 128)
        bias[...] = mask_ref[i] + window(bias_ref, i, slice(None))
        q = q_ref[0, rows, :]
        cells = mm(pool_q_ref[...], q).astype(BF)
        da = jnp.concatenate([mm(g1_ref[0, rows, :], wo_t_ref[:, t, :, :HALF].reshape(D, HALF)) for t in range(2)], axis=1)
        da = da.astype(BF)
        product = da.astype(F32) * (attn_ref[0, rows, :].astype(F32) + low_ref[0, rows, :].astype(F32))
        high = product.astype(BF)
        delta = mm_nt(heads, high) + mm_nt(heads, (product - high.astype(F32)).astype(BF))
        lse = lse_ref[0, :, rows]

        def quad(u):
            lanes = slice(256 * u, 256 * u + 256)
            pairs = [slice(0, 128), slice(128, 256)]
            keys = window(k_ref.at[0], i, lanes)
            values = window(v_ref.at[0], i, lanes)
            c_one, c_rest = four_rows(cells[:64, lanes]), four_rows(cells[64:, lanes])
            q_two = [two_rows(q[:, lanes][:, p]) for p in pairs]
            d_two = [two_rows(da[:, lanes][:, p]) for p in pairs]
            yield
            fine = [mm_nt(keys[:160, p], q_two[j]) for j, p in enumerate(pairs)]
            one, rest = mm_nt(keys[160:SPLIT], c_one), mm_nt(keys[SPLIT:], c_rest)
            dp = [mm_nt(values[:160, p], d_two[j]) for j, p in enumerate(pairs)]
            yield
            ones, rests, weights, shares, slopes, rows_delta = [], [], [], [], [], []
            for j, pair in enumerate(pairs):
                s_one, s_rest = one[:, pair] + bias[160:SPLIT], rest[:, pair] + bias[SPLIT:]
                top_one, top_rest = jnp.max(s_one, axis=0, keepdims=True), jnp.max(s_rest, axis=0, keepdims=True)
                ones.append(jnp.exp(s_one - top_one))
                rests.append(jnp.exp(s_rest - top_rest))
                pair_w, pair_p, pair_s = [], [], []
                for h, p in enumerate(pairs):
                    head = 4 * u + 2 * j + h
                    own_lse, own_delta = lse[head : head + 1], delta[head : head + 1]
                    pair_w.append(jnp.exp(to_rows(top_one, top_rest, stat_ref[h]) - own_lse))
                    share = jnp.exp(fine[j][:, p] + bias[:160] - own_lse)
                    pair_s.append((share * (dp[j][:, p] - own_delta)).astype(BF))
                    pair_p.append(share.astype(BF))
                weights.append(row_weights(pair_w, cell_rows_ref[...]))
                shares.append(jnp.concatenate(pair_p, axis=1))
                slopes.append(jnp.concatenate(pair_s, axis=1))
                head = 4 * u + 2 * j
                both = jnp.concatenate([delta[head : head + 1], delta[head + 1 : head + 2]], axis=1)
                top = both.astype(BF).astype(F32)
                rows_delta.append(jnp.concatenate([top, both - top, jnp.zeros((6, 256), F32)], axis=0).astype(BF))
            k_fine = [keys[:160, p].T for p in pairs]
            k_rough = [keys[160:, p].T for p in pairs]
            yield
            d_cells = [mm(weights[j], d_two[j]).astype(BF) for j in range(2)]
            delta_cells = [jnp.sum(mm_nt(rows_delta[j], weights[j]), axis=0, keepdims=True) for j in range(2)]
            dv_fine = [mm(shares[j], d_two[j]) for j in range(2)]
            yield
            d_one, d_rest = (corners(d_cells[0][a : a + 128], d_cells[1][a : a + 128]) for a in (0, 128))
            dp_one, dp_rest = mm_nt(values[160:SPLIT], d_one), mm_nt(values[SPLIT:], d_rest)
            dk_fine = [mm(slopes[j], q_two[j]) for j in range(2)]
            dq = [mm(k_fine[j], slopes[j]) for j in range(2)]
            yield
            s_one = [(ones[j] * (dp_one[:, p] - delta_cells[j][:, :128])).astype(BF) for j, p in enumerate(pairs)]
            s_rest = [(rests[j] * (dp_rest[:, p] - delta_cells[j][:, 128:])).astype(BF) for j, p in enumerate(pairs)]
            dv_one = mm(jnp.concatenate([e.astype(BF) for e in ones], axis=1), d_one)
            dv_rest = mm(jnp.concatenate([e.astype(BF) for e in rests], axis=1), d_rest)
            yield
            dq_cells = [mm(k_rough[j], corners(s_one[j], s_rest[j])).astype(BF) for j in range(2)]
            dk_one = mm(jnp.concatenate(s_one, axis=1), c_one)
            dk_rest = mm(jnp.concatenate(s_rest, axis=1), c_rest)
            yield
            dq = [diagonal(dq[j] + mm(dq_cells[j], expand_ref[...])) * 0.125 for j in range(2)]
            dk = jnp.concatenate([jnp.concatenate(dk_fine, axis=1), dk_one, dk_rest], axis=0)
            dv = jnp.concatenate([jnp.concatenate(dv_fine, axis=1), dv_one, dv_rest], axis=0)
            at = 0
            for start, count in window_parts(i):
                for seen, begin, n in runs(touched[u], start, count):
                    part = pl.ds(begin, n)
                    for ref, grad in ((dk_ref, dk), (dv_ref, dv)):
                        block = grad[at + begin - start : at + begin - start + n]
                        ref[part, lanes] = ref[part, lanes] + block if seen else block
                at += count
            yield
            for j in range(2):
                at = 3 * HALF * u + 128 * j
                dqkv_ref[rows, at : at + 128] = dq[j].T.astype(BF)
            yield

        return [quad(0), quad(1)]

    interleave([chain for i in range(TILES) for chain in tile(i, tile_bias_ref.at[i])], SKEW_B)

    sums = []
    pre_gain = vector(row_ref, 0)

    def finish(chunk):
        rows = pl.ds(256 * chunk, 256)
        own = pl.ds(16 + 256 * chunk, 256)
        live = lax.broadcasted_iota(jnp.int32, (256, D), 0) + 256 * chunk < length
        wide = []
        for ref in (dk_ref, dv_ref):
            cells = []
            for level in range(1, LEVELS):
                count = 256 // 2**level
                pad = 0 if level == 5 else 16
                part = pl.ds(BASE[level] + pad + count * chunk, count)
                cells.append(ref[part, :] * jnp.concatenate([inv_ref[part, :]] * PAIRS, axis=1))
            cells.append(jnp.zeros((8, D), F32))
            wide.append(jnp.concatenate(cells, axis=0).astype(BF))
        yield
        wide = [mm(spread_k_ref[...], w) for w in wide]
        yield
        for ref, at, w in zip((dk_ref, dv_ref), (HALF, 2 * HALF), wide):
            grad = jnp.where(live, ref[own, :] + w, 0.0).astype(BF)
            dqkv_ref[rows, at : at + HALF] = grad[:, :HALF]
            dqkv_ref[rows, at + 3 * HALF : at + 4 * HALF] = grad[:, HALF:]
        yield
        parts = [dqkv_ref[rows, 3 * HALF * t : 3 * HALF * t + 3 * HALF] for t in range(2)]
        dn1 = mm_nt(parts[0], w_ref[0]) + mm_nt(parts[1], w_ref[1])
        xhat, scale = norm_parts(x_ref[0, rows, :].astype(F32))
        yield
        dx = g1_ref[0, rows, :].astype(F32) + norm_back(dn1, xhat, scale, pre_gain)
        dx_ref[0, rows, :] = dx.astype(BF)
        col = [column_sum(part.astype(F32)) for part in parts]
        sums.append(
            jnp.concatenate(
                [
                    column_sum(dn1 * xhat), column_sum(dn1),
                    jnp.concatenate([c[:, :HALF] for c in col], axis=1),
                    jnp.concatenate([c[:, 2 * HALF :] for c in col], axis=1),
                    jnp.zeros((4, D), F32),
                ],
                axis=0,
            )
        )
        yield

    interleave([finish(chunk) for chunk in range(4)], SKEW_E)
    gvec_ref[...] += sums[0] + sums[1] + sums[2] + sums[3]
    n1_t = n1_ref[0].T
    for t in range(2):
        gqkv_ref[t] += mm(n1_t, dqkv_ref[:, 3 * HALF * t : 3 * HALF * t + 3 * HALF])


def whole(shape):
    return pl.BlockSpec(shape, lambda *_: (0,) * len(shape))


def per_sequence(*shape):
    return pl.BlockSpec((1,) + shape, lambda s, *_: (s,) + (0,) * len(shape))


LIMIT = 60 * 1024 * 1024


def attention_forward(x, lens, row, w, ends, const):
    count = x.shape[0]
    return pl.pallas_call(
        forward_kernel,
        grid_spec=pltpu.PrefetchScalarGridSpec(
            num_scalar_prefetch=1,
            grid=(count,),
            in_specs=[
                per_sequence(SLOT, D), whole((SMALL, 128)), whole((2, D, 3 * HALF)), whole((2, 16, 128)),
                whole((TILES, WIN, TILE)), whole((TILE, TILE)), whole((2, 8, TILE)), whole((TILE, TILE)), whole((256, 256)),
            ],
            out_specs=[
                per_sequence(SLOT, D), per_sequence(SLOT, D), per_sequence(CELL_ROWS, D), per_sequence(CELL_ROWS, D),
                per_sequence(SLOT, D), per_sequence(SLOT, D), per_sequence(HEADS, SLOT),
            ],
            scratch_shapes=[
                pltpu.VMEM((CELL_ROWS, 128), F32), pltpu.VMEM((CELL_ROWS, 128), F32), pltpu.VMEM((2, 32, D), F32),
                pltpu.VMEM((TILES, WIN, TILE), F32),
            ],
        ),
        out_shape=[
            jax.ShapeDtypeStruct((count, SLOT, D), BF), jax.ShapeDtypeStruct((count, SLOT, D), BF),
            jax.ShapeDtypeStruct((count, CELL_ROWS, D), BF), jax.ShapeDtypeStruct((count, CELL_ROWS, D), BF),
            jax.ShapeDtypeStruct((count, SLOT, D), BF), jax.ShapeDtypeStruct((count, SLOT, D), BF),
            jax.ShapeDtypeStruct((count, HEADS, SLOT), F32),
        ],
        compiler_params=pltpu.CompilerParams(vmem_limit_bytes=LIMIT),
        cost_estimate=pl.CostEstimate(flops=count * 30 * 10**9, bytes_accessed=count * 10**7, transcendentals=0),
        name="attention_forward",
    )(lens, x, row, w, ends, const["mask"], const["pool_q"], const["stat"], const["cell_rows"], const["pool_k"])


ROWS = 512


def middle(x, attn, cot, w, row, ends):
    total = x.shape[0]
    rows = pl.BlockSpec((ROWS, D), lambda s: (s, 0))
    return pl.pallas_call(
        middle_kernel,
        grid=(total // ROWS,),
        in_specs=[
            rows, rows, rows, whole(w.shape), whole((SMALL, 128)), whole((2, 16, 128)),
        ],
        out_specs=[rows, rows, whole(w.shape), whole((8, D)), whole((1, FF))],
        scratch_shapes=[pltpu.VMEM((D, D), F32), pltpu.VMEM((D, FF), F32), pltpu.VMEM((D, FF), F32)],
        out_shape=[
            jax.ShapeDtypeStruct((total, D), BF), jax.ShapeDtypeStruct((total, D), BF), jax.ShapeDtypeStruct(w.shape, BF),
            jax.ShapeDtypeStruct((8, D), F32), jax.ShapeDtypeStruct((1, FF), F32),
        ],
        compiler_params=pltpu.CompilerParams(vmem_limit_bytes=LIMIT),
        name="middle",
    )(x, attn, cot, w, row, ends)


def attention_backward(x, lens, n1, q, k, v, attn, low, lse, g1, row, w, rest, const):
    count = x.shape[0]
    wo_t = pl.BlockSpec(rest.shape[:3] + (HALF,), lambda *_: (0, 0, 0, 0))
    return pl.pallas_call(
        backward_kernel,
        grid_spec=pltpu.PrefetchScalarGridSpec(
            num_scalar_prefetch=1,
            grid=(count,),
            in_specs=[
                per_sequence(SLOT, D), per_sequence(SLOT, D), per_sequence(SLOT, D),
                per_sequence(CELL_ROWS, D), per_sequence(CELL_ROWS, D), per_sequence(SLOT, D), per_sequence(SLOT, D),
                per_sequence(HEADS, SLOT), per_sequence(SLOT, D),
                whole((SMALL, 128)), whole((2, D, 3 * HALF)), wo_t,
                whole((TILES, WIN, TILE)), whole((TILE, TILE)), whole((2, 8, TILE)), whole((TILE, TILE)),
                whole((256, 256)), whole((256, 256)),
            ],
            out_specs=[per_sequence(SLOT, D), whole((2, D, 3 * HALF)), whole((8, D))],
            scratch_shapes=[
                pltpu.VMEM((CELL_ROWS, 128), F32), pltpu.VMEM((CELL_ROWS, 128), F32), pltpu.VMEM((TILES, WIN, TILE), F32),
                pltpu.VMEM((CELL_ROWS, D), F32), pltpu.VMEM((CELL_ROWS, D), F32), pltpu.VMEM((SLOT, 3 * D), BF),
            ],
        ),
        out_shape=[
            jax.ShapeDtypeStruct((count, SLOT, D), BF), jax.ShapeDtypeStruct((2, D, 3 * HALF), F32),
            jax.ShapeDtypeStruct((8, D), F32),
        ],
        compiler_params=pltpu.CompilerParams(vmem_limit_bytes=LIMIT),
        cost_estimate=pl.CostEstimate(flops=count * 40 * 10**9, bytes_accessed=count * 10**7, transcendentals=0),
        name="attention_backward",
    )(
        lens, x, n1, q, k, v, attn, low, lse, g1, row, w, rest,
        const["mask"], const["pool_q"], const["stat"], const["cell_rows"], const["expand"], const["spread_k"],
    )


def bits_of(count):
    return count.bit_length() - 1


def all_bits(n_dp, n_t):
    return [("tensor", b) for b in reversed(range(bits_of(n_t)))] + [("dp", b) for b in reversed(range(bits_of(n_dp)))]


def gather_orders(n_dp, n_t):
    far = [("dp", b) for b in reversed(range(2, bits_of(n_dp)))]
    near = [("dp", 1)]
    side = [("tensor", b) for b in reversed(range(bits_of(n_t)))]
    core_bit = [("dp", 0)]
    return far + near + side + core_bit, far + side + near + core_bit


def own_bit(bit):
    axis, b = bit
    return (lax.axis_index(axis) // 2**b) % 2


def partner(bit):
    axis, b = bit
    return {axis: lax.axis_index(axis) + (1 - 2 * own_bit(bit)) * 2**b}


def meet(bits):
    barrier = pltpu.get_barrier_semaphore()
    for bit in bits:
        pl.semaphore_signal(barrier, inc=1, device_id=partner(bit), device_id_type=pl.DeviceIdType.MESH)
    pl.semaphore_wait(barrier, len(bits))


def halves(width):
    if width % 256:
        return [(0, width)]
    return [(0, width // 2), (width // 2, width // 2)]


def gather_kernel(
    bits, orders, parts, *refs
):
    *shard_refs, ends_ref, out_ref, all_ends_ref, own_sems, send_sems, recv_sems, ends_own_sem, ends_sems = refs
    slot = out_ref.at[tuple(own_bit(bit) for bit in bits)]
    width = shard_refs[0].shape[1]
    own = [
        pltpu.make_async_copy(ref, slot.at[:, pl.ds(width * j, width)], own_sems.at[j]) for j, ref in enumerate(shard_refs)
    ]
    for copy in own:
        copy.start()
    side = [bit for bit in bits if bit[0] == "tensor"]
    own_ends = pltpu.make_async_copy(ends_ref.at[pl.ds(0, 16)], all_ends_ref.at[tuple(own_bit(bit) for bit in side)], ends_own_sem)
    own_ends.start()
    meet(bits)
    pending = []
    own_ends.wait()
    for copy in own:
        copy.wait()

    def ends_copy(step):
        place = all_ends_ref.at[tuple(slice(None) if j < step else own_bit(bit) for j, bit in enumerate(side))]
        return pltpu.make_async_remote_copy(
            src_ref=place, dst_ref=place, send_sem=ends_sems.at[0, step], recv_sem=ends_sems.at[1, step],
            device_id=partner(side[step]), device_id_type=pl.DeviceIdType.MESH,
        )

    if side:
        ends_copy(0).start()
    for step in range(len(bits)):
        for part, (at, width) in enumerate(parts):
            order = orders[part]
            done = order[:step]
            index = tuple(slice(None) if bit in done else own_bit(bit) for bit in bits)
            place = out_ref.at[index + (slice(None), pl.ds(at, width))]
            if step > 0:
                pending[(step - 1) * len(parts) + part].wait_recv()
            copy = pltpu.make_async_remote_copy(
                src_ref=place, dst_ref=place,
                send_sem=send_sems.at[step, part], recv_sem=recv_sems.at[step, part],
                device_id=partner(order[step]), device_id_type=pl.DeviceIdType.MESH,
            )
            copy.start()
            pending.append(copy)
    for copy in pending[-len(parts) :]:
        copy.wait_recv()
    for step in range(len(side)):
        ends_copy(step).wait_recv()
        if step + 1 < len(side):
            ends_copy(step + 1).start()
    for step in range(len(side)):
        ends_copy(step).wait_send()
    for copy in pending:
        copy.wait_send()


def gather(shards, ends, n_dp, n_t):
    rows, width = shards[0].shape[0], len(shards) * shards[0].shape[1]
    bits, orders, parts = all_bits(n_dp, n_t), gather_orders(n_dp, n_t), halves(width)
    side = bits_of(n_t)
    anywhere = pl.BlockSpec(memory_space=pl.ANY)
    out, all_ends = pl.pallas_call(
        functools.partial(gather_kernel, bits, orders, parts),
        in_specs=[anywhere] * (len(shards) + 1),
        out_specs=[anywhere, anywhere],
        out_shape=[
            jax.ShapeDtypeStruct((2,) * len(bits) + (rows, width), BF),
            jax.ShapeDtypeStruct((2,) * side + (16, 128), BF),
        ],
        scratch_shapes=[
            pltpu.SemaphoreType.DMA((len(shards),)), pltpu.SemaphoreType.DMA((len(bits), len(parts))),
            pltpu.SemaphoreType.DMA((len(bits), len(parts))), pltpu.SemaphoreType.DMA,
            pltpu.SemaphoreType.DMA((2, max(side, 1))),
        ],
        compiler_params=pltpu.CompilerParams(collective_id=0, has_side_effects=True),
        name="gather",
    )(*shards, ends)
    return out.reshape(n_t, n_dp, rows, width), all_ends.reshape(n_t, 16, 128)


def reduce_kernel(bits, orders, parts, n_t, grad_ref, pre_ref, mid_ref, up_ref, out_ref, own_ref, *scratch):
    steps, count = len(bits), len(parts)
    sends, recvs, sums = (scratch[j * steps * count : (j + 1) * steps * count] for j in range(3))
    vec_out_ref, vec_recv, send_sems, recv_sems, vec_send_sems, vec_recv_sems = scratch[3 * steps * count :]
    meet(bits)
    vec_out_ref[0:4, :] = pre_ref[0:4, :]
    vec_out_ref[4:8, :] = mid_ref[0:4, :]
    for r in range(4):
        vec_out_ref[8 + r : 9 + r, :] = up_ref[:, D * r : D * r + D]
    vec_out_ref[12:16, :] = jnp.zeros((4, D), F32)

    def vec_copy(step):
        return pltpu.make_async_remote_copy(
            src_ref=vec_recv.at[2 * step], dst_ref=vec_recv.at[2 * step + 1],
            send_sem=vec_send_sems.at[step], recv_sem=vec_recv_sems.at[step],
            device_id=partner(orders[0][steps - 1 - step]), device_id_type=pl.DeviceIdType.MESH,
        )

    def copy_of(step, part):
        j = step * count + part
        return pltpu.make_async_remote_copy(
            src_ref=sends[j], dst_ref=recvs[j], send_sem=send_sems.at[step, part], recv_sem=recv_sems.at[step, part],
            device_id=partner(orders[part][steps - 1 - step]), device_id_type=pl.DeviceIdType.MESH,
        )

    def pieces(step, part):
        order = orders[part][::-1]
        left = [bit for bit in bits if bit not in order[:step]]
        j = left.index(order[step])
        low = 2 ** (len(left) - 1 - j)
        mine = own_bit(order[step])
        out = []
        for a in range(2**j):
            for c in range(low):
                out.append(((a * 2 + 1 - mine) * low + c, (a * 2 + mine) * low + c, a * low + c))
        at, width = parts[part]
        source = sums[(step - 1) * count + part] if step else grad_ref.at[:, :, pl.ds(at, width)]
        return out, source

    for step in range(steps):
        vec_recv[2 * step] = vec_out_ref[...]
        vec_copy(step).start()
        for part in range(count):
            blocks, source = pieces(step, part)
            for away, _, to in blocks:
                sends[step * count + part][to] = source[away].astype(BF)
            copy_of(step, part).start()
        for part in range(count):
            copy_of(step, part).wait_recv()
            blocks, source = pieces(step, part)
            for _, keep, to in blocks:
                total = source[keep] + recvs[step * count + part][to].astype(F32)
                if step == steps - 1:
                    at, width = parts[part]
                    out_ref[:, at : at + width] = total
                else:
                    sums[step * count + part][to] = total
        vec_copy(step).wait_recv()
        vec_out_ref[...] += vec_recv[2 * step + 1]
    own_ref[...] = jnp.zeros_like(own_ref)
    own_ref[0:8, 0:D] = vec_out_ref[0:8, :]
    t = lax.axis_index("tensor")
    for row in (2, 3):
        n = D // n_t
        full = vec_out_ref[row : row + 1, :]
        mine = full[:, :n]
        for j in range(1, n_t):
            mine = jnp.where(t == j, full[:, n * j : n * j + n], mine)
        own_ref[row : row + 1, 0:n] = mine
    n = FF // n_t
    full = jnp.concatenate([vec_out_ref[8 + r : 9 + r, :] for r in range(4)], axis=1)
    mine = full[:, :n]
    for j in range(1, n_t):
        mine = jnp.where(t == j, full[:, n * j : n * j + n], mine)
    own_ref[8:9, 0:n] = mine
    for step in range(steps):
        vec_copy(step).wait_send()
        for part in range(count):
            copy_of(step, part).wait_send()


def reduce(grad, pre, mid, up, n_dp, n_t):
    rows, width = grad.shape[2:]
    bits, orders, parts = all_bits(n_dp, n_t), gather_orders(n_dp, n_t), halves(width)
    steps = len(bits)
    blocks = [(2 ** (steps - 1 - step), rows, w) for step in range(steps) for _, w in parts]
    sems = pltpu.SemaphoreType.DMA
    vmem = pl.BlockSpec(memory_space=pltpu.VMEM)
    return pl.pallas_call(
        functools.partial(reduce_kernel, bits, orders, parts, n_t),
        in_specs=[vmem] * 4,
        out_specs=[vmem, vmem],
        out_shape=[jax.ShapeDtypeStruct((rows, width), F32), jax.ShapeDtypeStruct((16, max(D, FF // n_t)), F32)],
        scratch_shapes=[pltpu.VMEM(b, BF) for b in blocks] * 2
        + [pltpu.VMEM(b, F32) for b in blocks]
        + [
            pltpu.VMEM((16, D), F32), pltpu.VMEM((2 * steps, 16, D), F32), sems((steps, len(parts))), sems((steps, len(parts))),
            sems((steps,)), sems((steps,)),
        ],
        compiler_params=pltpu.CompilerParams(collective_id=1, has_side_effects=True, vmem_limit_bytes=LIMIT),
        name="reduce",
    )(grad.reshape(n_t * n_dp, rows, width), pre, mid, up)


def to_pairs(grid, widths):
    n_t, n_dp, rows, _ = grid.shape
    grid = grid.reshape(n_t, n_dp * rows, -1)
    if n_t == 2:
        return grid
    out, at = [], 0
    for width in widths:
        part = grid[:, :, at : at + width].reshape(2, n_t // 2, D, width)
        out.append(part.transpose(0, 2, 1, 3).reshape(2, D, n_t // 2 * width))
        at += width
    return jnp.concatenate(out, axis=2)


def from_pairs(grid, widths, n_dp, n_t):
    if n_t != 2:
        out, at = [], 0
        for width in widths:
            full = width * n_t // 2
            part = grid[:, :, at : at + full].reshape(2, D, n_t // 2, width)
            out.append(part.transpose(0, 2, 1, 3).reshape(n_t, D, width))
            at += full
        grid = jnp.concatenate(out, axis=2)
    return grid.reshape(n_t, n_dp, D // n_dp, -1)


def own_sequences(values, lengths, tensor_count):
    micro, rows, width = values[0].shape
    t = lax.axis_index("tensor")
    if rows % SLOT == 0:
        per = rows // SLOT
        own = lax.dynamic_slice_in_dim(lengths, t * per, per, 1).reshape(-1)
        return [v.reshape(micro * per, SLOT, width) for v in values], own
    pieces = SLOT // rows
    assert micro == pieces
    groups = [[g * pieces + j for j in range(pieces)] for g in range(tensor_count // pieces)]
    out = [lax.all_to_all(v, "tensor", 0, 1, axis_index_groups=groups, tiled=True) for v in values]
    sequence = lax.dynamic_slice(lengths, (t % pieces, t // pieces), (1, 1))
    return out, sequence.reshape(-1)


def own_rows(values, shape, tensor_count):
    micro, rows, width = shape
    if rows % SLOT == 0:
        return [v.reshape(shape) for v in values]
    pieces = SLOT // rows
    groups = [[g * pieces + j for j in range(pieces)] for g in range(tensor_count // pieces)]
    return [
        lax.all_to_all(v, "tensor", 1, 0, axis_index_groups=groups, tiled=True).reshape(shape) for v in values
    ]


def core(x, lens, cot, row, w, ends, rest):
    const = {name: jnp.asarray(value) for name, value in constants().items()}
    count = x.shape[0]
    flat = (count * SLOT, D)
    n1, q, k, v, attn, low, lse = attention_forward(x, lens, row, w, ends, const)
    out, g1, grad_rest, mid_vec, gbup = middle(
        x.reshape(flat), attn.reshape(flat), cot.reshape(flat), rest, row, ends
    )
    dx, gqkv, pre_vec = attention_backward(
        x, lens, n1, q, k, v, attn, low, lse, g1.reshape(count, SLOT, D), row, w, rest, const
    )
    return out, dx, grad_rest, mid_vec, gbup, gqkv, pre_vec


def on_device(
    inputs, lengths, pre_gain, pre_shift, query_weight, key_weight, value_weight, query_bias, value_bias,
    output_weight, output_bias, mid_gain, mid_shift, up_weight, up_bias, down_weight, down_bias, cotangent,
):
    n_dp, n_t = lax.axis_size("dp"), lax.axis_size("tensor")
    t = lax.axis_index("tensor")
    (x, cot), lens = own_sequences([inputs, cotangent], lengths, n_t)

    n_q, n_f = query_weight.shape[1], up_weight.shape[1]
    second = jnp.concatenate([output_weight.T, up_weight, down_weight.T], axis=1)
    small = ((query_bias, 0), (value_bias, n_q), (up_bias, 2 * n_q))
    vectors = (pre_gain, pre_shift, output_bias, mid_gain, mid_shift, down_bias)
    small += tuple((v, 2048 + D * j) for j, v in enumerate(vectors))
    row = sum(lax.pad(v, jnp.zeros((), BF), [(at, SMALL * 128 - at - v.shape[0], 0)]) for v, at in small)
    row = row.reshape(SMALL, 128)
    first = (query_weight, key_weight, value_weight)
    if n_q % 128:
        first = (jnp.concatenate(first, axis=1),)
    w, ends = gather(first, row, n_dp, n_t)
    w = to_pairs(w, (n_q,) * 3)
    rest = lax.all_gather(second, ("dp", "tensor"), axis=0, tiled=False)
    rest = rest.reshape(n_dp, n_t, D // n_dp, -1)
    if n_t != 2:
        rest = to_pairs(rest.transpose(1, 0, 2, 3), (n_q, n_f, n_f)).reshape(2, 16, 32, REST).transpose(1, 0, 2, 3)
        flat = ends.reshape(n_t, -1)
        parts = [flat[:, a : a + n].reshape(2, -1) for a, n in ((0, n_q), (n_q, n_q), (2 * n_q, n_f))]
        ends = jnp.concatenate(parts + [jnp.zeros((2, 512), ends.dtype)], axis=1).reshape(2, 16, 128)
    out, dx, grad_rest, mid_vec, gbup, gqkv, pre_vec = core(x, lens, cot, row, w, ends, rest)
    if n_t != 2:
        grad_rest = grad_rest.transpose(1, 0, 2, 3).reshape(2, D, REST)
        grad_rest = from_pairs(grad_rest, (n_q, n_f, n_f), n_dp, n_t).transpose(1, 0, 2, 3)
    grad_rest = grad_rest.reshape(n_dp * n_t, D // n_dp, -1)
    grad_rest = lax.psum_scatter(grad_rest, ("dp", "tensor"), scatter_dimension=0, tiled=False).astype(F32)
    grad_first, vec = reduce(from_pairs(gqkv, (n_q,) * 3, n_dp, n_t), pre_vec, mid_vec, gbup, n_dp, n_t)
    grad_q, grad_k, grad_v = (grad_first[:, n_q * j : n_q * j + n_q] for j in range(3))
    grad_o, grad_up, grad_down = grad_rest[:, :n_q].T, grad_rest[:, n_q : n_q + n_f], grad_rest[:, n_q + n_f :].T

    out, dx = own_rows([out.reshape(x.shape), dx], inputs.shape, n_t)
    each = [vec[j, :D] for j in range(8)]
    return (
        out, dx, each[0], each[1], grad_q, grad_k, grad_v, vec[2, :n_q], vec[3, :n_q], grad_o, each[4], each[5], each[6],
        grad_up, vec[8, :n_f], grad_down, each[7],
    )


def solution(mesh):
    rows = P(None, ("dp", "tensor"), None)
    by_row, by_column = P("dp", "tensor"), P("tensor", "dp")
    in_specs = (
        rows, P(None, "dp"), P(), P(), by_row, by_row, by_row, P("tensor"), P("tensor"), by_column, P(), P(), P(),
        by_row, P("tensor"), by_column, P(), rows,
    )
    out_specs = (
        rows, rows, P(), P(), by_row, by_row, by_row, P("tensor"), P("tensor"), by_column, P(), P(), P(),
        by_row, P("tensor"), by_column, P(),
    )
    return jax.shard_map(on_device, mesh=mesh, in_specs=in_specs, out_specs=out_specs, check_vma=False)
```

```python
import functools

import jax
import jax.numpy as jnp
import ml_dtypes
import numpy as np
from jax import lax
from jax.experimental import pallas as pl
from jax.experimental.pallas import tpu as pltpu
from jax.sharding import PartitionSpec as P

D = 512
HD = 64
FF = 2048
NR = 16
LEVELS = 6
SLOT = 1024
TILE = 128
TILES = SLOT // TILE
PAIRS = D // 128
HEADS = D // HD
HALF = D // 2
REST = HALF + FF
SMALL = 40
EPS = 1e-05
NEG = -1e30

BASE = (0, 1056, 1600, 1888, 2048, 2144)
CELL_ROWS = 2176
WIN_ROWS = (160, 96, 64, 32, 32, 16)
WIN_AT = (0, 160, 256, 320, 352, 384)
WIN = 400
COARSE = WIN - 160
LANE_AT = (0, 0, 0, 32, 48, 56)
SPLIT = WIN_AT[2]
BF = jnp.bfloat16
F32 = jnp.float32


def window_parts(i):
    two, four = i // 2, i // 4
    return (
        (128 * i, 160),
        (BASE[1] + 64 * i, 96),
        (BASE[2] + 32 * i, 64),
        (BASE[3] + 16 * i, 16),
        (BASE[3] + 16 * i + 32, 16),
        (BASE[4] + 16 * two, 16),
        (BASE[4] + 16 * two + 32, 16),
        (BASE[5] + 16 * (1 - four), 16),
    )


def mask_table():
    table = np.full((TILES, WIN, TILE), NEG, np.float32)
    for i in range(TILES):
        at = 0
        for start, count in window_parts(i):
            level = max(l for l in range(LEVELS) if WIN_AT[l] <= at)
            pad = 0 if level == 5 else 16
            cell = (start - BASE[level] - pad + np.arange(count))[:, None]
            here = TILE >> level
            query = (((128 * i) >> level) + np.arange(here))[None, :]
            good = np.abs(cell // 16 - query // 16) <= 1
            if level > 0:
                good &= np.abs((2 * cell) // 16 - (2 * query) // 16) > 1
            for head in range(1 if level == 0 else 2):
                lane = 64 * head + LANE_AT[level]
                table[i, at : at + count, lane : lane + here] = np.where(good, 0.0, NEG)
            at += count
    return table


def constants():
    t = np.arange(TILE)
    pool_q = np.zeros((TILE, TILE), np.float32)
    stat = np.zeros((2, 8, TILE), np.int32)
    expand = np.zeros((256, 256), np.float32)
    pool_k = np.zeros((256, 256), np.float32)
    t2 = np.arange(256)
    at = 0
    for level in range(1, LEVELS):
        width = 2**level
        half = 0 if level == 1 else 64
        pool_q[half + LANE_AT[level] + t // width, t] = 1.0 / width
        for head in range(2):
            stat[head, level - 1 :] = 64 * head + LANE_AT[level] + t // width
            expand[2 * half + 64 * head + LANE_AT[level] + t // width, 128 * head + t] = 1.0 / width
        pool_k[at + t2 // width, t2] = 1.0
        at += 256 // width
    half = ml_dtypes.bfloat16
    return {
        "mask": mask_table(),
        "pool_q": pool_q.astype(half),
        "stat": stat,
        "cell_rows": (pool_q > 0).astype(np.float32),
        "expand": expand.astype(half),
        "pool_k": pool_k.astype(half),
        "spread_k": pool_k.T.copy().astype(half),
    }


def mm(a, b):
    return lax.dot_general(a, b, (((1,), (0,)), ((), ())), preferred_element_type=F32)


def mm_nt(a, b):
    return lax.dot_general(a, b, (((1,), (1,)), ((), ())), preferred_element_type=F32)


def mm_tn(a, b):
    return lax.dot_general(a, b, (((0,), (0,)), ((), ())), preferred_element_type=F32)


def norm_parts(values):
    centre = values - jnp.mean(values, axis=-1, keepdims=True)
    spread = jnp.mean(centre * centre, axis=-1, keepdims=True)
    scale = lax.rsqrt(spread + EPS)
    return centre * scale, scale


def norm_back(grad, xhat, scale, gain):
    e = grad * gain
    return (e - jnp.mean(e, axis=-1, keepdims=True) - xhat * jnp.mean(e * xhat, axis=-1, keepdims=True)) * scale


def joined(ref, first, count):
    parts = [ref[t, r : r + 1, :].astype(F32) for t in range(2) for r in range(first, first + count)]
    return jnp.concatenate(parts, axis=1)


def vector(ref, j):
    return jnp.concatenate([ref[16 + 4 * j + r : 17 + 4 * j + r, :].astype(F32) for r in range(4)], axis=1)


def column_sum(values):
    return jnp.sum(values, axis=0, keepdims=True)


def count_tables(length, bias_ref, inv_ref):
    length = length.astype(F32)
    for level in range(LEVELS):
        width = 2**level
        pad = 0 if level == 5 else 16
        count = SLOT // width + 2 * pad
        cell = lax.broadcasted_iota(jnp.int32, (count, 128), 0) - pad
        live = jnp.where(cell < 0, 0.0, length - (cell * width).astype(F32))
        rows = pl.ds(BASE[level], count)
        if level == 0:
            bias_ref[rows, :] = jnp.where(live > 0.0, 0.0, NEG)
        else:
            some = jnp.clip(live, 1.0, np.float32(width))
            bias_ref[rows, :] = jnp.where(live > 0.0, jnp.log(some), NEG)
            inv_ref[rows, :] = 1.0 / some


SKEW_F = 1
SKEW_B = 0
SKEW_P = 1
SKEW_E = 0
SKEW_M = 0


def interleave(chains, skew):
    live = dict(enumerate(chains))
    turn = 0
    while live:
        for j in sorted(live):
            if turn >= skew * j and next(live[j], live) is live:
                del live[j]
        turn += 1


def runs(touched, start, count):
    out = []
    for begin in range(start, start + count, 16):
        seen = begin in touched
        touched.add(begin)
        if out and out[-1][0] == seen:
            out[-1][2] += 16
        else:
            out.append([seen, begin, 16])
    return out


def window(ref, i, lanes):
    parts = []
    for start, count in window_parts(i):
        parts.append(ref[pl.ds(start, count), lanes])
    return jnp.concatenate(parts, axis=0)


def two_rows(block):
    first = lax.broadcasted_iota(jnp.int32, block.shape, 1) < 64
    zero = jnp.zeros_like(block)
    return jnp.concatenate([jnp.where(first, block, zero), jnp.where(first, zero, block)], axis=0)


def diagonal(block):
    n = block.shape[1] // 2
    return jnp.concatenate([block[:64, :n], block[64:, n:]], axis=0)


def four_rows(block):
    head = lax.broadcasted_iota(jnp.int32, block.shape, 1) // 64
    zero = jnp.zeros_like(block)
    return jnp.concatenate([jnp.where(head == j, block, zero) for j in range(4)], axis=0)


def corners(first, second):
    top = jnp.concatenate([first, jnp.zeros((first.shape[0], second.shape[1]), first.dtype)], axis=1)
    low = jnp.concatenate([jnp.zeros((second.shape[0], first.shape[1]), first.dtype), second], axis=1)
    return jnp.concatenate([top, low], axis=0)


def to_rows(level_one, others, index):
    row = lax.broadcasted_iota(jnp.int32, (8, TILE), 0)
    both = jnp.where(row == 0, jnp.broadcast_to(level_one, (8, TILE)), jnp.broadcast_to(others, (8, TILE)))
    return jnp.take_along_axis(both, index, axis=1)


def row_weights(weights, cell_rows):
    ones, rest = [], []
    for w in weights:
        wide = [jnp.broadcast_to(w[l : l + 1], (n, TILE)) for l, n in ((0, 64), (1, 32), (2, 16), (3, 8), (4, 8))]
        full = (jnp.concatenate(wide, axis=0) * cell_rows).astype(BF)
        ones.append(full[:64])
        rest.append(full[64:])
    return jnp.concatenate([corners(*ones), corners(*rest)], axis=0)


def keep_live(full, length, chunk, out_ref):
    row = lax.broadcasted_iota(jnp.int32, full.shape, 0) + 256 * chunk
    live = jnp.where(row < length, full, 0.0).astype(BF)
    out_ref[0, pl.ds(16 + 256 * chunk, 256), :] = live
    return live


def pack_cells(sums, chunk, out_ref, rough_ref, inv_ref):
    at = 0
    for level in range(1, LEVELS):
        count = 256 // 2**level
        pad = 0 if level == 5 else 16
        rows = pl.ds(BASE[level] + pad + count * chunk, count)
        cells = sums[at : at + count] * jnp.concatenate([inv_ref[rows, :]] * PAIRS, axis=1)
        if level == 5:
            rough_ref[pl.ds(8 * chunk, 8), :] = cells
        else:
            out_ref[0, rows, :] = cells.astype(BF)
        at += count


def forward_kernel(
    lens, x_ref, row_ref, w_ref, ends_ref,
    mask_ref, pool_q_ref, stat_ref, cell_rows_ref, pool_k_ref,
    n1_ref, q_ref, k_ref, v_ref, attn_ref, low_ref, lse_ref,
    bias_ref, inv_ref, rough_ref, tile_bias_ref,
):
    length = lens[pl.program_id(0)]
    count_tables(length, bias_ref, inv_ref)
    zeros = jnp.zeros((16, D), BF)
    for level in range(LEVELS - 1):
        cells = SLOT // 2**level
        for ref in (k_ref, v_ref):
            ref[0, pl.ds(BASE[level], 16), :] = zeros
            ref[0, pl.ds(BASE[level] + 16 + cells, 16), :] = zeros
    rough_k, rough_v = rough_ref.at[0], rough_ref.at[1]
    pre_gain, pre_shift = vector(row_ref, 0), vector(row_ref, 1)
    query_shift, value_shift = joined(ends_ref, 0, 2), joined(ends_ref, 2, 2)

    def project(chunk):
        rows = pl.ds(256 * chunk, 256)
        xhat, _ = norm_parts(x_ref[0, rows, :].astype(F32))
        n1 = (xhat * pre_gain + pre_shift).astype(BF)
        n1_ref[0, rows, :] = n1
        yield
        joint = [mm(n1, w_ref[t]) for t in range(2)]
        yield
        q, k, v = (jnp.concatenate([j[:, at : at + HALF] for j in joint], axis=1) for at in (0, HALF, 2 * HALF))
        q_ref[0, rows, :] = (q + query_shift).astype(BF) * BF(0.125)
        k = keep_live(k, length, chunk, k_ref)
        v = keep_live(v + value_shift, length, chunk, v_ref)
        yield
        k, v = mm(pool_k_ref[...], k), mm(pool_k_ref[...], v)
        yield
        pack_cells(k, chunk, k_ref, rough_k, inv_ref)
        pack_cells(v, chunk, v_ref, rough_v, inv_ref)
        yield

    interleave([project(chunk) for chunk in range(4)], SKEW_P)
    k_ref[0, pl.ds(BASE[5], 32), :] = rough_k[...].astype(BF)
    v_ref[0, pl.ds(BASE[5], 32), :] = rough_v[...].astype(BF)

    def tile(i, bias):
        rows = pl.ds(128 * i, 128)
        bias[...] = mask_ref[i] + window(bias_ref, i, slice(None))
        q = q_ref[0, rows, :]
        cells = mm(pool_q_ref[...], q).astype(BF)
        lse = {}

        def quad(u):
            lanes = slice(256 * u, 256 * u + 256)
            pairs = [slice(0, 128), slice(128, 256)]
            keys = window(k_ref.at[0], i, lanes)
            c_one, c_rest = four_rows(cells[:64, lanes]), four_rows(cells[64:, lanes])
            q_two = [two_rows(q[:, lanes][:, p]) for p in pairs]
            yield
            fine = [mm_nt(keys[:160, p], q_two[j]) for j, p in enumerate(pairs)]
            one, rest = mm_nt(keys[160:SPLIT], c_one), mm_nt(keys[SPLIT:], c_rest)
            yield
            one = [one[:, p] + bias[160:SPLIT] for p in pairs]
            rest = [rest[:, p] + bias[SPLIT:] for p in pairs]
            fine = [[f[:, p] + bias[:160] for p in pairs] for f in fine]
            top_one = [jnp.max(s, axis=0, keepdims=True) for s in one]
            top_rest = [jnp.max(s, axis=0, keepdims=True) for s in rest]
            top_fine = [[jnp.max(s, axis=0, keepdims=True) for s in f] for f in fine]
            yield
            one = [jnp.exp(s - top) for s, top in zip(one, top_one)]
            rest = [jnp.exp(s - top) for s, top in zip(rest, top_rest)]
            weights, shares, inverse = [], [], []
            row = lax.broadcasted_iota(jnp.int32, (8, TILE), 0)
            for j in range(2):
                sum_one = jnp.sum(one[j], axis=0, keepdims=True)
                sum_rest = jnp.sum(rest[j], axis=0, keepdims=True)
                pair_w, pair_p, pair_i = [], [], []
                for h in range(2):
                    tops = to_rows(top_one[j], top_rest[j], stat_ref[h])
                    sums = to_rows(sum_one, sum_rest, stat_ref[h])
                    top = jnp.maximum(top_fine[j][h], jnp.max(tops, axis=0, keepdims=True))
                    w = jnp.exp(tops - top).astype(BF).astype(F32)
                    p = jnp.exp(fine[j][h] - top)
                    total = jnp.sum(p, axis=0, keepdims=True)
                    total = total + jnp.sum(jnp.where(row < 5, w * sums, 0.0), axis=0, keepdims=True)
                    lse[4 * u + 2 * j + h] = top + jnp.log(total)
                    pair_w.append(w)
                    pair_p.append(p.astype(BF))
                    pair_i.append(1.0 / total)
                weights.append(row_weights(pair_w, cell_rows_ref[...]))
                shares.append(jnp.concatenate(pair_p, axis=1))
                inverse.append(jnp.concatenate(pair_i, axis=1))
            values = window(v_ref.at[0], i, lanes)
            v_fine = [values[:160, p].T for p in pairs]
            v_rough = [values[160:, p].T for p in pairs]
            yield
            mixed = [mm(v_rough[j], corners(one[j].astype(BF), rest[j].astype(BF))) for j in range(2)]
            out = [mm(v_fine[j], shares[j]) for j in range(2)]
            yield
            out = [out[j] + mm(mixed[j].astype(BF), weights[j]) for j in range(2)]
            yield
            for j in range(2):
                full = diagonal(out[j] * inverse[j]).T
                high = full.astype(BF)
                own = slice(256 * u + 128 * j, 256 * u + 128 * j + 128)
                attn_ref[0, rows, own] = high
                low_ref[0, rows, own] = (full - high.astype(F32)).astype(BF)
            if u == 1:
                lse_ref[0, :, rows] = jnp.concatenate([lse[h] for h in range(HEADS)], axis=0)
            yield

        return [quad(0), quad(1)]

    interleave([chain for i in range(TILES) for chain in tile(i, tile_bias_ref.at[i])], SKEW_F)


def middle_kernel(
    x_ref, attn_ref, cot_ref, w_ref, row_ref, ends_ref,
    out_ref, g1_ref, grad_ref, gvec_ref, gbup_ref,
    gwo_ref, gup_ref, gdown_ref,
):
    step = pl.program_id(0)

    @pl.when(step == 0)
    def _():
        gwo_ref[...] = jnp.zeros_like(gwo_ref)
        gup_ref[...] = jnp.zeros_like(gup_ref)
        gdown_ref[...] = jnp.zeros_like(gdown_ref)
        gvec_ref[...] = jnp.zeros_like(gvec_ref)
        gbup_ref[...] = jnp.zeros_like(gbup_ref)

    attn = attn_ref[...]
    cot = cot_ref[...]
    branch = sum(mm_nt(attn[:, HALF * t : HALF * t + HALF], w_ref[:, t, :, :HALF].reshape(D, HALF)) for t in range(2))
    y1 = x_ref[...].astype(F32) + (branch + vector(row_ref, 2))
    xhat, scale = norm_parts(y1)
    mid_gain = vector(row_ref, 3)
    n2 = (xhat * mid_gain + vector(row_ref, 4)).astype(BF)
    up_shift = joined(ends_ref, 4, 8)
    n2_t = n2.T
    cot_t = cot.T
    total = [y1 + vector(row_ref, 5), jnp.zeros_like(y1)]
    c = np.float32(np.sqrt(2.0 / np.pi))

    def hidden(part):
        cols = slice(256 * part, 256 * part + 256)
        at = HALF + 256 * (part % 4)
        up = w_ref[:, part // 4, :, at : at + 256].reshape(D, 256)
        at += FF // 2
        down_t = w_ref[:, part // 4, :, at : at + 256].reshape(D, 256)
        u = mm(n2, up) + up_shift[:, cols]
        dh = mm(cot, down_t)
        yield
        u2 = u * u
        t = jnp.tanh(u * (c + (c * 0.044715) * u2))
        h = 0.5 + 0.5 * t
        hid = (u * h).astype(BF)
        slope = h + (h - h * h) * (u * (2.0 * c + (6.0 * c * 0.044715) * u2))
        dhp = dh * slope
        dhp_b = dhp.astype(BF)
        gbup_ref[:, cols] += column_sum(dhp)
        yield
        total[0] = total[0] + mm_nt(hid, down_t)
        total[1] = total[1] + mm_nt(dhp_b, up)
        yield
        gdown_ref[:, cols] += mm(cot_t, hid)
        gup_ref[:, cols] += mm(n2_t, dhp_b)
        yield

    interleave([hidden(part) for part in range(8)], SKEW_M)
    out, dn2 = total
    out_ref[...] = out.astype(BF)
    cot_f = cot.astype(F32)
    dy1 = cot_f + norm_back(dn2, xhat, scale, mid_gain)
    g1 = dy1.astype(BF)
    g1_ref[...] = g1
    gwo_ref[...] += mm(g1.T, attn)
    gvec_ref[...] += jnp.concatenate(
        [column_sum(g1.astype(F32)), column_sum(dn2 * xhat), column_sum(dn2), column_sum(cot_f), jnp.zeros((4, D), F32)],
        axis=0,
    )


    @pl.when(step == pl.num_programs(0) - 1)
    def _():
        rows = D // grad_ref.shape[0]
        for t in range(2):
            at = 0
            for ref, width in ((gwo_ref, HALF), (gup_ref, FF // 2), (gdown_ref, FF // 2)):
                part = ref[:, width * t : width * t + width].astype(BF)
                grad_ref[:, t, :, at : at + width] = part.reshape(grad_ref.shape[0], rows, width)
                at += width


def backward_kernel(
    lens, x_ref, n1_ref, q_ref, k_ref, v_ref, attn_ref, low_ref, lse_ref, g1_ref,
    row_ref, w_ref, wo_t_ref,
    mask_ref, pool_q_ref, stat_ref, cell_rows_ref, expand_ref, spread_k_ref,
    dx_ref, gqkv_ref, gvec_ref,
    bias_ref, inv_ref, tile_bias_ref, dk_ref, dv_ref, dqkv_ref,
):
    step = pl.program_id(0)

    @pl.when(step == 0)
    def _():
        gqkv_ref[...] = jnp.zeros_like(gqkv_ref)
        gvec_ref[...] = jnp.zeros_like(gvec_ref)

    length = lens[step]
    count_tables(length, bias_ref, inv_ref)
    touched = (set(), set())
    head_of = lax.broadcasted_iota(jnp.int32, (HEADS, D), 1) // HD
    heads = (head_of == lax.broadcasted_iota(jnp.int32, (HEADS, D), 0)).astype(BF)

    def tile(i, bias):
        rows = pl.ds(128 * i, 128)
        bias[...] = mask_ref[i] + window(bias_ref, i, slice(None))
        q = q_ref[0, rows, :]
        cells = mm(pool_q_ref[...], q).astype(BF)
        da = jnp.concatenate([mm(g1_ref[0, rows, :], wo_t_ref[:, t, :, :HALF].reshape(D, HALF)) for t in range(2)], axis=1)
        da = da.astype(BF)
        product = da.astype(F32) * (attn_ref[0, rows, :].astype(F32) + low_ref[0, rows, :].astype(F32))
        high = product.astype(BF)
        delta = mm_nt(heads, high) + mm_nt(heads, (product - high.astype(F32)).astype(BF))
        lse = lse_ref[0, :, rows]

        def quad(u):
            lanes = slice(256 * u, 256 * u + 256)
            pairs = [slice(0, 128), slice(128, 256)]
            keys = window(k_ref.at[0], i, lanes)
            values = window(v_ref.at[0], i, lanes)
            c_one, c_rest = four_rows(cells[:64, lanes]), four_rows(cells[64:, lanes])
            q_two = [two_rows(q[:, lanes][:, p]) for p in pairs]
            d_two = [two_rows(da[:, lanes][:, p]) for p in pairs]
            yield
            fine = [mm_nt(keys[:160, p], q_two[j]) for j, p in enumerate(pairs)]
            one, rest = mm_nt(keys[160:SPLIT], c_one), mm_nt(keys[SPLIT:], c_rest)
            dp = [mm_nt(values[:160, p], d_two[j]) for j, p in enumerate(pairs)]
            yield
            ones, rests, weights, shares, slopes, rows_delta = [], [], [], [], [], []
            for j, pair in enumerate(pairs):
                s_one, s_rest = one[:, pair] + bias[160:SPLIT], rest[:, pair] + bias[SPLIT:]
                top_one, top_rest = jnp.max(s_one, axis=0, keepdims=True), jnp.max(s_rest, axis=0, keepdims=True)
                ones.append(jnp.exp(s_one - top_one))
                rests.append(jnp.exp(s_rest - top_rest))
                pair_w, pair_p, pair_s = [], [], []
                for h, p in enumerate(pairs):
                    head = 4 * u + 2 * j + h
                    own_lse, own_delta = lse[head : head + 1], delta[head : head + 1]
                    pair_w.append(jnp.exp(to_rows(top_one, top_rest, stat_ref[h]) - own_lse))
                    share = jnp.exp(fine[j][:, p] + bias[:160] - own_lse)
                    pair_s.append((share * (dp[j][:, p] - own_delta)).astype(BF))
                    pair_p.append(share.astype(BF))
                weights.append(row_weights(pair_w, cell_rows_ref[...]))
                shares.append(jnp.concatenate(pair_p, axis=1))
                slopes.append(jnp.concatenate(pair_s, axis=1))
                head = 4 * u + 2 * j
                both = jnp.concatenate([delta[head : head + 1], delta[head + 1 : head + 2]], axis=1)
                top = both.astype(BF).astype(F32)
                rows_delta.append(jnp.concatenate([top, both - top, jnp.zeros((6, 256), F32)], axis=0).astype(BF))
            k_fine = [keys[:160, p].T for p in pairs]
            k_rough = [keys[160:, p].T for p in pairs]
            yield
            d_cells = [mm(weights[j], d_two[j]).astype(BF) for j in range(2)]
            delta_cells = [jnp.sum(mm_nt(rows_delta[j], weights[j]), axis=0, keepdims=True) for j in range(2)]
            dv_fine = [mm(shares[j], d_two[j]) for j in range(2)]
            yield
            d_one, d_rest = (corners(d_cells[0][a : a + 128], d_cells[1][a : a + 128]) for a in (0, 128))
            dp_one, dp_rest = mm_nt(values[160:SPLIT], d_one), mm_nt(values[SPLIT:], d_rest)
            dk_fine = [mm(slopes[j], q_two[j]) for j in range(2)]
            dq = [mm(k_fine[j], slopes[j]) for j in range(2)]
            yield
            s_one = [(ones[j] * (dp_one[:, p] - delta_cells[j][:, :128])).astype(BF) for j, p in enumerate(pairs)]
            s_rest = [(rests[j] * (dp_rest[:, p] - delta_cells[j][:, 128:])).astype(BF) for j, p in enumerate(pairs)]
            dv_one = mm(jnp.concatenate([e.astype(BF) for e in ones], axis=1), d_one)
            dv_rest = mm(jnp.concatenate([e.astype(BF) for e in rests], axis=1), d_rest)
            yield
            dq_cells = [mm(k_rough[j], corners(s_one[j], s_rest[j])).astype(BF) for j in range(2)]
            dk_one = mm(jnp.concatenate(s_one, axis=1), c_one)
            dk_rest = mm(jnp.concatenate(s_rest, axis=1), c_rest)
            yield
            dq = [diagonal(dq[j] + mm(dq_cells[j], expand_ref[...])) * 0.125 for j in range(2)]
            dk = jnp.concatenate([jnp.concatenate(dk_fine, axis=1), dk_one, dk_rest], axis=0)
            dv = jnp.concatenate([jnp.concatenate(dv_fine, axis=1), dv_one, dv_rest], axis=0)
            at = 0
            for start, count in window_parts(i):
                for seen, begin, n in runs(touched[u], start, count):
                    part = pl.ds(begin, n)
                    for ref, grad in ((dk_ref, dk), (dv_ref, dv)):
                        block = grad[at + begin - start : at + begin - start + n]
                        ref[part, lanes] = ref[part, lanes] + block if seen else block
                at += count
            yield
            for j in range(2):
                at = 3 * HALF * u + 128 * j
                dqkv_ref[rows, at : at + 128] = dq[j].T.astype(BF)
            yield

        return [quad(0), quad(1)]

    interleave([chain for i in range(TILES) for chain in tile(i, tile_bias_ref.at[i])], SKEW_B)

    sums = []
    pre_gain = vector(row_ref, 0)

    def finish(chunk):
        rows = pl.ds(256 * chunk, 256)
        own = pl.ds(16 + 256 * chunk, 256)
        live = lax.broadcasted_iota(jnp.int32, (256, D), 0) + 256 * chunk < length
        wide = []
        for ref in (dk_ref, dv_ref):
            cells = []
            for level in range(1, LEVELS):
                count = 256 // 2**level
                pad = 0 if level == 5 else 16
                part = pl.ds(BASE[level] + pad + count * chunk, count)
                cells.append(ref[part, :] * jnp.concatenate([inv_ref[part, :]] * PAIRS, axis=1))
            cells.append(jnp.zeros((8, D), F32))
            wide.append(jnp.concatenate(cells, axis=0).astype(BF))
        yield
        wide = [mm(spread_k_ref[...], w) for w in wide]
        yield
        for ref, at, w in zip((dk_ref, dv_ref), (HALF, 2 * HALF), wide):
            grad = jnp.where(live, ref[own, :] + w, 0.0).astype(BF)
            dqkv_ref[rows, at : at + HALF] = grad[:, :HALF]
            dqkv_ref[rows, at + 3 * HALF : at + 4 * HALF] = grad[:, HALF:]
        yield
        parts = [dqkv_ref[rows, 3 * HALF * t : 3 * HALF * t + 3 * HALF] for t in range(2)]
        dn1 = mm_nt(parts[0], w_ref[0]) + mm_nt(parts[1], w_ref[1])
        xhat, scale = norm_parts(x_ref[0, rows, :].astype(F32))
        yield
        dx = g1_ref[0, rows, :].astype(F32) + norm_back(dn1, xhat, scale, pre_gain)
        dx_ref[0, rows, :] = dx.astype(BF)
        col = [column_sum(part.astype(F32)) for part in parts]
        sums.append(
            jnp.concatenate(
                [
                    column_sum(dn1 * xhat), column_sum(dn1),
                    jnp.concatenate([c[:, :HALF] for c in col], axis=1),
                    jnp.concatenate([c[:, 2 * HALF :] for c in col], axis=1),
                    jnp.zeros((4, D), F32),
                ],
                axis=0,
            )
        )
        yield

    interleave([finish(chunk) for chunk in range(4)], SKEW_E)
    gvec_ref[...] += sums[0] + sums[1] + sums[2] + sums[3]
    n1_t = n1_ref[0].T
    for t in range(2):
        gqkv_ref[t] += mm(n1_t, dqkv_ref[:, 3 * HALF * t : 3 * HALF * t + 3 * HALF])


def whole(shape):
    return pl.BlockSpec(shape, lambda *_: (0,) * len(shape))


def per_sequence(*shape):
    return pl.BlockSpec((1,) + shape, lambda s, *_: (s,) + (0,) * len(shape))


LIMIT = 60 * 1024 * 1024


def attention_forward(x, lens, row, w, ends, const):
    count = x.shape[0]
    return pl.pallas_call(
        forward_kernel,
        grid_spec=pltpu.PrefetchScalarGridSpec(
            num_scalar_prefetch=1,
            grid=(count,),
            in_specs=[
                per_sequence(SLOT, D), whole((SMALL, 128)), whole((2, D, 3 * HALF)), whole((2, 16, 128)),
                whole((TILES, WIN, TILE)), whole((TILE, TILE)), whole((2, 8, TILE)), whole((TILE, TILE)), whole((256, 256)),
            ],
            out_specs=[
                per_sequence(SLOT, D), per_sequence(SLOT, D), per_sequence(CELL_ROWS, D), per_sequence(CELL_ROWS, D),
                per_sequence(SLOT, D), per_sequence(SLOT, D), per_sequence(HEADS, SLOT),
            ],
            scratch_shapes=[
                pltpu.VMEM((CELL_ROWS, 128), F32), pltpu.VMEM((CELL_ROWS, 128), F32), pltpu.VMEM((2, 32, D), F32),
                pltpu.VMEM((TILES, WIN, TILE), F32),
            ],
        ),
        out_shape=[
            jax.ShapeDtypeStruct((count, SLOT, D), BF), jax.ShapeDtypeStruct((count, SLOT, D), BF),
            jax.ShapeDtypeStruct((count, CELL_ROWS, D), BF), jax.ShapeDtypeStruct((count, CELL_ROWS, D), BF),
            jax.ShapeDtypeStruct((count, SLOT, D), BF), jax.ShapeDtypeStruct((count, SLOT, D), BF),
            jax.ShapeDtypeStruct((count, HEADS, SLOT), F32),
        ],
        compiler_params=pltpu.CompilerParams(vmem_limit_bytes=LIMIT),
        cost_estimate=pl.CostEstimate(flops=count * 30 * 10**9, bytes_accessed=count * 10**7, transcendentals=0),
        name="attention_forward",
    )(lens, x, row, w, ends, const["mask"], const["pool_q"], const["stat"], const["cell_rows"], const["pool_k"])


ROWS = 512


def middle(x, attn, cot, w, row, ends):
    total = x.shape[0]
    rows = pl.BlockSpec((ROWS, D), lambda s: (s, 0))
    return pl.pallas_call(
        middle_kernel,
        grid=(total // ROWS,),
        in_specs=[
            rows, rows, rows, whole(w.shape), whole((SMALL, 128)), whole((2, 16, 128)),
        ],
        out_specs=[rows, rows, whole(w.shape), whole((8, D)), whole((1, FF))],
        scratch_shapes=[pltpu.VMEM((D, D), F32), pltpu.VMEM((D, FF), F32), pltpu.VMEM((D, FF), F32)],
        out_shape=[
            jax.ShapeDtypeStruct((total, D), BF), jax.ShapeDtypeStruct((total, D), BF), jax.ShapeDtypeStruct(w.shape, BF),
            jax.ShapeDtypeStruct((8, D), F32), jax.ShapeDtypeStruct((1, FF), F32),
        ],
        compiler_params=pltpu.CompilerParams(vmem_limit_bytes=LIMIT),
        name="middle",
    )(x, attn, cot, w, row, ends)


def attention_backward(x, lens, n1, q, k, v, attn, low, lse, g1, row, w, rest, const):
    count = x.shape[0]
    wo_t = pl.BlockSpec(rest.shape[:3] + (HALF,), lambda *_: (0, 0, 0, 0))
    return pl.pallas_call(
        backward_kernel,
        grid_spec=pltpu.PrefetchScalarGridSpec(
            num_scalar_prefetch=1,
            grid=(count,),
            in_specs=[
                per_sequence(SLOT, D), per_sequence(SLOT, D), per_sequence(SLOT, D),
                per_sequence(CELL_ROWS, D), per_sequence(CELL_ROWS, D), per_sequence(SLOT, D), per_sequence(SLOT, D),
                per_sequence(HEADS, SLOT), per_sequence(SLOT, D),
                whole((SMALL, 128)), whole((2, D, 3 * HALF)), wo_t,
                whole((TILES, WIN, TILE)), whole((TILE, TILE)), whole((2, 8, TILE)), whole((TILE, TILE)),
                whole((256, 256)), whole((256, 256)),
            ],
            out_specs=[per_sequence(SLOT, D), whole((2, D, 3 * HALF)), whole((8, D))],
            scratch_shapes=[
                pltpu.VMEM((CELL_ROWS, 128), F32), pltpu.VMEM((CELL_ROWS, 128), F32), pltpu.VMEM((TILES, WIN, TILE), F32),
                pltpu.VMEM((CELL_ROWS, D), F32), pltpu.VMEM((CELL_ROWS, D), F32), pltpu.VMEM((SLOT, 3 * D), BF),
            ],
        ),
        out_shape=[
            jax.ShapeDtypeStruct((count, SLOT, D), BF), jax.ShapeDtypeStruct((2, D, 3 * HALF), F32),
            jax.ShapeDtypeStruct((8, D), F32),
        ],
        compiler_params=pltpu.CompilerParams(vmem_limit_bytes=LIMIT),
        cost_estimate=pl.CostEstimate(flops=count * 40 * 10**9, bytes_accessed=count * 10**7, transcendentals=0),
        name="attention_backward",
    )(
        lens, x, n1, q, k, v, attn, low, lse, g1, row, w, rest,
        const["mask"], const["pool_q"], const["stat"], const["cell_rows"], const["expand"], const["spread_k"],
    )


def bits_of(count):
    return count.bit_length() - 1


def all_bits(n_dp, n_t):
    return [("tensor", b) for b in reversed(range(bits_of(n_t)))] + [("dp", b) for b in reversed(range(bits_of(n_dp)))]


def gather_orders(n_dp, n_t):
    far = [("dp", b) for b in reversed(range(2, bits_of(n_dp)))]
    near = [("dp", 1)]
    side = [("tensor", b) for b in reversed(range(bits_of(n_t)))]
    core_bit = [("dp", 0)]
    return far + near + side + core_bit, far + side + near + core_bit


def own_bit(bit):
    axis, b = bit
    return (lax.axis_index(axis) // 2**b) % 2


def partner(bit):
    axis, b = bit
    return {axis: lax.axis_index(axis) + (1 - 2 * own_bit(bit)) * 2**b}


def meet(bits):
    barrier = pltpu.get_barrier_semaphore()
    for bit in bits:
        pl.semaphore_signal(barrier, inc=1, device_id=partner(bit), device_id_type=pl.DeviceIdType.MESH)
    pl.semaphore_wait(barrier, len(bits))


def halves(width):
    if width % 256:
        return [(0, width)]
    return [(0, width // 2), (width // 2, width // 2)]


def gather_kernel(
    bits, orders, parts, *refs
):
    *shard_refs, ends_ref, out_ref, all_ends_ref, own_sems, send_sems, recv_sems, ends_own_sem, ends_sems = refs
    slot = out_ref.at[tuple(own_bit(bit) for bit in bits)]
    width = shard_refs[0].shape[1]
    own = [
        pltpu.make_async_copy(ref, slot.at[:, pl.ds(width * j, width)], own_sems.at[j]) for j, ref in enumerate(shard_refs)
    ]
    for copy in own:
        copy.start()
    side = [bit for bit in bits if bit[0] == "tensor"]
    own_ends = pltpu.make_async_copy(ends_ref.at[pl.ds(0, 16)], all_ends_ref.at[tuple(own_bit(bit) for bit in side)], ends_own_sem)
    own_ends.start()
    meet(bits)
    pending = []
    own_ends.wait()
    for copy in own:
        copy.wait()

    def ends_copy(step):
        place = all_ends_ref.at[tuple(slice(None) if j < step else own_bit(bit) for j, bit in enumerate(side))]
        return pltpu.make_async_remote_copy(
            src_ref=place, dst_ref=place, send_sem=ends_sems.at[0, step], recv_sem=ends_sems.at[1, step],
            device_id=partner(side[step]), device_id_type=pl.DeviceIdType.MESH,
        )

    if side:
        ends_copy(0).start()
    for step in range(len(bits)):
        for part, (at, width) in enumerate(parts):
            order = orders[part]
            done = order[:step]
            index = tuple(slice(None) if bit in done else own_bit(bit) for bit in bits)
            place = out_ref.at[index + (slice(None), pl.ds(at, width))]
            if step > 0:
                pending[(step - 1) * len(parts) + part].wait_recv()
            copy = pltpu.make_async_remote_copy(
                src_ref=place, dst_ref=place,
                send_sem=send_sems.at[step, part], recv_sem=recv_sems.at[step, part],
                device_id=partner(order[step]), device_id_type=pl.DeviceIdType.MESH,
            )
            copy.start()
            pending.append(copy)
    for copy in pending[-len(parts) :]:
        copy.wait_recv()
    for step in range(len(side)):
        ends_copy(step).wait_recv()
        if step + 1 < len(side):
            ends_copy(step + 1).start()
    for step in range(len(side)):
        ends_copy(step).wait_send()
    for copy in pending:
        copy.wait_send()


def gather(shards, ends, n_dp, n_t):
    rows, width = shards[0].shape[0], len(shards) * shards[0].shape[1]
    bits, orders, parts = all_bits(n_dp, n_t), gather_orders(n_dp, n_t), halves(width)
    side = bits_of(n_t)
    anywhere = pl.BlockSpec(memory_space=pl.ANY)
    out, all_ends = pl.pallas_call(
        functools.partial(gather_kernel, bits, orders, parts),
        in_specs=[anywhere] * (len(shards) + 1),
        out_specs=[anywhere, anywhere],
        out_shape=[
            jax.ShapeDtypeStruct((2,) * len(bits) + (rows, width), BF),
            jax.ShapeDtypeStruct((2,) * side + (16, 128), BF),
        ],
        scratch_shapes=[
            pltpu.SemaphoreType.DMA((len(shards),)), pltpu.SemaphoreType.DMA((len(bits), len(parts))),
            pltpu.SemaphoreType.DMA((len(bits), len(parts))), pltpu.SemaphoreType.DMA,
            pltpu.SemaphoreType.DMA((2, max(side, 1))),
        ],
        compiler_params=pltpu.CompilerParams(collective_id=0, has_side_effects=True),
        name="gather",
    )(*shards, ends)
    return out.reshape(n_t, n_dp, rows, width), all_ends.reshape(n_t, 16, 128)


def reduce_kernel(bits, orders, parts, n_t, grad_ref, pre_ref, mid_ref, up_ref, out_ref, own_ref, *scratch):
    steps, count = len(bits), len(parts)
    sends, recvs, sums = (scratch[j * steps * count : (j + 1) * steps * count] for j in range(3))
    vec_out_ref, vec_recv, send_sems, recv_sems, vec_send_sems, vec_recv_sems = scratch[3 * steps * count :]
    meet(bits)
    vec_out_ref[0:4, :] = pre_ref[0:4, :]
    vec_out_ref[4:8, :] = mid_ref[0:4, :]
    for r in range(4):
        vec_out_ref[8 + r : 9 + r, :] = up_ref[:, D * r : D * r + D]
    vec_out_ref[12:16, :] = jnp.zeros((4, D), F32)

    def vec_copy(step):
        return pltpu.make_async_remote_copy(
            src_ref=vec_recv.at[2 * step], dst_ref=vec_recv.at[2 * step + 1],
            send_sem=vec_send_sems.at[step], recv_sem=vec_recv_sems.at[step],
            device_id=partner(orders[0][steps - 1 - step]), device_id_type=pl.DeviceIdType.MESH,
        )

    def copy_of(step, part):
        j = step * count + part
        return pltpu.make_async_remote_copy(
            src_ref=sends[j], dst_ref=recvs[j], send_sem=send_sems.at[step, part], recv_sem=recv_sems.at[step, part],
            device_id=partner(orders[part][steps - 1 - step]), device_id_type=pl.DeviceIdType.MESH,
        )

    def pieces(step, part):
        order = orders[part][::-1]
        left = [bit for bit in bits if bit not in order[:step]]
        j = left.index(order[step])
        low = 2 ** (len(left) - 1 - j)
        mine = own_bit(order[step])
        out = []
        for a in range(2**j):
            for c in range(low):
                out.append(((a * 2 + 1 - mine) * low + c, (a * 2 + mine) * low + c, a * low + c))
        at, width = parts[part]
        source = sums[(step - 1) * count + part] if step else grad_ref.at[:, :, pl.ds(at, width)]
        return out, source

    for step in range(steps):
        vec_recv[2 * step] = vec_out_ref[...]
        vec_copy(step).start()
        for part in range(count):
            blocks, source = pieces(step, part)
            for away, _, to in blocks:
                sends[step * count + part][to] = source[away].astype(BF)
            copy_of(step, part).start()
        for part in range(count):
            copy_of(step, part).wait_recv()
            blocks, source = pieces(step, part)
            for _, keep, to in blocks:
                total = source[keep] + recvs[step * count + part][to].astype(F32)
                if step == steps - 1:
                    at, width = parts[part]
                    out_ref[:, at : at + width] = total
                else:
                    sums[step * count + part][to] = total
        vec_copy(step).wait_recv()
        vec_out_ref[...] += vec_recv[2 * step + 1]
    own_ref[...] = jnp.zeros_like(own_ref)
    own_ref[0:8, 0:D] = vec_out_ref[0:8, :]
    t = lax.axis_index("tensor")
    for row in (2, 3):
        n = D // n_t
        full = vec_out_ref[row : row + 1, :]
        mine = full[:, :n]
        for j in range(1, n_t):
            mine = jnp.where(t == j, full[:, n * j : n * j + n], mine)
        own_ref[row : row + 1, 0:n] = mine
    n = FF // n_t
    full = jnp.concatenate([vec_out_ref[8 + r : 9 + r, :] for r in range(4)], axis=1)
    mine = full[:, :n]
    for j in range(1, n_t):
        mine = jnp.where(t == j, full[:, n * j : n * j + n], mine)
    own_ref[8:9, 0:n] = mine
    for step in range(steps):
        vec_copy(step).wait_send()
        for part in range(count):
            copy_of(step, part).wait_send()


def reduce(grad, pre, mid, up, n_dp, n_t):
    rows, width = grad.shape[2:]
    bits, orders, parts = all_bits(n_dp, n_t), gather_orders(n_dp, n_t), halves(width)
    steps = len(bits)
    blocks = [(2 ** (steps - 1 - step), rows, w) for step in range(steps) for _, w in parts]
    sems = pltpu.SemaphoreType.DMA
    vmem = pl.BlockSpec(memory_space=pltpu.VMEM)
    return pl.pallas_call(
        functools.partial(reduce_kernel, bits, orders, parts, n_t),
        in_specs=[vmem] * 4,
        out_specs=[vmem, vmem],
        out_shape=[jax.ShapeDtypeStruct((rows, width), F32), jax.ShapeDtypeStruct((16, max(D, FF // n_t)), F32)],
        scratch_shapes=[pltpu.VMEM(b, BF) for b in blocks] * 2
        + [pltpu.VMEM(b, F32) for b in blocks]
        + [
            pltpu.VMEM((16, D), F32), pltpu.VMEM((2 * steps, 16, D), F32), sems((steps, len(parts))), sems((steps, len(parts))),
            sems((steps,)), sems((steps,)),
        ],
        compiler_params=pltpu.CompilerParams(collective_id=1, has_side_effects=True, vmem_limit_bytes=LIMIT),
        name="reduce",
    )(grad.reshape(n_t * n_dp, rows, width), pre, mid, up)


def to_pairs(grid, widths):
    n_t, n_dp, rows, _ = grid.shape
    grid = grid.reshape(n_t, n_dp * rows, -1)
    if n_t == 2:
        return grid
    out, at = [], 0
    for width in widths:
        part = grid[:, :, at : at + width].reshape(2, n_t // 2, D, width)
        out.append(part.transpose(0, 2, 1, 3).reshape(2, D, n_t // 2 * width))
        at += width
    return jnp.concatenate(out, axis=2)


def from_pairs(grid, widths, n_dp, n_t):
    if n_t != 2:
        out, at = [], 0
        for width in widths:
            full = width * n_t // 2
            part = grid[:, :, at : at + full].reshape(2, D, n_t // 2, width)
            out.append(part.transpose(0, 2, 1, 3).reshape(n_t, D, width))
            at += full
        grid = jnp.concatenate(out, axis=2)
    return grid.reshape(n_t, n_dp, D // n_dp, -1)


def own_sequences(values, lengths, tensor_count):
    micro, rows, width = values[0].shape
    t = lax.axis_index("tensor")
    if rows % SLOT == 0:
        per = rows // SLOT
        own = lax.dynamic_slice_in_dim(lengths, t * per, per, 1).reshape(-1)
        return [v.reshape(micro * per, SLOT, width) for v in values], own
    pieces = SLOT // rows
    assert micro == pieces
    groups = [[g * pieces + j for j in range(pieces)] for g in range(tensor_count // pieces)]
    out = [lax.all_to_all(v, "tensor", 0, 1, axis_index_groups=groups, tiled=True) for v in values]
    sequence = lax.dynamic_slice(lengths, (t % pieces, t // pieces), (1, 1))
    return out, sequence.reshape(-1)


def own_rows(values, shape, tensor_count):
    micro, rows, width = shape
    if rows % SLOT == 0:
        return [v.reshape(shape) for v in values]
    pieces = SLOT // rows
    groups = [[g * pieces + j for j in range(pieces)] for g in range(tensor_count // pieces)]
    return [
        lax.all_to_all(v, "tensor", 1, 0, axis_index_groups=groups, tiled=True).reshape(shape) for v in values
    ]


def core(x, lens, cot, row, w, ends, rest):
    const = {name: jnp.asarray(value) for name, value in constants().items()}
    count = x.shape[0]
    flat = (count * SLOT, D)
    n1, q, k, v, attn, low, lse = attention_forward(x, lens, row, w, ends, const)
    out, g1, grad_rest, mid_vec, gbup = middle(
        x.reshape(flat), attn.reshape(flat), cot.reshape(flat), rest, row, ends
    )
    dx, gqkv, pre_vec = attention_backward(
        x, lens, n1, q, k, v, attn, low, lse, g1.reshape(count, SLOT, D), row, w, rest, const
    )
    return out, dx, grad_rest, mid_vec, gbup, gqkv, pre_vec


def on_device(
    inputs, lengths, pre_gain, pre_shift, query_weight, key_weight, value_weight, query_bias, value_bias,
    output_weight, output_bias, mid_gain, mid_shift, up_weight, up_bias, down_weight, down_bias, cotangent,
):
    n_dp, n_t = lax.axis_size("dp"), lax.axis_size("tensor")
    t = lax.axis_index("tensor")
    (x, cot), lens = own_sequences([inputs, cotangent], lengths, n_t)

    n_q, n_f = query_weight.shape[1], up_weight.shape[1]
    second = jnp.concatenate([output_weight.T, up_weight, down_weight.T], axis=1)
    small = ((query_bias, 0), (value_bias, n_q), (up_bias, 2 * n_q))
    vectors = (pre_gain, pre_shift, output_bias, mid_gain, mid_shift, down_bias)
    small += tuple((v, 2048 + D * j) for j, v in enumerate(vectors))
    row = sum(lax.pad(v, jnp.zeros((), BF), [(at, SMALL * 128 - at - v.shape[0], 0)]) for v, at in small)
    row = row.reshape(SMALL, 128)
    first = (query_weight, key_weight, value_weight)
    if n_q % 128:
        first = (jnp.concatenate(first, axis=1),)
    w, ends = gather(first, row, n_dp, n_t)
    w = to_pairs(w, (n_q,) * 3)
    rest = lax.all_gather(second, ("dp", "tensor"), axis=0, tiled=False)
    rest = rest.reshape(n_dp, n_t, D // n_dp, -1)
    if n_t != 2:
        rest = to_pairs(rest.transpose(1, 0, 2, 3), (n_q, n_f, n_f)).reshape(2, 16, 32, REST).transpose(1, 0, 2, 3)
        flat = ends.reshape(n_t, -1)
        parts = [flat[:, a : a + n].reshape(2, -1) for a, n in ((0, n_q), (n_q, n_q), (2 * n_q, n_f))]
        ends = jnp.concatenate(parts + [jnp.zeros((2, 512), ends.dtype)], axis=1).reshape(2, 16, 128)
    out, dx, grad_rest, mid_vec, gbup, gqkv, pre_vec = core(x, lens, cot, row, w, ends, rest)
    if n_t != 2:
        grad_rest = grad_rest.transpose(1, 0, 2, 3).reshape(2, D, REST)
        grad_rest = from_pairs(grad_rest, (n_q, n_f, n_f), n_dp, n_t).transpose(1, 0, 2, 3)
    grad_rest = grad_rest.reshape(n_dp * n_t, D // n_dp, -1)
    grad_rest = lax.psum_scatter(grad_rest, ("dp", "tensor"), scatter_dimension=0, tiled=False)
    grad_first, vec = reduce(from_pairs(gqkv, (n_q,) * 3, n_dp, n_t), pre_vec, mid_vec, gbup, n_dp, n_t)
    grad_q, grad_k, grad_v = (grad_first[:, n_q * j : n_q * j + n_q] for j in range(3))
    grad_o, grad_up, grad_down = grad_rest[:, :n_q].T, grad_rest[:, n_q : n_q + n_f], grad_rest[:, n_q + n_f :].T
    grad_o, grad_up, grad_down = grad_o.astype(F32), grad_up.astype(F32), grad_down.astype(F32)

    out, dx = own_rows([out.reshape(x.shape), dx], inputs.shape, n_t)
    each = [vec[j, :D] for j in range(8)]
    return (
        out, dx, each[0], each[1], grad_q, grad_k, grad_v, vec[2, :n_q], vec[3, :n_q], grad_o, each[4], each[5], each[6],
        grad_up, vec[8, :n_f], grad_down, each[7],
    )


def solution(mesh):
    rows = P(None, ("dp", "tensor"), None)
    by_row, by_column = P("dp", "tensor"), P("tensor", "dp")
    in_specs = (
        rows, P(None, "dp"), P(), P(), by_row, by_row, by_row, P("tensor"), P("tensor"), by_column, P(), P(), P(),
        by_row, P("tensor"), by_column, P(), rows,
    )
    out_specs = (
        rows, rows, P(), P(), by_row, by_row, by_row, P("tensor"), P("tensor"), by_column, P(), P(), P(),
        by_row, P("tensor"), by_column, P(),
    )
    return jax.shard_map(on_device, mesh=mesh, in_specs=in_specs, out_specs=out_specs, check_vma=False)
```
